32 devices in a mesh: replica: 2 (over x), fsdp: 16 (over z, y, core).
Axes of the slice: x: 2, y: 2, z: 4, core: 2. Of those that a mesh axis runs over, the one named last changes fastest.
Arguments:
- tokens: bfloat16 [16384, 1536], P(('replica', 'fsdp')), may hold values from -6 to 6
- cotangent: bfloat16 [16384, 1536], P(('replica', 'fsdp')), may hold values from -6 to 6
- needle_mask: int32 [16384], P(('replica', 'fsdp')), may hold values from 0 to 1
- segment_ids: int32 [32, 512], P(('replica', 'fsdp')), may hold values from 0 to 2, never falling along the last dimension, each value on 1 to 256 neighbouring positions
- attn_weight: float32 [1536, 6144], P('fsdp'), may hold values from -0.15625 to 0.15625
- ffn_weight: float32 [1536, 12288], P('fsdp'), may hold values from -0.15625 to 0.15625
- vector_params: float32 [3456], replicated
- attn_error: float32 [2, 1536, 6144], P('replica', 'fsdp'), may hold values from -160 to 160
- ffn_error: float32 [2, 1536, 12288], P('replica', 'fsdp'), may hold values from -160 to 160
- attn_momentum: float32 [1536, 6144], P('fsdp'), may hold values from -16 to 16
- ffn_momentum: float32 [1536, 12288], P('fsdp'), may hold values from -16 to 16
- attn_start: float32 [16, 8, 6144], P('fsdp'), may hold values from -6 to 6
- ffn_start: float32 [16, 8, 12288], P('fsdp'), may hold values from -6 to 6
- vector_momentum: float32 [3456], replicated, may hold values from -24 to 24
Outputs:
- mixed: bfloat16 [16384, 1536], P(('replica', 'fsdp'))
- grad_tokens: float32 [16384, 1536], P(('replica', 'fsdp'))
- grad_attn: float32 [2, 1536, 6144], P('replica', 'fsdp')
- grad_ffn: float32 [2, 1536, 12288], P('replica', 'fsdp')
- left_attn: float32 [8, 1536], P(None, 'fsdp')
- left_ffn: float32 [8, 1536], P(None, 'fsdp')
- right_attn: float32 [16, 8, 6144], P('fsdp')
- right_ffn: float32 [16, 8, 12288], P('fsdp')
- attn_error_new: float32 [2, 1536, 6144], P('replica', 'fsdp')
- ffn_error_new: float32 [2, 1536, 12288], P('replica', 'fsdp')
- attn_momentum_new: float32 [1536, 6144], P('fsdp')
- ffn_momentum_new: float32 [1536, 12288], P('fsdp')
- attn_weight_new: float32 [1536, 6144], P('fsdp')
- ffn_weight_new: float32 [1536, 12288], P('fsdp')
- vector_momentum_new: float32 [3456], replicated
- vector_new: float32 [3456], replicated
The draws below stay inside these ranges and needn't reach their ends.
Inputs may be any that keep to these rules, and one draw needn't show every extreme that they name: `segment_ids`: within each row the document numbers never fall.
All inputs are finite; a program needn't handle non-finite values.
Results may differ from the reference program's by a relative error of at most 0.022.
The reference program's roundings to bfloat16 on the way count: a program that leaves them out, or rounds other values in their place, can miss the bound.
Values may be sent and summed in bfloat16 or wider, within the bound.
No kernel may reach another device: no remote copies, remote signals or barrier semaphores. Data moves between devices by JAX's collectives and lax.ppermute only.
A program may use at most 448 MiB of HBM per device.

```python
import math
from functools import partial
import jax
import jax.numpy as jnp
import numpy as np
from jax import lax

D = 1536
HEADS = 12
HD = 64
FF = 4096
TOK_DEV = 512
RANK = 8
DOCS = 3
SHARDS = 16
REPLICAS = 2
SEQS = 32
TOKENS = 16384
VEC = 3456


def draw_needle_mask(key, part):
    key = jax.random.fold_in(key, 11)
    ticket = jax.random.randint(key, (TOKENS,), 0, 1000)
    row_index = jnp.arange(TOKENS, dtype=jnp.int32) // TOK_DEV
    shard_index = row_index % SHARDS
    copy_index = row_index // SHARDS
    limit = 50 + 750 * shard_index // max(SHARDS - 1, 1) + 150 * copy_index
    return (ticket < limit).astype(jnp.int32)


def draw_vector_params(key, part):
    key = jax.random.fold_in(key, 5)
    gain_key, lambda_key = jax.random.split(key)
    gains = jnp.exp(0.25 * jax.random.truncated_normal(gain_key, -2.0, 2.0, (2 * D + 2 * HD,), jnp.float32))
    lambdas = 0.15 * jax.random.normal(lambda_key, (4 * HD,), jnp.float32)
    return jnp.concatenate([gains, lambdas])


def block_scale(stream_key, extent, cuts, low, largest):
    gain, own = 1.0, jax.random.fold_in(stream_key, 6)
    for dim, blocks in cuts:
        steps = jnp.exp(jax.random.uniform(jax.random.fold_in(own, dim), (blocks,), jnp.float32, low / len(cuts), largest / len(cuts)))
        gain = gain * jnp.repeat(steps, extent[dim] // blocks).reshape([-1 if axis == dim else 1 for axis in range(len(extent))])
    return gain


def profile(amount, total, reach, slope):
    portions = [(1 << 20) // math.isqrt(grade ** slope) + 1 for grade in range(2, amount + 1)]
    spare, given = total - reach - (amount - 1), [1] * (amount - 1)
    while spare > 0:
        movable = [i for i in range(amount - 1) if given[i] < reach]
        pool, budget = sum([portions[i] for i in movable]), spare
        for i in movable:
            extra = min(reach - given[i], max(1, budget * portions[i] // pool), spare)
            given[i] = given[i] + extra
            spare = spare - extra
    return np.array([reach] + given)


def uneven(key, count, total, most, lean):
    if count == 2:
        one = jax.random.randint(key, (), max(1, total - most), min(most, total - 1) + 1)
        return jnp.stack([one, total - one])
    tallies = jnp.asarray(profile(count, total, most, lean), jnp.int32)
    pairs = (count - 1) // 2
    source_of, taker = tallies[1:1 + 2 * pairs:2], tallies[2:2 + 2 * pairs:2]
    margin = jnp.minimum(source_of - 1, most - taker)
    moved = jax.random.randint(jax.random.fold_in(key, 1), (pairs,), 0, 1 << 20) % (margin + 1)
    tallies = tallies.at[1:1 + 2 * pairs:2].set(source_of - moved).at[2:2 + 2 * pairs:2].set(taker + moved)
    return tallies[jax.random.permutation(jax.random.fold_in(key, 2), count)]


def normal_values(stream_key, extent, deviation, most, cuts=(), kind=jnp.bfloat16):
    array = jax.random.normal(stream_key, extent, jnp.float32) * deviation
    if len(cuts) > 0:
        array = block_scale(stream_key, extent, cuts, -0.22, 0.18) * array
    return jnp.clip(array, min=-most, max=most).astype(kind)


def setup_inputs(seed: int = 0) -> dict:
    keys = jax.random.split(jax.random.key(seed), 15)
    tokens = normal_values(keys[0], (TOKENS, D), 1.0, 6.0, ((0, 32),))
    cotangent = normal_values(keys[1], (TOKENS, D), 1.0, 6.0, ((0, 32),))
    needle_mask = draw_needle_mask(jax.random.fold_in(keys[14], 71), 0)
    segment_ids = jax.vmap(lambda own: jnp.searchsorted(jnp.cumsum(uneven(own, DOCS, TOK_DEV, TOK_DEV // 2, 0)), jnp.arange(TOK_DEV), side="right"))(jax.random.split(keys[3], SEQS)).reshape((SEQS, TOK_DEV)).astype(jnp.int32)
    attn_weight = normal_values(keys[4], (D, 4 * D), D ** -0.5, 0.15625, ((0, 16),), jnp.float32)
    ffn_weight = normal_values(keys[5], (D, 3 * FF), D ** -0.5, 0.15625, ((0, 16),), jnp.float32)
    vector_params = draw_vector_params(jax.random.fold_in(keys[14], 71), 0)
    attn_error = normal_values(keys[7], (REPLICAS, D, 4 * D), (0.3 * (TOK_DEV * SHARDS) ** 0.5), 160.0, ((0, 2), (1, 16)), jnp.float32)
    ffn_error = normal_values(keys[8], (REPLICAS, D, 3 * FF), (0.3 * (TOK_DEV * SHARDS) ** 0.5), 160.0, ((0, 2), (1, 16)), jnp.float32)
    attn_momentum = normal_values(keys[9], (D, 4 * D), (0.03 * (TOK_DEV * SHARDS) ** 0.5), 16.0, ((0, 16),), jnp.float32)
    ffn_momentum = normal_values(keys[10], (D, 3 * FF), (0.03 * (TOK_DEV * SHARDS) ** 0.5), 16.0, ((0, 16),), jnp.float32)
    attn_start = normal_values(keys[11], (SHARDS, RANK, 4 * D), 1.0, 6.0, ((0, 16),), jnp.float32)
    ffn_start = normal_values(keys[12], (SHARDS, RANK, 3 * FF), 1.0, 6.0, ((0, 16),), jnp.float32)
    vector_momentum = normal_values(keys[13], (VEC,), (0.03 * TOKENS ** 0.5), 24.0, (), jnp.float32)
    return {"tokens": tokens, "cotangent": cotangent, "needle_mask": needle_mask, "segment_ids": segment_ids, "attn_weight": attn_weight, "ffn_weight": ffn_weight, "vector_params": vector_params, "attn_error": attn_error, "ffn_error": ffn_error, "attn_momentum": attn_momentum, "ffn_momentum": ffn_momentum, "attn_start": attn_start, "ffn_start": ffn_start, "vector_momentum": vector_momentum}


NEEDLE = 3.0
LAMBDA_INIT = 0.2
DECAY_ERROR = 0.5
MOMENTUM = 0.9
RATE_MATRIX = 0.005
RATE_VECTOR = 0.02
MASKED = -1e+30
HIGHEST = lax.Precision.HIGHEST

@jax.custom_vjp
def low(v):
    return lax.optimization_barrier(v.astype(jnp.bfloat16)).astype(jnp.float32)

@jax.custom_vjp
def low_back(v):
    return v

def low_keep(v):
    return (low(v), None)

def low_pass(kept, grad):
    return (grad,)

def back_keep(v):
    return (v, None)

def back_low(kept, grad):
    return (low(grad),)
low.defvjp(low_keep, low_pass)
low_back.defvjp(back_keep, back_low)

def matmul(left, right):
    return jnp.dot(left, right, preferred_element_type=jnp.float32, precision=HIGHEST)

def rms_scale(values, epsilon):
    return lax.rsqrt(lax.optimization_barrier(jnp.mean(values * values, -1, keepdims=True)) + epsilon)

def layer(residual_in, attn_weight, ffn_weight, vector_params, segments):
    gain_in = vector_params[0:D]
    gain_mid = vector_params[D:2 * D]
    gain_head = vector_params[2 * D:2 * D + 2 * HD]
    lambda_q_one = vector_params[2 * D + 2 * HD:2 * D + 3 * HD]
    lambda_k_one = vector_params[2 * D + 3 * HD:2 * D + 4 * HD]
    lambda_q_two = vector_params[2 * D + 4 * HD:2 * D + 5 * HD]
    lambda_k_two = vector_params[2 * D + 5 * HD:2 * D + 6 * HD]
    attn_low = low(attn_weight)
    ffn_low = low(ffn_weight)
    normed_in = residual_in * rms_scale(residual_in, 1e-06)
    normed_low = low(normed_in * gain_in)
    qkv_proj = low(low_back(matmul(normed_low, attn_low[:, 0:3 * D])))
    queries = qkv_proj[:, 0:D].reshape(TOK_DEV, HEADS, 2, HD)
    keys_all = qkv_proj[:, D:2 * D].reshape(TOK_DEV, HEADS, 2, HD)
    values = qkv_proj[:, 2 * D:3 * D].reshape(TOK_DEV, HEADS, 2 * HD)
    key_one = keys_all[:, :, 0]
    key_two = keys_all[:, :, 1]
    lambda_value = jnp.exp(jnp.sum(lambda_q_one * lambda_k_one)) - jnp.exp(jnp.sum(lambda_q_two * lambda_k_two)) + LAMBDA_INIT
    score_scale = HD ** (-0.5)
    block_rows = min(512, TOK_DEV)
    block_count = TOK_DEV // block_rows
    positions = jnp.arange(TOK_DEV, dtype=jnp.int32)

    def attend(piece):
        query_one, query_two, query_pos, query_seg = piece
        allowed = (positions[None, :] <= query_pos[:, None]) & (segments[None, :] == query_seg[:, None])
        score_one = low_back(jnp.einsum('ihd,thd->hit', query_one, key_one, precision=HIGHEST) * score_scale)
        score_two = low_back(jnp.einsum('ihd,thd->hit', query_two, key_two, precision=HIGHEST) * score_scale)
        prob_one = jax.nn.softmax(jnp.where(allowed[None], score_one, MASKED), axis=-1)
        prob_two = jax.nn.softmax(jnp.where(allowed[None], score_two, MASKED), axis=-1)
        mixture = low(prob_one - lambda_value * prob_two)
        return low_back(jnp.einsum('hit,the->ihe', mixture, values, precision=HIGHEST))
    pieces = (queries[:, :, 0].reshape(block_count, block_rows, HEADS, HD), queries[:, :, 1].reshape(block_count, block_rows, HEADS, HD), positions.reshape(block_count, block_rows), segments.reshape(block_count, block_rows))
    heads_out = lax.map(jax.checkpoint(attend), pieces).reshape(TOK_DEV, HEADS, 2 * HD)
    normed_head = heads_out * rms_scale(heads_out, 1e-05)
    heads_low = low((normed_head * gain_head * (1.0 - LAMBDA_INIT)).reshape(TOK_DEV, D))
    residual_mid = residual_in + low_back(matmul(heads_low, attn_low[:, 3 * D:4 * D]))
    normed_mid = residual_mid * rms_scale(residual_mid, 1e-06)
    mid_low = low(normed_mid * gain_mid)
    gate_up = low_back(matmul(mid_low, ffn_low[:, 0:2 * FF]))
    hidden = low(jax.nn.silu(gate_up[:, 0:FF]) * gate_up[:, FF:2 * FF])
    ffn_out = low_back(matmul(hidden, ffn_low[:, 2 * FF:3 * FF].T))
    return residual_mid + ffn_out

def orthonormal(left):
    columns = []
    for number in range(left.shape[-1]):
        column = left[..., number]
        for earlier in columns:
            column = column - lax.optimization_barrier(jnp.sum(earlier * column, -1, keepdims=True)) * earlier
        column = column * lax.rsqrt(lax.optimization_barrier(jnp.sum(column * column, -1, keepdims=True)))
        columns.append(column)
    return jnp.stack(columns, -1)

def compress(gradients, error_buf, momentum, weight, start_factor, columns):
    merged = (gradients + DECAY_ERROR * error_buf).reshape(REPLICAS, SHARDS, D // SHARDS, columns)
    left_sum = jnp.einsum('rfsc,fkc->fsk', merged, start_factor, precision=HIGHEST)
    left_ortho = orthonormal(left_sum)
    right_mean = jnp.einsum('fsk,rfsc->fkc', left_ortho, merged, precision=HIGHEST) / REPLICAS
    approx = jnp.einsum('fsk,fkc->fsc', left_ortho, right_mean, precision=HIGHEST)
    error_new = (merged - approx[None]).reshape(REPLICAS, D, columns)
    momentum_new = MOMENTUM * momentum + (1.0 - MOMENTUM) * approx.reshape(D, columns)
    weight_new = weight - RATE_MATRIX * momentum_new
    left_out = left_ortho.transpose(2, 0, 1).reshape(RANK, D)
    return (left_out, right_mean, error_new, momentum_new, weight_new)

def reference(tokens, cotangent, needle_mask, segment_ids, attn_weight, ffn_weight, vector_params, attn_error, ffn_error, attn_momentum, ffn_momentum, attn_start, ffn_start, vector_momentum):
    loss_weights = 1.0 + NEEDLE * needle_mask.astype(jnp.float32)
    weight_total = jnp.sum(loss_weights)
    loss_scale = loss_weights * (TOKENS / weight_total)
    inputs = tokens.astype(jnp.float32).reshape(REPLICAS, SHARDS, TOK_DEV, D)
    pulls = (cotangent.astype(jnp.float32) * loss_scale[:, None]).reshape(REPLICAS, SHARDS, TOK_DEV, D)
    segs = segment_ids.reshape(REPLICAS, SHARDS, TOK_DEV)

    def one_context(totals, context_item):
        context_in, context_back, context_segs = context_item
        result, pullback = jax.vjp(partial(layer, segments=context_segs), context_in, attn_weight, ffn_weight, vector_params)
        grad_in, grad_attn_part, grad_ffn_part, grad_vec_part = pullback(context_back)
        new_totals = (totals[0] + grad_attn_part, totals[1] + grad_ffn_part, totals[2] + grad_vec_part)
        return (new_totals, (result.astype(jnp.bfloat16), grad_in))
    grads_attn = []
    grads_ffn = []
    mixed_parts = []
    grad_parts = []
    vector_grad = jnp.zeros((VEC,), jnp.float32)
    for replica_index in range(REPLICAS):
        zeros_start = (jnp.zeros((D, 4 * D), jnp.float32), jnp.zeros((D, 3 * FF), jnp.float32), jnp.zeros((VEC,), jnp.float32))
        totals, outputs = lax.scan(one_context, zeros_start, (inputs[replica_index], pulls[replica_index], segs[replica_index]))
        grads_attn.append(totals[0])
        grads_ffn.append(totals[1])
        vector_grad = vector_grad + totals[2]
        mixed_parts.append(outputs[0])
        grad_parts.append(outputs[1])
    mixed = jnp.stack(mixed_parts).reshape(TOKENS, D)
    grad_tokens = jnp.stack(grad_parts).reshape(TOKENS, D)
    grad_attn = jnp.stack(grads_attn)
    grad_ffn = jnp.stack(grads_ffn)
    left_attn, right_attn, attn_error_new, attn_momentum_new, attn_weight_new = compress(grad_attn, attn_error, attn_momentum, attn_weight, attn_start, 4 * D)
    left_ffn, right_ffn, ffn_error_new, ffn_momentum_new, ffn_weight_new = compress(grad_ffn, ffn_error, ffn_momentum, ffn_weight, ffn_start, 3 * FF)
    vector_momentum_new = MOMENTUM * vector_momentum + (1.0 - MOMENTUM) * vector_grad
    vector_new = vector_params - RATE_VECTOR * vector_momentum_new
    return (mixed, grad_tokens, grad_attn, grad_ffn, left_attn, left_ffn, right_attn, right_ffn, attn_error_new, ffn_error_new, attn_momentum_new, ffn_momentum_new, attn_weight_new, ffn_weight_new, vector_momentum_new, vector_new)
```

```python
from functools import partial

import jax
import jax.numpy as jnp
from jax import lax
from jax.experimental import pallas as pl
from jax.experimental.pallas import tpu as pltpu
from jax.sharding import PartitionSpec as P

D = 1536
HEADS = 12
HD = 64
FF = 4096

NEEDLE = 3.0
LAMBDA_INIT = 0.2
KEEP = 1.0 - LAMBDA_INIT
DECAY_ERROR = 0.5
MOMENTUM = 0.9
RATE_MATRIX = 0.005
RATE_VECTOR = 0.02
MASKED = -1e30
HIGHEST = lax.Precision.HIGHEST
BF16 = jnp.bfloat16
F32 = jnp.float32

GROUP = 4
BLOCK = 128
REACH = 256
WIDTH = 2 * HD
OWN_HEADS = HEADS // GROUP
ATTN_Q = D // GROUP
FF_Q = FF // GROUP


def rms_scale(values, epsilon):
    return lax.rsqrt(jnp.mean(values * values, -1, keepdims=True) + epsilon)


def norm_back(grad_normed, normed, scale):
    return scale * (grad_normed - normed * jnp.mean(grad_normed * normed, -1, keepdims=True))


def dot(left, right, left_dim=1, right_dim=0, **kinds):
    return lax.dot_general(
        left, right, (((left_dim,), (right_dim,)), ((), ())), preferred_element_type=F32, **kinds
    )


def score_parts(qkv_ref, head, block, reach, lam, bias):
    rows = pl.ds(block * BLOCK, BLOCK)
    lane = lax.broadcasted_iota(jnp.int32, (1, WIDTH), 1)
    first = lane < HD
    query = qkv_ref[rows, head * WIDTH : (head + 1) * WIDTH] * BF16(HD**-0.5)
    key = qkv_ref[reach, ATTN_Q + head * WIDTH : ATTN_Q + (head + 1) * WIDTH]
    value = qkv_ref[reach, 2 * ATTN_Q + head * WIDTH : 2 * ATTN_Q + (head + 1) * WIDTH]
    zero = jnp.zeros((), BF16)
    query_one = jnp.where(first, query, zero)
    query_two = jnp.where(first, zero, query)
    probs = []
    for half in (query_one, query_two):
        score = dot(half, key, 1, 1) + bias
        expo = jnp.exp(score - jnp.max(score, -1, keepdims=True))
        probs.append(expo * (1.0 / jnp.sum(expo, -1, keepdims=True)))
    mixture = (probs[0] - lam * probs[1]).astype(BF16)
    return query_one, query_two, key, value, probs[0], probs[1], mixture


def block_bias(seg_q_ref, seg_k_ref, block, low, high):
    rows = lax.broadcasted_iota(jnp.int32, (BLOCK, high - low), 0) + block * BLOCK
    cols = lax.broadcasted_iota(jnp.int32, (BLOCK, high - low), 1) + low
    same = seg_q_ref[0, block * BLOCK : (block + 1) * BLOCK, :] == seg_k_ref[0, :, low:high]
    return jnp.where((cols <= rows) & same, 0.0, MASKED)


def reach_of(block):
    return max(0, block - REACH // BLOCK) * BLOCK, (block + 1) * BLOCK


def attend_kernel(lam_ref, qkv_ref, seg_q_ref, seg_k_ref, gain_ref, heads_ref):
    lam = lam_ref[0]
    gain = gain_ref[...] * KEEP
    for block in range(qkv_ref.shape[0] // BLOCK):
        low, high = reach_of(block)
        bias = block_bias(seg_q_ref, seg_k_ref, block, low, high)
        for head in range(OWN_HEADS):
            parts = score_parts(qkv_ref, head, block, pl.ds(low, high - low), lam, bias)
            out = dot(parts[6], parts[3])
            normed = out * rms_scale(out, 1e-05)
            heads_ref[pl.ds(block * BLOCK, BLOCK), head * WIDTH : (head + 1) * WIDTH] = (
                normed * gain
            ).astype(BF16)


def attend_back_kernel(
    lam_ref, qkv_ref, seg_q_ref, seg_k_ref, gain_ref, grad_ref, out_ref, stat_ref, dk_ref, dv_ref
):
    lam = lam_ref[0]
    gain = gain_ref[...] * KEEP
    blocks = qkv_ref.shape[0] // BLOCK
    first = lax.broadcasted_iota(jnp.int32, (1, WIDTH), 1) < HD
    zero = jnp.zeros((), BF16)
    gain_total = jnp.zeros((1, WIDTH), F32)
    lam_total = jnp.zeros((1, 1), F32)
    biases = [block_bias(seg_q_ref, seg_k_ref, b, *reach_of(b)) for b in range(blocks)]
    for head in range(OWN_HEADS):
        lanes = slice(head * WIDTH, (head + 1) * WIDTH)
        dk_ref[...] = jnp.zeros_like(dk_ref)
        dv_ref[...] = jnp.zeros_like(dv_ref)
        for block in range(blocks):
            low, high = reach_of(block)
            rows, reach = pl.ds(block * BLOCK, BLOCK), pl.ds(low, high - low)
            query_one, query_two, key, value, prob_one, prob_two, mixture = score_parts(
                qkv_ref, head, block, reach, lam, biases[block]
            )
            out = dot(mixture, value)
            scale = rms_scale(out, 1e-05)
            normed = out * scale
            grad = grad_ref[rows, lanes].astype(F32)
            gain_total = gain_total + jnp.sum(grad * normed, 0, keepdims=True)
            grad_out = norm_back(grad * gain, normed, scale).astype(BF16)
            grad_mix = dot(grad_out, value, 1, 1)
            mean_one = jnp.sum(grad_mix * prob_one, -1, keepdims=True)
            mean_two = jnp.sum(grad_mix * prob_two, -1, keepdims=True)
            lam_total = lam_total - jnp.sum(mean_two, 0, keepdims=True)
            low_one = (prob_one * (grad_mix - mean_one)).astype(BF16)
            low_two = (prob_two * (-lam * (grad_mix - mean_two))).astype(BF16)
            dv_ref[reach, :] += dot(mixture, grad_out, 0, 0)
            dk_ref[reach, :] += dot(low_one, query_one, 0, 0) + dot(low_two, query_two, 0, 0)
            grad_query = dot(low_one, jnp.where(first, key, zero)) + dot(
                low_two, jnp.where(first, zero, key)
            )
            out_ref[rows, lanes] = (grad_query * HD**-0.5).astype(BF16)
        out_ref[:, ATTN_Q + head * WIDTH : ATTN_Q + (head + 1) * WIDTH] = dk_ref[...].astype(BF16)
        out_ref[:, 2 * ATTN_Q + head * WIDTH : 2 * ATTN_Q + (head + 1) * WIDTH] = dv_ref[
            ...
        ].astype(BF16)
    stat_ref[0, 0:1, :] = gain_total * KEEP
    stat_ref[0, 1:2, :] = jnp.broadcast_to(lam_total, (1, WIDTH))
    stat_ref[0, 2:8, :] = jnp.zeros((6, WIDTH), F32)


def attention_specs(length):
    return [
        pl.BlockSpec(memory_space=pltpu.SMEM),
        pl.BlockSpec((length, 3 * ATTN_Q), lambda i: (i, 0)),
        pl.BlockSpec((1, length, 1), lambda i: (i, 0, 0)),
        pl.BlockSpec((1, 1, length), lambda i: (i, 0, 0)),
        pl.BlockSpec((1, WIDTH), lambda i: (0, 0)),
    ]


def attend(lam, qkv, segments, gain):
    length = segments.shape[1]
    return pl.pallas_call(
        attend_kernel,
        grid=(GROUP,),
        in_specs=attention_specs(length),
        out_specs=pl.BlockSpec((length, ATTN_Q), lambda i: (i, 0)),
        out_shape=jax.ShapeDtypeStruct((GROUP * length, ATTN_Q), BF16),
        compiler_params=pltpu.CompilerParams(vmem_limit_bytes=32 * 2**20),
        cost_estimate=pl.CostEstimate(
            flops=GROUP * OWN_HEADS * 2 * 4 * length * 320 * WIDTH,
            bytes_accessed=GROUP * length * 8 * ATTN_Q,
            transcendentals=GROUP * OWN_HEADS * 2 * length * 320,
        ),
        name="attend",
    )(lam, qkv, segments[:, :, None], segments[:, None, :], gain)


def attend_back(lam, qkv, segments, gain, grad):
    length = segments.shape[1]
    return pl.pallas_call(
        attend_back_kernel,
        grid=(GROUP,),
        in_specs=attention_specs(length)
        + [pl.BlockSpec((length, ATTN_Q), lambda i: (i, 0))],
        out_specs=[
            pl.BlockSpec((length, 3 * ATTN_Q), lambda i: (i, 0)),
            pl.BlockSpec((1, 8, WIDTH), lambda i: (i, 0, 0)),
        ],
        out_shape=[
            jax.ShapeDtypeStruct((GROUP * length, 3 * ATTN_Q), BF16),
            jax.ShapeDtypeStruct((GROUP, 8, WIDTH), F32),
        ],
        scratch_shapes=[pltpu.VMEM((length, WIDTH), F32), pltpu.VMEM((length, WIDTH), F32)],
        compiler_params=pltpu.CompilerParams(vmem_limit_bytes=32 * 2**20),
        cost_estimate=pl.CostEstimate(
            flops=GROUP * OWN_HEADS * 2 * 10 * length * 320 * WIDTH,
            bytes_accessed=GROUP * length * 14 * ATTN_Q,
            transcendentals=GROUP * OWN_HEADS * 2 * length * 320,
        ),
        name="attend_back",
    )(lam, qkv, segments[:, :, None], segments[:, None, :], gain, grad)


def orthonormal_kernel(attn_ref, ffn_ref, attn_out_ref, ffn_out_ref):
    for source, target in ((attn_ref, attn_out_ref), (ffn_ref, ffn_out_ref)):
        left = source[...]
        number = lax.broadcasted_iota(jnp.int32, (left.shape[0], 1), 0)
        for step in range(left.shape[0]):
            row = left[step : step + 1]
            row = row * lax.rsqrt(jnp.sum(row * row, -1, keepdims=True))
            share = jnp.sum(left * row, -1, keepdims=True)
            left = jnp.where(
                number > step, left - share * row, jnp.where(number == step, row, left)
            )
        target[...] = left


def orthonormal(attn, ffn):
    kind = jax.ShapeDtypeStruct(attn.shape, F32)
    return pl.pallas_call(orthonormal_kernel, out_shape=[kind, kind], name="orthonormal")(attn, ffn)


def swap(value, bits, shards):
    return lax.ppermute(value, "fsdp", [(f, f ^ bits) for f in range(shards)])


def hop(value, low, high, step):
    pairs = [
        (GROUP * z + j, GROUP * (z + step) + j) for z in range(low, high + 1) for j in range(GROUP)
    ]
    return lax.ppermute(value, "fsdp", pairs)


def cross(value, low, high, shards, copies):
    pairs = [
        (r * shards + GROUP * z + j, (r + 1) % copies * shards + GROUP * z + j)
        for r in range(copies)
        for z in range(low, high + 1)
        for j in range(GROUP)
    ]
    return lax.ppermute(value, ("replica", "fsdp"), pairs)


def arrange(items, member):
    low, high = (member & 1) == 1, (member & 2) == 2
    pairs = [jnp.where(low, items[t ^ 1], items[t]) for t in range(GROUP)]
    return [jnp.where(high, pairs[t ^ 2], pairs[t]) for t in range(GROUP)]


def share_out(items, member, shards):
    mine = arrange(items, member)
    return [mine[0]] + [swap(mine[k], k, shards) for k in range(1, GROUP)]


def gather_group(value, shards):
    beside = swap(value, 1, shards)
    across = swap(value, 2, shards)
    return [value, beside, across, swap(across, 1, shards)]


def gather_rows(block, layer, copy, layers, shards, copies):
    half, cols = block.shape[0] // 2, block.shape[1]
    mine = lax.dynamic_index_in_dim(block.reshape(2, half, cols), copy, 0, False)
    ups, downs = [None], [None]
    up = down = mine
    for step in range(1, layers):
        up = hop(up, step - 1, layers - 2, 1)
        down = hop(down, 1, layers - step, -1)
        ups.append((up, cross(up, step, layers - 1, shards, copies)))
        downs.append((down, cross(down, 0, layers - 1 - step, shards, copies)))
    whole = jnp.zeros((layers, 2, half, cols), block.dtype)
    whole = lax.dynamic_update_slice(
        whole, block.reshape(1, 2, half, cols), (layer, 0, 0, 0)
    )
    for shift in range(1, layers):
        below = layer >= shift
        source = jnp.where(below, layer - shift, layer - shift + layers)
        for part, owner in ((0, copy), (1, 1 - copy)):
            piece = jnp.where(below, ups[shift][part], downs[layers - shift][part])
            whole = lax.dynamic_update_slice(whole, piece[None, None], (source, owner, 0, 0))
    return whole.reshape(layers * 2 * half, cols)


def scatter_rows(partials, layer, layers):
    blocks = partials.reshape(layers, partials.shape[0] // layers, partials.shape[1])

    def block_of(number):
        number = jnp.where(number < 0, number + layers, number)
        number = jnp.where(number >= layers, number - layers, number)
        return lax.dynamic_index_in_dim(blocks, number, 0, False).astype(F32)

    up = down = None
    for step in range(1, layers):
        send_up, send_down = block_of(layer - step), block_of(layer + step)
        if step > 1:
            send_up = send_up + up.astype(F32)
            send_down = send_down + down.astype(F32)
        up = hop(send_up.astype(BF16), 0, min(step - 1, layers - 2), 1)
        down = hop(send_down.astype(BF16), max(layers - step, 1), layers - 1, -1)
    total = block_of(layer)
    if layers > 1:
        total = total + up.astype(F32) + down.astype(F32)
    return total


def own_rows(total, member, shards):
    rows = total.shape[0] // GROUP
    parts = share_out(
        [total[t * rows : (t + 1) * rows].astype(BF16) for t in range(GROUP)], member, shards
    )
    return arrange(parts, member)


def sum_everywhere(value, shards, copies):
    bits = 1
    while bits < shards:
        value = value + swap(value, bits, shards)
        bits *= 2
    return value + cross_all(value, copies)


def cross_all(value, copies):
    return lax.ppermute(value, "replica", [(r, (r + 1) % copies) for r in range(copies)])


def local(
    shards,
    copies,
    tokens,
    cotangent,
    needle_mask,
    segment_ids,
    attn_weight,
    ffn_weight,
    vector_params,
    attn_error,
    ffn_error,
    attn_momentum,
    ffn_momentum,
    attn_start,
    ffn_start,
    vector_momentum,
):
    length = tokens.shape[0]
    layers = shards // GROUP
    place = lax.axis_index("fsdp")
    copy = lax.axis_index("replica")
    layer, member = place // GROUP, place % GROUP

    gain_in = vector_params[0:D]
    gain_mid = vector_params[D : 2 * D]
    gain_head = vector_params[2 * D : 2 * D + 2 * HD]
    lambda_q_one = vector_params[2 * D + 2 * HD : 2 * D + 3 * HD]
    lambda_k_one = vector_params[2 * D + 3 * HD : 2 * D + 4 * HD]
    lambda_q_two = vector_params[2 * D + 4 * HD : 2 * D + 5 * HD]
    lambda_k_two = vector_params[2 * D + 5 * HD : 2 * D + 6 * HD]
    exp_one = jnp.exp(jnp.sum(lambda_q_one * lambda_k_one))
    exp_two = jnp.exp(jnp.sum(lambda_q_two * lambda_k_two))
    lam = (exp_one - exp_two + LAMBDA_INIT).reshape(1)

    gather = partial(
        gather_rows, layer=layer, copy=copy, layers=layers, shards=shards, copies=copies
    )

    def layer_block(weight, sections, width):
        quarters = [
            jnp.concatenate(
                [
                    weight[:, s * GROUP * width + t * width : s * GROUP * width + (t + 1) * width]
                    for s in sections
                ],
                1,
            ).astype(BF16)
            for t in range(GROUP)
        ]
        return jnp.concatenate(arrange(share_out(quarters, member, shards), member), 0)

    qkv_weight = gather(layer_block(attn_weight, (0, 1, 2), ATTN_Q))
    residual_in = tokens.astype(F32)
    scale_in = rms_scale(residual_in, 1e-06)
    normed_in = residual_in * scale_in
    normed_all = jnp.concatenate(gather_group((normed_in * gain_in).astype(BF16), shards), 0)
    segments = jnp.concatenate(gather_group(segment_ids, shards), 0)
    out_weight = lax.all_gather(attn_weight[:, 3 * D :].astype(BF16), "fsdp", axis=0, tiled=True)
    up_weight = gather(layer_block(ffn_weight, (0, 1), FF_Q))
    down_weight = gather(layer_block(ffn_weight, (2,), FF_Q))

    qkv = dot(normed_all, qkv_weight).astype(BF16)
    heads_part = attend(lam, qkv, segments, gain_head[None])
    heads_shares = [heads_part[k * length : (k + 1) * length] for k in range(GROUP)]
    heads_got = [heads_shares[0]] + [swap(heads_shares[k], k, shards) for k in range(1, GROUP)]
    heads_low = jnp.concatenate(arrange(heads_got, member), 1)
    residual_mid = residual_in + dot(heads_low, out_weight)
    scale_mid = rms_scale(residual_mid, 1e-06)
    normed_mid = residual_mid * scale_mid
    mid_all = jnp.concatenate(gather_group((normed_mid * gain_mid).astype(BF16), shards), 0)

    loss_weights = 1.0 + NEEDLE * needle_mask.astype(F32)
    weight_total = sum_everywhere(
        jnp.broadcast_to(jnp.sum(loss_weights), (8, 128)), shards, copies
    )[0, 0]
    everyone = length * shards * copies
    grad_out = cotangent.astype(F32) * (loss_weights * (everyone / weight_total))[:, None]
    grad_out_all = jnp.concatenate(gather_group(grad_out.astype(BF16), shards), 0)

    gate_up = dot(mid_all, up_weight)
    gate_proj, up_proj = gate_up[:, :FF_Q], gate_up[:, FF_Q:]
    sigmoid_gate = jax.nn.sigmoid(gate_proj)
    activated = gate_proj * sigmoid_gate
    hidden = (activated * up_proj).astype(BF16)
    grad_hidden = dot(grad_out_all, down_weight)
    grad_gate = grad_hidden * up_proj * (sigmoid_gate * (1.0 + gate_proj * (1.0 - sigmoid_gate)))
    grad_up = grad_hidden * activated
    grad_gu = jnp.concatenate([grad_gate, grad_up], 1).astype(BF16)

    def sum_group(parts):
        got = [swap(parts[k], 1, shards) for k in (3, 1)]
        across = parts[2].astype(F32) + got[0].astype(F32)
        across = swap(across.astype(BF16), 2, shards)
        return parts[0].astype(F32) + got[1].astype(F32) + across.astype(F32)

    def token_parts(values):
        return [values[k * length : (k + 1) * length] for k in range(GROUP)]

    grad_mid_low = sum_group(token_parts(dot(grad_gu, up_weight, 1, 1).astype(BF16)))
    ffn_out = sum_group(token_parts(dot(hidden, down_weight, 1, 1).astype(BF16)))
    mixed = (residual_mid + ffn_out).astype(BF16)

    down_grad = scatter_rows(dot(grad_out_all, hidden, 0, 0).astype(BF16), layer, layers)
    up_partials = dot(mid_all, grad_gu, 0, 0).astype(BF16)
    gate_grad = scatter_rows(up_partials[:, :FF_Q], layer, layers)
    up_grad = scatter_rows(up_partials[:, FF_Q:], layer, layers)
    ffn_grad = jnp.concatenate(
        sum([own_rows(part, member, shards) for part in (gate_grad, up_grad, down_grad)], []), 1
    ).astype(F32)

    grad_gain_mid = jnp.sum(grad_mid_low * normed_mid, 0)
    grad_mid = grad_out + norm_back(grad_mid_low * gain_mid, normed_mid, scale_mid)
    grad_attn_low = grad_mid.astype(BF16)
    grad_heads = dot(grad_attn_low, out_weight, 1, 1).astype(BF16)
    grad_heads_all = jnp.concatenate(
        share_out(
            [grad_heads[:, t * ATTN_Q : (t + 1) * ATTN_Q] for t in range(GROUP)], member, shards
        ),
        0,
    )
    grad_qkv, stats = attend_back(lam, qkv, segments, gain_head[None], grad_heads_all)
    stats = jnp.sum(stats, 0)
    grad_gain_head, grad_lambda = stats[0], stats[1, 0]

    heads_all = jnp.concatenate(gather_group(heads_low, shards), 0)
    grad_attn_all = jnp.concatenate(
        share_out(
            [grad_attn_low[:, t * ATTN_Q : (t + 1) * ATTN_Q] for t in range(GROUP)], member, shards
        ),
        0,
    )
    out_grad = scatter_rows(dot(heads_all, grad_attn_all, 0, 0).astype(BF16), layer, layers)
    qkv_grad = scatter_rows(dot(normed_all, grad_qkv, 0, 0).astype(BF16), layer, layers)
    qkv_rows = own_rows(qkv_grad, member, shards)
    attn_grad = jnp.concatenate(
        [part[:, s * ATTN_Q : (s + 1) * ATTN_Q] for s in range(3) for part in qkv_rows]
        + own_rows(out_grad, member, shards),
        1,
    ).astype(F32)

    grad_in_low = sum_group(token_parts(dot(grad_qkv, qkv_weight, 1, 1).astype(BF16)))
    grad_gain_in = jnp.sum(grad_in_low * normed_in, 0)
    grad_tokens = grad_mid + norm_back(grad_in_low * gain_in, normed_in, scale_in)

    vector_local = jnp.concatenate(
        [
            grad_gain_in,
            grad_gain_mid,
            grad_gain_head,
            grad_lambda * exp_one * lambda_k_one,
            grad_lambda * exp_one * lambda_q_one,
            -grad_lambda * exp_two * lambda_k_two,
            -grad_lambda * exp_two * lambda_q_two,
        ]
    )
    vector_grad = sum_everywhere(vector_local, shards, copies)

    merged_attn = attn_grad + DECAY_ERROR * attn_error[0]
    merged_ffn = ffn_grad + DECAY_ERROR * ffn_error[0]
    left_attn = dot(attn_start[0], merged_attn, 1, 1, precision=HIGHEST)
    left_ffn = dot(ffn_start[0], merged_ffn, 1, 1, precision=HIGHEST)
    left_attn = left_attn + cross_all(left_attn, copies)
    left_ffn = left_ffn + cross_all(left_ffn, copies)
    ortho_attn, ortho_ffn = orthonormal(left_attn, left_ffn)

    def update(ortho, merged, momentum, weight):
        right = dot(ortho, merged, 1, 0, precision=HIGHEST).astype(BF16)
        other = cross_all(right, copies)
        right = (right.astype(F32) + other.astype(F32)) / copies
        approx = dot(ortho, right, 0, 0, precision=HIGHEST)
        momentum_new = MOMENTUM * momentum + (1.0 - MOMENTUM) * approx
        return right, merged - approx, momentum_new, weight - RATE_MATRIX * momentum_new

    right_ffn, ffn_error_new, ffn_momentum_new, ffn_weight_new = update(
        ortho_ffn, merged_ffn, ffn_momentum, ffn_weight
    )
    right_attn, attn_error_new, attn_momentum_new, attn_weight_new = update(
        ortho_attn, merged_attn, attn_momentum, attn_weight
    )
    vector_momentum_new = MOMENTUM * vector_momentum + (1.0 - MOMENTUM) * vector_grad
    vector_new = vector_params - RATE_VECTOR * vector_momentum_new
    return (
        mixed,
        grad_tokens,
        attn_grad[None],
        ffn_grad[None],
        ortho_attn,
        ortho_ffn,
        right_attn[None],
        right_ffn[None],
        attn_error_new[None],
        ffn_error_new[None],
        attn_momentum_new,
        ffn_momentum_new,
        attn_weight_new,
        ffn_weight_new,
        vector_momentum_new,
        vector_new,
    )


def solution(mesh):
    in_specs = (
        P(("replica", "fsdp"), None),
        P(("replica", "fsdp"), None),
        P(("replica", "fsdp")),
        P(("replica", "fsdp"), None),
        P("fsdp", None),
        P("fsdp", None),
        P(),
        P("replica", "fsdp", None),
        P("replica", "fsdp", None),
        P("fsdp", None),
        P("fsdp", None),
        P("fsdp", None, None),
        P("fsdp", None, None),
        P(),
    )
    out_specs = (
        P(("replica", "fsdp"), None),
        P(("replica", "fsdp"), None),
        P("replica", "fsdp", None),
        P("replica", "fsdp", None),
        P(None, "fsdp"),
        P(None, "fsdp"),
        P("fsdp", None, None),
        P("fsdp", None, None),
        P("replica", "fsdp", None),
        P("replica", "fsdp", None),
        P("fsdp", None),
        P("fsdp", None),
        P("fsdp", None),
        P("fsdp", None),
        P(),
        P(),
    )
    step = partial(local, mesh.shape["fsdp"], mesh.shape["replica"])
    return jax.shard_map(step, mesh=mesh, in_specs=in_specs, out_specs=out_specs, check_vma=False)
```

```python
from functools import partial

import jax
import jax.numpy as jnp
from jax import lax
from jax.experimental import pallas as pl
from jax.experimental.pallas import tpu as pltpu
from jax.sharding import PartitionSpec as P

D = 1536
HEADS = 12
HD = 64
FF = 4096

NEEDLE = 3.0
LAMBDA_INIT = 0.2
KEEP = 1.0 - LAMBDA_INIT
DECAY_ERROR = 0.5
MOMENTUM = 0.9
RATE_MATRIX = 0.005
RATE_VECTOR = 0.02
MASKED = -1e30
HIGHEST = lax.Precision.HIGHEST
BF16 = jnp.bfloat16
F32 = jnp.float32

GROUP = 4
BLOCK = 128
REACH = 256
WIDTH = 2 * HD
OWN_HEADS = HEADS // GROUP
ATTN_Q = D // GROUP
FF_Q = FF // GROUP


def rms_scale(values, epsilon):
    return lax.rsqrt(jnp.mean(values * values, -1, keepdims=True) + epsilon)


def norm_back(grad_normed, normed, scale):
    return scale * (grad_normed - normed * jnp.mean(grad_normed * normed, -1, keepdims=True))


def dot(left, right, left_dim=1, right_dim=0, **kinds):
    return lax.dot_general(
        left, right, (((left_dim,), (right_dim,)), ((), ())), preferred_element_type=F32, **kinds
    )


def score_parts(qkv_ref, head, block, reach, lam, bias):
    rows = pl.ds(block * BLOCK, BLOCK)
    lane = lax.broadcasted_iota(jnp.int32, (1, WIDTH), 1)
    first = lane < HD
    query = qkv_ref[rows, head * WIDTH : (head + 1) * WIDTH] * BF16(HD**-0.5)
    key = qkv_ref[reach, ATTN_Q + head * WIDTH : ATTN_Q + (head + 1) * WIDTH]
    value = qkv_ref[reach, 2 * ATTN_Q + head * WIDTH : 2 * ATTN_Q + (head + 1) * WIDTH]
    zero = jnp.zeros((), BF16)
    query_one = jnp.where(first, query, zero)
    query_two = jnp.where(first, zero, query)
    probs = []
    for half in (query_one, query_two):
        score = dot(half, key, 1, 1) + bias
        expo = jnp.exp(score - jnp.max(score, -1, keepdims=True))
        probs.append(expo * (1.0 / jnp.sum(expo, -1, keepdims=True)))
    mixture = (probs[0] - lam * probs[1]).astype(BF16)
    return query_one, query_two, key, value, probs[0], probs[1], mixture


def block_bias(seg_q_ref, seg_k_ref, block, low, high):
    rows = lax.broadcasted_iota(jnp.int32, (BLOCK, high - low), 0) + block * BLOCK
    cols = lax.broadcasted_iota(jnp.int32, (BLOCK, high - low), 1) + low
    same = seg_q_ref[block * BLOCK : (block + 1) * BLOCK, :] == seg_k_ref[:, low:high]
    return jnp.where((cols <= rows) & same, 0.0, MASKED)


def reach_of(block):
    return max(0, block - REACH // BLOCK) * BLOCK, (block + 1) * BLOCK


def attend_kernel(lam_ref, qkv_ref, seg_q_ref, seg_k_ref, gain_ref, heads_ref):
    lam = lam_ref[0]
    gain = gain_ref[...] * KEEP
    for block in range(qkv_ref.shape[0] // BLOCK):
        low, high = reach_of(block)
        bias = block_bias(seg_q_ref, seg_k_ref, block, low, high)
        for head in range(OWN_HEADS):
            parts = score_parts(qkv_ref, head, block, pl.ds(low, high - low), lam, bias)
            out = dot(parts[6], parts[3])
            normed = out * rms_scale(out, 1e-05)
            heads_ref[pl.ds(block * BLOCK, BLOCK), head * WIDTH : (head + 1) * WIDTH] = (
                normed * gain
            ).astype(BF16)


def attend_back_kernel(
    lam_ref, qkv_ref, seg_q_ref, seg_k_ref, gain_ref, grad_ref, out_ref, stat_ref, dk_ref, dv_ref
):
    lam = lam_ref[0]
    gain = gain_ref[...] * KEEP
    blocks = qkv_ref.shape[0] // BLOCK
    first = lax.broadcasted_iota(jnp.int32, (1, WIDTH), 1) < HD
    zero = jnp.zeros((), BF16)
    gain_total = jnp.zeros((1, WIDTH), F32)
    lam_total = jnp.zeros((1, 1), F32)
    biases = [block_bias(seg_q_ref, seg_k_ref, b, *reach_of(b)) for b in range(blocks)]
    for head in range(OWN_HEADS):
        lanes = slice(head * WIDTH, (head + 1) * WIDTH)
        dk_ref[...] = jnp.zeros_like(dk_ref)
        dv_ref[...] = jnp.zeros_like(dv_ref)
        for block in range(blocks):
            low, high = reach_of(block)
            rows, reach = pl.ds(block * BLOCK, BLOCK), pl.ds(low, high - low)
            query_one, query_two, key, value, prob_one, prob_two, mixture = score_parts(
                qkv_ref, head, block, reach, lam, biases[block]
            )
            out = dot(mixture, value)
            scale = rms_scale(out, 1e-05)
            normed = out * scale
            grad = grad_ref[rows, lanes].astype(F32)
            gain_total = gain_total + jnp.sum(grad * normed, 0, keepdims=True)
            grad_out = norm_back(grad * gain, normed, scale).astype(BF16)
            grad_mix = dot(grad_out, value, 1, 1)
            mean_one = jnp.sum(grad_mix * prob_one, -1, keepdims=True)
            mean_two = jnp.sum(grad_mix * prob_two, -1, keepdims=True)
            lam_total = lam_total - jnp.sum(mean_two, 0, keepdims=True)
            low_one = (prob_one * (grad_mix - mean_one)).astype(BF16)
            low_two = (prob_two * (-lam * (grad_mix - mean_two))).astype(BF16)
            dv_ref[reach, :] += dot(mixture, grad_out, 0, 0)
            dk_ref[reach, :] += dot(low_one, query_one, 0, 0) + dot(low_two, query_two, 0, 0)
            grad_query = dot(low_one, jnp.where(first, key, zero)) + dot(
                low_two, jnp.where(first, zero, key)
            )
            out_ref[rows, lanes] = (grad_query * HD**-0.5).astype(BF16)
        out_ref[:, ATTN_Q + head * WIDTH : ATTN_Q + (head + 1) * WIDTH] = dk_ref[...].astype(BF16)
        out_ref[:, 2 * ATTN_Q + head * WIDTH : 2 * ATTN_Q + (head + 1) * WIDTH] = dv_ref[
            ...
        ].astype(BF16)
    stat_ref[0:1, :] = gain_total * KEEP
    stat_ref[1:2, :] = jnp.broadcast_to(lam_total, (1, WIDTH))
    stat_ref[2:8, :] = jnp.zeros((6, WIDTH), F32)


def attention_specs(length):
    return [
        pl.BlockSpec(memory_space=pltpu.SMEM),
        pl.BlockSpec((length, 3 * ATTN_Q), lambda i: (0, 0)),
        pl.BlockSpec((length, 1), lambda i: (0, 0)),
        pl.BlockSpec((1, length), lambda i: (0, 0)),
        pl.BlockSpec((1, WIDTH), lambda i: (0, 0)),
    ]


def attend(lam, qkv, segments, gain):
    length = segments.shape[0]
    return pl.pallas_call(
        attend_kernel,
        grid=(1,),
        in_specs=attention_specs(length),
        out_specs=pl.BlockSpec((length, ATTN_Q), lambda i: (0, 0)),
        out_shape=jax.ShapeDtypeStruct((length, ATTN_Q), BF16),
        compiler_params=pltpu.CompilerParams(vmem_limit_bytes=32 * 2**20),
        cost_estimate=pl.CostEstimate(
            flops=OWN_HEADS * 2 * 4 * length * 320 * WIDTH,
            bytes_accessed=length * 8 * ATTN_Q,
            transcendentals=OWN_HEADS * 2 * length * 320,
        ),
        name="attend",
    )(lam, qkv, segments[:, None], segments[None, :], gain)


def attend_back(lam, qkv, segments, gain, grad):
    length = segments.shape[0]
    return pl.pallas_call(
        attend_back_kernel,
        grid=(1,),
        in_specs=attention_specs(length) + [pl.BlockSpec((length, ATTN_Q), lambda i: (0, 0))],
        out_specs=[
            pl.BlockSpec((length, 3 * ATTN_Q), lambda i: (0, 0)),
            pl.BlockSpec((8, WIDTH), lambda i: (0, 0)),
        ],
        out_shape=[
            jax.ShapeDtypeStruct((length, 3 * ATTN_Q), BF16),
            jax.ShapeDtypeStruct((8, WIDTH), F32),
        ],
        scratch_shapes=[pltpu.VMEM((length, WIDTH), F32), pltpu.VMEM((length, WIDTH), F32)],
        compiler_params=pltpu.CompilerParams(vmem_limit_bytes=32 * 2**20),
        cost_estimate=pl.CostEstimate(
            flops=OWN_HEADS * 2 * 10 * length * 320 * WIDTH,
            bytes_accessed=length * 14 * ATTN_Q,
            transcendentals=OWN_HEADS * 2 * length * 320,
        ),
        name="attend_back",
    )(lam, qkv, segments[:, None], segments[None, :], gain, grad)


def quarter_kernel(member_ref, *refs):
    for source, target in zip(refs[:GROUP], refs[GROUP:]):
        target[...] = source[...].astype(BF16)


def quarters(member, weight, sections, width):
    rows = weight.shape[0]

    def columns(bits):
        return lambda i, member: (0, i * GROUP + (member[0] ^ bits))

    kind = jax.ShapeDtypeStruct((rows, sections * width), BF16)
    return pl.pallas_call(
        quarter_kernel,
        grid_spec=pltpu.PrefetchScalarGridSpec(
            num_scalar_prefetch=1,
            grid=(sections,),
            in_specs=[pl.BlockSpec((rows, width), columns(bits)) for bits in range(GROUP)],
            out_specs=[pl.BlockSpec((rows, width), lambda i, member: (0, i))] * GROUP,
        ),
        out_shape=[kind] * GROUP,
        compiler_params=pltpu.CompilerParams(vmem_limit_bytes=32 * 2**20),
        cost_estimate=pl.CostEstimate(flops=0, bytes_accessed=rows * width, transcendentals=0),
        name="quarters",
    )(member.reshape(1), *[weight] * GROUP)


def back_kernel(pairs, *refs):
    total = None
    for left, right in zip(refs[:pairs], refs[pairs : 2 * pairs]):
        part = dot(left[...], right[...], 1, 1)
        total = part if total is None else total + part
    if len(refs) > 2 * pairs + 1:
        total = total + refs[2 * pairs][...].astype(F32)
    refs[-1][...] = total.astype(refs[-1].dtype)


def back_product(lefts, right, got=None, kind=BF16, tile=512, first=0, share=32):
    pairs, (length, depth) = len(lefts), lefts[0].shape
    width = right.shape[0]
    specs = [pl.BlockSpec((length, depth), lambda i: (0, 0))] * pairs
    for number in range(pairs):
        specs.append(pl.BlockSpec((tile, depth), lambda i, s=first + number: (i, s)))
    out_spec = pl.BlockSpec((length, tile), lambda i: (0, i))
    operands = list(lefts) + [right] * pairs
    if got is not None:
        specs.append(out_spec)
        operands.append(got)
    return pl.pallas_call(
        partial(back_kernel, pairs),
        grid=(width // tile,),
        in_specs=specs,
        out_specs=out_spec,
        out_shape=jax.ShapeDtypeStruct((length, width), kind),
        compiler_params=pltpu.CompilerParams(vmem_limit_bytes=48 * 2**20),
        cost_estimate=pl.CostEstimate(
            flops=2 * pairs * length * depth * width // share,
            bytes_accessed=2 * pairs * (length + width) * depth // share,
            transcendentals=0,
        ),
        name="back_product",
    )(*operands)


def weight_kernel(*refs):
    out_ref = refs[-1]
    total = None
    for left, right in zip(refs[:GROUP], refs[GROUP : 2 * GROUP]):
        part = dot(left[...], right[...], 0, 0)
        total = part if total is None else total + part
    out_ref[...] = total.astype(BF16)


def weight_product(lefts, rights, columns, place, into=None, rows=512):
    length, depth = lefts[0].shape
    width = rights[0].shape[1]
    specs = [pl.BlockSpec((length, rows), lambda i: (0, i))] * GROUP
    specs += [pl.BlockSpec((length, width), lambda i: (0, 0))] * GROUP
    operands = [*lefts, *rights]
    if into is not None:
        specs.append(pl.BlockSpec(memory_space=pl.ANY))
        operands.append(into)
    return pl.pallas_call(
        weight_kernel,
        grid=(depth // rows,),
        in_specs=specs,
        out_specs=pl.BlockSpec((rows, width), lambda i: (i, place)),
        out_shape=jax.ShapeDtypeStruct((depth, columns), BF16),
        input_output_aliases={} if into is None else {2 * GROUP: 0},
        compiler_params=pltpu.CompilerParams(vmem_limit_bytes=48 * 2**20),
        cost_estimate=pl.CostEstimate(
            flops=GROUP * length * depth * width // 32,
            bytes_accessed=GROUP * length * (depth + width) // 32,
            transcendentals=0,
        ),
        name="weight_product",
    )(*operands)


def project_kernel(left_ref, right_ref, out_ref):
    out_ref[...] = dot(left_ref[...], right_ref[...]).astype(BF16)


def project(left, right, tile=384):
    (length, depth), width = left.shape, right.shape[1]
    return pl.pallas_call(
        project_kernel,
        grid=(width // tile,),
        in_specs=[
            pl.BlockSpec((length, depth), lambda i: (0, 0)),
            pl.BlockSpec((depth, tile), lambda i: (0, i)),
        ],
        out_specs=pl.BlockSpec((length, tile), lambda i: (0, i)),
        out_shape=jax.ShapeDtypeStruct((length, width), BF16),
        compiler_params=pltpu.CompilerParams(vmem_limit_bytes=48 * 2**20),
        cost_estimate=pl.CostEstimate(flops=0, bytes_accessed=length * depth, transcendentals=0),
        name="project",
    )(left, right)


def raise_kernel(*refs):
    mids, (gate_ref, up_ref), outs = refs[:GROUP], refs[GROUP : GROUP + 2], refs[GROUP + 2 :]
    for k, mid_ref in enumerate(mids):
        gate = dot(mid_ref[...], gate_ref[...])
        up = dot(mid_ref[...], up_ref[...])
        outs[k][...] = (gate * jax.nn.sigmoid(gate) * up).astype(BF16)
        outs[GROUP + k][...] = gate
        outs[2 * GROUP + k][...] = up


def raise_up(mids, weight, tile=256):
    length, depth = mids[0].shape
    count = FF_Q // tile
    out_spec = pl.BlockSpec((length, tile), lambda i: (0, i))
    low = jax.ShapeDtypeStruct((length, FF_Q), BF16)
    high = jax.ShapeDtypeStruct((length, FF_Q), F32)
    outs = pl.pallas_call(
        raise_kernel,
        grid=(count,),
        in_specs=[pl.BlockSpec((length, depth), lambda i: (0, 0))] * GROUP
        + [
            pl.BlockSpec((depth, tile), lambda i: (0, i)),
            pl.BlockSpec((depth, tile), lambda i: (0, i + count)),
        ],
        out_specs=[out_spec] * (3 * GROUP),
        out_shape=[low] * GROUP + [high] * (2 * GROUP),
        compiler_params=pltpu.CompilerParams(vmem_limit_bytes=48 * 2**20),
        cost_estimate=pl.CostEstimate(flops=0, bytes_accessed=length * depth, transcendentals=0),
        name="raise_up",
    )(*mids, weight, weight)
    return outs[:GROUP], outs[GROUP : 2 * GROUP], outs[2 * GROUP :]


def raise_back_kernel(*refs):
    grads, down_ref, gates = refs[:GROUP], refs[GROUP], refs[GROUP + 1 : 2 * GROUP + 1]
    ups, outs = refs[2 * GROUP + 1 : 3 * GROUP + 1], refs[3 * GROUP + 1 :]
    for k in range(GROUP):
        grad_hidden = dot(grads[k][...], down_ref[...])
        gate = gates[k][...]
        sigmoid = jax.nn.sigmoid(gate)
        slope = sigmoid * (1.0 + gate * (1.0 - sigmoid))
        outs[k][...] = (grad_hidden * ups[k][...] * slope).astype(BF16)
        outs[GROUP + k][...] = (grad_hidden * gate * sigmoid).astype(BF16)


def raise_back(grads, weight, gates, ups, tile=256):
    length, depth = grads[0].shape
    count = FF_Q // tile
    spec = pl.BlockSpec((length, tile), lambda i: (0, i))
    kind = jax.ShapeDtypeStruct((length, FF_Q), BF16)
    outs = pl.pallas_call(
        raise_back_kernel,
        grid=(count,),
        in_specs=[pl.BlockSpec((length, depth), lambda i: (0, 0))] * GROUP
        + [pl.BlockSpec((depth, tile), lambda i: (0, i + 2 * count))]
        + [spec] * (2 * GROUP),
        out_specs=[spec] * (2 * GROUP),
        out_shape=[kind] * (2 * GROUP),
        compiler_params=pltpu.CompilerParams(vmem_limit_bytes=48 * 2**20),
        cost_estimate=pl.CostEstimate(flops=0, bytes_accessed=length * depth, transcendentals=0),
        name="raise_back",
    )(*grads, weight, *gates, *ups)
    return outs[:GROUP], outs[GROUP:]


def assemble_kernel(place_ref, *refs):
    out_ref = refs[-1]
    number = pl.program_id(0)
    for step, ref in enumerate(refs[:-1]):

        @pl.when(number == step)
        def _():
            out_ref[0, 0] = ref[...]


def assemble(layer, copy, layers, pieces):
    rows, cols = pieces[0].shape

    def target(i, place):
        step, part = i // 2, i % 2
        source = place[0] - step
        source = jnp.where(source < 0, source + layers, source)
        part = jnp.where(step == 0, part, jnp.where(part == 0, place[1], 1 - place[1]))
        return source, part, 0, 0

    return pl.pallas_call(
        assemble_kernel,
        grid_spec=pltpu.PrefetchScalarGridSpec(
            num_scalar_prefetch=1,
            grid=(2 * layers,),
            in_specs=[pl.BlockSpec((rows, cols), lambda i, place: (0, 0))] * (2 * layers),
            out_specs=pl.BlockSpec((1, 1, rows, cols), target),
        ),
        out_shape=jax.ShapeDtypeStruct((layers, 2, rows, cols), pieces[0].dtype),
        compiler_params=pltpu.CompilerParams(vmem_limit_bytes=48 * 2**20),
        cost_estimate=pl.CostEstimate(flops=0, bytes_accessed=rows * cols, transcendentals=0),
        name="assemble",
    )(jnp.stack([layer, copy]), *pieces)


def interleave_kernel(core_ref, own_ref, other_ref, out_ref):
    rows = own_ref.shape[0]
    first = core_ref[0] == 0
    own, other = own_ref[...], other_ref[...]
    out_ref[0:rows] = jnp.where(first, own, other)
    out_ref[rows : 2 * rows] = jnp.where(first, other, own)


def interleave(core, own, other, rows):
    total, cols = own.shape
    spec = pl.BlockSpec((rows, cols), lambda i: (i, 0))
    return pl.pallas_call(
        interleave_kernel,
        grid=(total // rows,),
        in_specs=[pl.BlockSpec(memory_space=pltpu.SMEM), spec, spec],
        out_specs=pl.BlockSpec((2 * rows, cols), lambda i: (i, 0)),
        out_shape=jax.ShapeDtypeStruct((2 * total, cols), own.dtype),
        cost_estimate=pl.CostEstimate(
            flops=0, bytes_accessed=8 * total * cols, transcendentals=0
        ),
        name="interleave",
    )(core.reshape(1), own, other)


def orthonormal_kernel(source, target):
    left = source[...]
    number = lax.broadcasted_iota(jnp.int32, (left.shape[0], 1), 0)
    for step in range(left.shape[0]):
        row = left[step : step + 1]
        row = row * lax.rsqrt(jnp.sum(row * row, -1, keepdims=True))
        share = jnp.sum(left * row, -1, keepdims=True)
        left = jnp.where(
            number > step, left - share * row, jnp.where(number == step, row, left)
        )
    target[...] = left


def orthonormal(left):
    kind = jax.ShapeDtypeStruct(left.shape, F32)
    return pl.pallas_call(orthonormal_kernel, out_shape=kind, name="orthonormal")(left)


def after(value, *earlier):
    return lax.optimization_barrier((value, *earlier))[0]


def swap(value, bits):
    return lax.ppermute(value, "member", [(j, j ^ bits) for j in range(GROUP)])


def swap_layers(value, bits, layers):
    return lax.ppermute(value, "layer", [(z, z ^ bits) for z in range(layers)])


def ring(value, layers):
    return lax.ppermute(value, "layer", [(z, (z + 1) % layers) for z in range(layers)])


def cross(value, copies):
    return lax.ppermute(value, "replica", [(r, (r + 1) % copies) for r in range(copies)])


def sum_layers(partials):
    return lax.psum_scatter(partials, "layer", scatter_dimension=0, tiled=True)


def arrange(items, member):
    low, high = (member & 1) == 1, (member & 2) == 2
    pairs = [jnp.where(low, items[t ^ 1], items[t]) for t in range(GROUP)]
    return [jnp.where(high, pairs[t ^ 2], pairs[t]) for t in range(GROUP)]


class Line:
    def __init__(self, token):
        self.token = token

    def __call__(self, value):
        value, self.token = lax.optimization_barrier((value, self.token))
        return value

    def run(self, step, first, *others):
        return self(step(self(first), *others))


class Gather:
    def __init__(self, line, halves, layer, copy, layers, copies):
        self.line, self.layer, self.copy = line, layer, copy
        self.layers, self.copies = layers, copies
        self.halves = halves
        self.got = jnp.where(copy == 0, halves[0], halves[1])
        self.way, self.over_way, self.pieces, self.over = None, [], [], []

    def hop(self):
        self.way = ring(self.line(self.got), self.layers)

    def land(self):
        self.got = self.line(self.way)
        self.pieces.append(self.got)
        self.over_way.append(cross(self.got, self.copies))

    def land_over(self):
        self.over.append(self.line(self.over_way[len(self.over)]))

    def finish(self):
        while len(self.over) < self.layers - 1:
            if len(self.pieces) < self.layers - 1 and len(self.pieces) == len(self.over):
                self.hop()
                self.land()
            self.land_over()
        pieces = list(self.halves)
        for own, other in zip(self.pieces, self.over):
            pieces += [own, other]
        whole = assemble(self.layer, self.copy, self.layers, pieces)
        return whole.reshape(-1, whole.shape[-1])


def local(
    layers,
    copies,
    tokens,
    cotangent,
    needle_mask,
    segment_ids,
    attn_weight,
    ffn_weight,
    vector_params,
    attn_error,
    ffn_error,
    attn_momentum,
    ffn_momentum,
    attn_start,
    ffn_start,
    vector_momentum,
):
    length = tokens.shape[0]
    copy = lax.axis_index("replica")
    layer, member = lax.axis_index("layer"), lax.axis_index("member")

    gain_in = vector_params[0:D]
    gain_mid = vector_params[D : 2 * D]
    gain_head = vector_params[2 * D : 2 * D + 2 * HD]
    lambda_q_one = vector_params[2 * D + 2 * HD : 2 * D + 3 * HD]
    lambda_k_one = vector_params[2 * D + 3 * HD : 2 * D + 4 * HD]
    lambda_q_two = vector_params[2 * D + 4 * HD : 2 * D + 5 * HD]
    lambda_k_two = vector_params[2 * D + 5 * HD : 2 * D + 6 * HD]
    exp_one = jnp.exp(jnp.sum(lambda_q_one * lambda_k_one))
    exp_two = jnp.exp(jnp.sum(lambda_q_two * lambda_k_two))
    lam = (exp_one - exp_two + LAMBDA_INIT).reshape(1)

    line = Line(jnp.zeros((8, 128), F32))

    def gather(halves):
        return Gather(line, halves, layer, copy, layers, copies)

    def halves_of(block):
        rows = block.shape[0] // 2
        return block[:rows], block[rows:]

    def columns(values, width):
        return [values[:, t * width : (t + 1) * width] for t in range(GROUP)]

    def layer_block(parts):
        return jnp.concatenate(arrange(parts, member), 0)

    needles = jnp.broadcast_to(jnp.sum(needle_mask).astype(F32), (8, 128))
    needles_other = cross(needles, copies)
    qkv_parts = quarters(member, attn_weight, 3, ATTN_Q)
    qkv_got = [swap(qkv_parts[k], k) for k in (2, 3, 1)]
    needles = needles + line(needles_other)
    bits = 1
    while bits < layers:
        needles = needles + line(swap_layers(needles, bits, layers))
        bits *= 2
    qkv_got = [line(got) for got in qkv_got]
    qkv_block = layer_block([qkv_parts[0], qkv_got[2], qkv_got[0], qkv_got[1]])
    qkv_gather = gather(halves_of(qkv_block))
    qkv_gather.hop()
    ffn_parts = quarters(member, line(ffn_weight), 3, FF_Q)
    ffn_got = [swap(line(ffn_parts[k]), k) for k in (2, 3, 1)]
    out_own = line(attn_weight)[:, 3 * D :].astype(BF16)
    out_across = swap(out_own, 2)
    qkv_gather.land()
    qkv_gather.hop()
    residual_in = line(tokens).astype(F32)
    scale_in = rms_scale(residual_in, 1e-06)
    normed_in = residual_in * scale_in
    normed_low = line((normed_in * gain_in).astype(BF16))
    qkv_gather.land()
    qkv_gather.hop()
    lines = length // 128
    marks = segment_ids.reshape(lines, 128) + GROUP * needle_mask.reshape(lines, 128)
    small = jnp.concatenate([marks.astype(F32), needles[: 8 - lines % 8]])
    rows = small.shape[0]
    small_pair = jnp.concatenate([small, line(swap(line(small), 1))])
    out_across = swap(line(out_own), 2)
    qkv_gather.land()
    ffn_got = [line(got) for got in ffn_got]
    normed_across = swap(line(normed_low), 2)
    small_across = swap(small_pair, 2)
    normed_beside = swap(normed_low, 1)
    ffn_half = layer_block([ffn_parts[0], ffn_got[2], ffn_got[0], ffn_got[1]])
    ffn_half = ffn_half.reshape(2, -1, ffn_half.shape[1])
    ffn_half = line(lax.dynamic_index_in_dim(ffn_half, copy, 0, False))
    out_across = line(out_across)
    side = (member // 2) == 0
    out_gather = gather(
        (jnp.where(side, out_own, out_across), jnp.where(side, out_across, out_own))
    )
    out_gather.hop()
    qkv_gather.land_over()
    qkv_gather.land_over()
    out_gather.land()
    out_gather.hop()
    qkv_gather.land_over()
    ffn_weight_low = lax.all_gather(line(ffn_half), ("layer", "replica"), axis=0, tiled=True)
    out_gather.land()
    out_gather.hop()
    normed_across = line(normed_across)
    small_across = line(small_across)
    normed_opposite = swap(normed_across, 1)
    cotangent_across = swap(line(cotangent), 2)
    qkv_weight = qkv_gather.finish()
    normed_beside = line(normed_beside)

    def heads_of(qkv, segments):
        return attend(lam, qkv, segments, gain_head[None])

    qkv = [None] * GROUP
    heads = [None] * GROUP
    qkv[0] = line.run(project, normed_low, qkv_weight)
    qkv[1] = line.run(project, normed_beside, qkv_weight)
    small_beside, small_own = small_pair[rows:], small_pair[:rows]

    def marks_of(part):
        marks = part[:lines].reshape(length)
        mask = (marks >= GROUP).astype(F32)
        return marks - GROUP * mask, mask

    segments, masks = [None] * GROUP, [None] * GROUP
    segments[0], masks[0] = marks_of(small_own)
    segments[1], masks[1] = marks_of(small_beside)
    heads[0] = line.run(heads_of, qkv[0], segments[0])
    heads[1] = line.run(heads_of, qkv[1], segments[1])
    heads_beside = swap(heads[1], 1)
    segments[2], masks[2] = marks_of(small_across[:rows])
    segments[3], masks[3] = marks_of(small_across[rows:])
    out_gather.land()
    qkv[2] = line.run(project, normed_across, qkv_weight)
    heads[2] = line.run(heads_of, qkv[2], segments[2])
    heads_across = swap(heads[2], 2)
    normed_opposite = line(normed_opposite)
    cotangent_across = line(cotangent_across)
    cotangent_near = swap(line(cotangent), 1)
    cotangent_far = swap(cotangent_across, 1)
    normed_all = [normed_low, normed_beside, normed_across, normed_opposite]
    qkv[3] = line.run(project, normed_opposite, qkv_weight)
    heads[3] = line.run(heads_of, qkv[3], segments[3])
    heads_opposite = swap(heads[3], 3)
    out_mine = out_gather.finish()
    out_rest = swap(out_mine, 1)
    heads_beside, heads_across = line(heads_beside), line(heads_across)
    out_rest = line(out_rest)
    out_weight = interleave(member % 2, out_mine, out_rest, D // (layers * GROUP))
    heads_opposite = line(heads_opposite)
    heads_low = jnp.concatenate(
        arrange([heads[0], heads_beside, heads_across, heads_opposite], member), 1
    )
    residual_mid = line.run(lambda x: residual_in + dot(x, out_weight), heads_low)
    scale_mid = rms_scale(residual_mid, 1e-06)
    normed_mid = residual_mid * scale_mid
    mid_low = line((normed_mid * gain_mid).astype(BF16))
    mid_across = swap(mid_low, 2)
    mid_beside = swap(mid_low, 1)
    mid_across = line(mid_across)
    mid_opposite = swap(mid_across, 1)
    heads_across_all = swap(line(heads_low), 2)
    small = jnp.concatenate([small_pair, small_across])
    needles = sum([small[k * rows + lines, 0] for k in range(GROUP)])
    everyone = length * layers * GROUP * copies
    weight_total = everyone + NEEDLE * needles

    def grad_of(cotangent, k):
        loss_weights = 1.0 + NEEDLE * masks[k]
        return cotangent.astype(F32) * (loss_weights * (everyone / weight_total))[:, None]

    mid_beside, mid_opposite = line(mid_beside), line(mid_opposite)
    cotangents = [cotangent, line(cotangent_near), cotangent_across, line(cotangent_far)]
    grad_out = grad_of(cotangent, 0)
    grad_out_all = [line(grad_of(one, k).astype(BF16)) for k, one in enumerate(cotangents)]
    ffn_weight_low = line(ffn_weight_low)

    def product(lefts, rights, columns, place, into=None):
        return line.run(
            lambda x: weight_product([x, *lefts[1:]], rights, columns, place, into), lefts[0]
        )

    mid_all = [mid_low, mid_beside, mid_across, mid_opposite]
    hidden, gate_proj, up_proj = line.run(
        lambda x: raise_up([x, *mid_all[1:]], ffn_weight_low), mid_low
    )
    grad_gate, grad_up = line.run(
        lambda x: raise_back([x, *grad_out_all[1:]], ffn_weight_low, gate_proj, up_proj),
        grad_out_all[0],
    )
    ffn_partial = product(grad_out_all, hidden, 3 * FF_Q, 2)
    ffn_partial = product(mid_all, grad_gate, 3 * FF_Q, 0, ffn_partial)
    heads_across_all = line(heads_across_all)
    heads_beside_all = swap(line(heads_low), 1)
    heads_opposite_all = swap(heads_across_all, 1)
    ffn_partial = product(mid_all, grad_up, 3 * FF_Q, 1, ffn_partial)
    ffn_total = sum_layers(ffn_partial)

    def lower(k, got=None, kind=BF16):
        return line.run(
            lambda x: back_product([x, grad_up[k]], ffn_weight_low, got, kind), grad_gate[k]
        )

    def lower_hidden(k, got=None, kind=BF16):
        return line.run(
            lambda x: back_product([x], ffn_weight_low, got, kind, first=2), hidden[k]
        )

    opposite_got = swap(lower(3), 1)
    beside_got = swap(lower(1), 1)
    opposite_got = line(opposite_got)
    beside_got = line(beside_got)
    mid_sum = swap(lower(2, opposite_got), 2)
    grad_mid_own = lower(0, beside_got, F32)
    ffn_opposite_got = swap(lower_hidden(3), 1)
    ffn_beside_got = swap(lower_hidden(1), 1)
    mid_sum = line(mid_sum)

    grad_mid_low = grad_mid_own + mid_sum.astype(F32)
    grad_gain_mid = jnp.sum(grad_mid_low * normed_mid, 0)
    grad_mid = grad_out + norm_back(grad_mid_low * gain_mid, normed_mid, scale_mid)
    grad_attn_low = grad_mid.astype(BF16)
    grad_heads = line.run(lambda x: dot(x, out_weight, 1, 1).astype(BF16), grad_attn_low)
    grad_heads = arrange(columns(grad_heads, ATTN_Q), member)
    grad_heads_got = [swap(grad_heads[k], k) for k in (2, 3, 1)]
    grad_attn = arrange(columns(grad_attn_low, ATTN_Q), member)

    def back(grad, k):
        return attend_back(lam, qkv[k], segments[k], gain_head[None], grad)

    grad_qkv, stats = [None] * GROUP, [None] * GROUP
    grad_qkv[0], stats[0] = line.run(back, grad_heads[0], 0)
    grad_qkv[1], stats[1] = line.run(back, line(grad_heads_got[2]), 1)
    grad_heads_across, grad_heads_opposite = line(grad_heads_got[0]), line(grad_heads_got[1])
    grad_attn_got = [swap(line(grad_attn[k]), k) for k in (2, 3, 1)]
    grad_qkv[2], stats[2] = line.run(back, grad_heads_across, 2)
    grad_attn_got = [line(got) for got in grad_attn_got]
    heads_all = [heads_low, line(heads_beside_all), heads_across_all, line(heads_opposite_all)]
    grad_attn_all = [grad_attn[0], grad_attn_got[2], grad_attn_got[0], grad_attn_got[1]]
    ffn_opposite_got = line(ffn_opposite_got)
    ffn_sum = swap(lower_hidden(2, ffn_opposite_got), 2)
    attn_partial = product(heads_all, grad_attn_all, 4 * ATTN_Q, 3)
    grad_qkv[3], stats[3] = line.run(back, grad_heads_opposite, 3)
    attn_partial = product(normed_all, grad_qkv, 4 * ATTN_Q, 0, attn_partial)
    attn_total = sum_layers(attn_partial)
    ffn_sum = line(ffn_sum)
    stats = sum(stats)
    grad_gain_head, grad_lambda = stats[0], stats[1, 0]

    def lower_in(k, got=None, kind=BF16):
        return line.run(
            lambda x: back_product([x], qkv_weight, got, kind, share=1), grad_qkv[k]
        )

    def rows_of(total):
        size = total.shape[0] // GROUP
        return arrange([total[t * size : (t + 1) * size] for t in range(GROUP)], member)

    def share(parts):
        return [parts[0]] + [swap(line(parts[k]), k) for k in range(1, GROUP)]

    def landed(parts):
        return arrange([parts[0]] + [line(part) for part in parts[1:]], member)

    def left_of(grad, error, start):
        merged = grad + DECAY_ERROR * error[0]
        left = line.run(lambda x: dot(start[0], x, 1, 1, precision=HIGHEST), merged)
        return merged, left, cross(left, copies)

    def right_of(merged, left, other):
        ortho = orthonormal(left + line(other))
        right = line(dot(ortho, merged, 1, 0, precision=HIGHEST).astype(BF16))
        return ortho, right, cross(right, copies)

    def update(ortho, merged, right, other, momentum, weight):
        right = (right.astype(F32) + line(other).astype(F32)) / copies
        approx = dot(ortho, right, 0, 0, precision=HIGHEST)
        momentum_new = MOMENTUM * momentum + (1.0 - MOMENTUM) * approx
        weight_new = line(weight - RATE_MATRIX * momentum_new)
        return right, merged - approx, momentum_new, weight_new

    in_opposite_got = swap(lower_in(3), 1)
    in_beside_got = swap(lower_in(1), 1)
    ffn_shares = share(rows_of(line(ffn_total)))
    in_opposite_got = line(in_opposite_got)
    in_sent = lower_in(2, in_opposite_got)
    in_beside_got = line(in_beside_got)
    in_own = lower_in(0, in_beside_got, F32)
    ffn_own = lower_hidden(0, line(ffn_beside_got), F32)
    mixed = line((residual_mid + ffn_own + ffn_sum.astype(F32)).astype(BF16))
    ffn_rows = landed(ffn_shares)
    in_sum = swap(line(in_sent), 2)
    ffn_grad = jnp.concatenate(
        [part[:, s * FF_Q : (s + 1) * FF_Q] for s in range(3) for part in ffn_rows], 1
    ).astype(F32)
    merged_ffn, left_ffn, left_ffn_other = left_of(ffn_grad, ffn_error, ffn_start)
    ortho_ffn, right_ffn, right_ffn_other = right_of(merged_ffn, left_ffn, left_ffn_other)
    right_ffn, ffn_error_new, ffn_momentum_new, ffn_weight_new = update(
        ortho_ffn, merged_ffn, right_ffn, right_ffn_other, ffn_momentum, ffn_weight
    )
    in_sum = line(in_sum)
    grad_in_low = in_own + in_sum.astype(F32)
    grad_gain_in = line(jnp.sum(grad_in_low * normed_in, 0))
    vector_grad = jnp.concatenate(
        [
            grad_gain_in,
            grad_gain_mid,
            grad_gain_head,
            grad_lambda * exp_one * lambda_k_one,
            grad_lambda * exp_one * lambda_q_one,
            -grad_lambda * exp_two * lambda_k_two,
            -grad_lambda * exp_two * lambda_q_two,
        ]
    ).reshape(-1, 128)
    attn_shares = share(rows_of(line(attn_total)))
    attn_rows = landed(attn_shares)
    attn_grad = jnp.concatenate(
        [part[:, s * ATTN_Q : (s + 1) * ATTN_Q] for s in range(4) for part in attn_rows],
        1,
    ).astype(F32)
    merged_attn, left_attn, left_attn_other = left_of(attn_grad, attn_error, attn_start)
    vector_other = cross(line(vector_grad), copies)
    ortho_attn, right_attn, right_attn_other = right_of(merged_attn, left_attn, left_attn_other)
    vector_grad = vector_grad + line(vector_other)
    vector_other = swap(vector_grad, 1)
    grad_tokens = line(grad_mid + norm_back(grad_in_low * gain_in, normed_in, scale_in))
    right_attn, attn_error_new, attn_momentum_new, attn_weight_new = update(
        ortho_attn, merged_attn, right_attn, right_attn_other, attn_momentum, attn_weight
    )
    vector_grad = vector_grad + line(vector_other)
    bits = 1
    while bits < layers:
        vector_grad = vector_grad + line(swap_layers(vector_grad, bits, layers))
        bits *= 2
    vector_grad = (vector_grad + line(swap(vector_grad, 2))).reshape(-1)
    vector_grad = vector_grad + line.token[0, 0]
    vector_momentum_new = MOMENTUM * vector_momentum + (1.0 - MOMENTUM) * vector_grad
    vector_new = vector_params - RATE_VECTOR * vector_momentum_new
    return (
        mixed,
        grad_tokens,
        attn_grad[None],
        ffn_grad[None],
        ortho_attn,
        ortho_ffn,
        right_attn[None],
        right_ffn[None],
        attn_error_new[None],
        ffn_error_new[None],
        attn_momentum_new,
        ffn_momentum_new,
        attn_weight_new,
        ffn_weight_new,
        vector_momentum_new,
        vector_new,
    )


def solution(mesh):
    copies, shards = mesh.shape["replica"], mesh.shape["fsdp"]
    layers = shards // GROUP
    mesh = jax.sharding.Mesh(
        mesh.devices.reshape(copies, layers, GROUP), ("replica", "layer", "member")
    )
    fsdp = ("layer", "member")
    everywhere = ("replica", *fsdp)
    in_specs = (
        P(everywhere, None),
        P(everywhere, None),
        P(everywhere),
        P(everywhere, None),
        P(fsdp, None),
        P(fsdp, None),
        P(),
        P("replica", fsdp, None),
        P("replica", fsdp, None),
        P(fsdp, None),
        P(fsdp, None),
        P(fsdp, None, None),
        P(fsdp, None, None),
        P(),
    )
    out_specs = (
        P(everywhere, None),
        P(everywhere, None),
        P("replica", fsdp, None),
        P("replica", fsdp, None),
        P(None, fsdp),
        P(None, fsdp),
        P(fsdp, None, None),
        P(fsdp, None, None),
        P("replica", fsdp, None),
        P("replica", fsdp, None),
        P(fsdp, None),
        P(fsdp, None),
        P(fsdp, None),
        P(fsdp, None),
        P(),
        P(),
    )
    step = partial(local, layers, copies)
    return jax.shard_map(step, mesh=mesh, in_specs=in_specs, out_specs=out_specs, check_vma=False)
```

```python
from functools import partial

import jax
import jax.numpy as jnp
from jax import lax
from jax.experimental import pallas as pl
from jax.experimental.pallas import tpu as pltpu
from jax.sharding import PartitionSpec as P

D = 1536
HEADS = 12
HD = 64
FF = 4096

NEEDLE = 3.0
LAMBDA_INIT = 0.2
KEEP = 1.0 - LAMBDA_INIT
DECAY_ERROR = 0.5
MOMENTUM = 0.9
RATE_MATRIX = 0.005
RATE_VECTOR = 0.02
MASKED = -1e30
HIGHEST = lax.Precision.HIGHEST
BF16 = jnp.bfloat16
F32 = jnp.float32

GROUP = 4
BLOCK = 128
REACH = 256
WIDTH = 2 * HD
OWN_HEADS = HEADS // GROUP
ATTN_Q = D // GROUP
FF_Q = FF // GROUP


def rms_scale(values, epsilon):
    return lax.rsqrt(jnp.mean(values * values, -1, keepdims=True) + epsilon)


def norm_back(grad_normed, normed, scale):
    return scale * (grad_normed - normed * jnp.mean(grad_normed * normed, -1, keepdims=True))


def dot(left, right, left_dim=1, right_dim=0, **kinds):
    return lax.dot_general(
        left, right, (((left_dim,), (right_dim,)), ((), ())), preferred_element_type=F32, **kinds
    )


def score_parts(qkv_ref, head, block, low, high, lam, bias):
    rows, reach = pl.ds(block * BLOCK, BLOCK), pl.ds(low, high - low)
    first = lax.broadcasted_iota(jnp.int32, (1, WIDTH), 1) < HD
    query = qkv_ref[rows, head * WIDTH : (head + 1) * WIDTH] * BF16(HD**-0.5)
    key = qkv_ref[reach, ATTN_Q + head * WIDTH : ATTN_Q + (head + 1) * WIDTH]
    value = qkv_ref[reach, 2 * ATTN_Q + head * WIDTH : 2 * ATTN_Q + (head + 1) * WIDTH]
    zero = jnp.zeros((), BF16)
    queries = jnp.concatenate(
        [jnp.where(first, query, zero), jnp.where(first, zero, query)], 0
    )
    score = dot(queries, key, 1, 1) + jnp.concatenate([bias, bias], 0)
    expo = jnp.exp(score - jnp.max(score, -1, keepdims=True))
    probs = expo * (1.0 / jnp.sum(expo, -1, keepdims=True))
    mixture = (probs[:BLOCK] - lam * probs[BLOCK:]).astype(BF16)
    return queries, key, value, probs, mixture


def column_of(row):
    rows = lax.broadcasted_iota(jnp.int32, (BLOCK, BLOCK), 0)
    cols = lax.broadcasted_iota(jnp.int32, (BLOCK, BLOCK), 1)
    return jnp.sum(jnp.where(rows == cols, row, 0.0), -1, keepdims=True)


def documents_of(marks):
    return jnp.where(marks >= GROUP, marks - GROUP, marks)


def block_bias(marks_ref, block, low, high):
    rows = lax.broadcasted_iota(jnp.int32, (BLOCK, high - low), 0) + block * BLOCK
    cols = lax.broadcasted_iota(jnp.int32, (BLOCK, high - low), 1) + low
    keys = jnp.concatenate(
        [marks_ref[b : b + 1, :] for b in range(low // BLOCK, high // BLOCK)], 1
    )
    queries = column_of(marks_ref[block : block + 1, :])
    same = documents_of(queries) == documents_of(keys)
    return jnp.where((cols <= rows) & same, 0.0, MASKED)


def reach_of(block):
    return max(0, block - REACH // BLOCK) * BLOCK, (block + 1) * BLOCK


def attend_kernel(lam_ref, qkv_ref, marks_ref, gain_ref, heads_ref):
    lam = lam_ref[0]
    gain = gain_ref[...] * KEEP
    for block in range(qkv_ref.shape[0] // BLOCK):
        low, high = reach_of(block)
        bias = block_bias(marks_ref, block, low, high)
        for head in range(OWN_HEADS):
            _, _, value, _, mixture = score_parts(qkv_ref, head, block, low, high, lam, bias)
            out = dot(mixture, value)
            normed = out * rms_scale(out, 1e-05)
            heads_ref[pl.ds(block * BLOCK, BLOCK), head * WIDTH : (head + 1) * WIDTH] = (
                normed * gain
            ).astype(BF16)


def attend_back_kernel(
    lam_ref, qkv_ref, marks_ref, gain_ref, grad_ref, out_ref, stat_ref, dk_ref, dv_ref
):
    lam = lam_ref[0]
    gain = gain_ref[...] * KEEP
    blocks = qkv_ref.shape[0] // BLOCK
    first = lax.broadcasted_iota(jnp.int32, (1, WIDTH), 1) < HD
    upper = lax.broadcasted_iota(jnp.int32, (2 * BLOCK, 1), 0) < BLOCK
    share = jnp.where(upper, 1.0, -lam)
    gain_total = jnp.zeros((1, WIDTH), F32)
    lam_total = jnp.zeros((1, 1), F32)
    biases = [block_bias(marks_ref, b, *reach_of(b)) for b in range(blocks)]
    for head in range(OWN_HEADS):
        lanes = slice(head * WIDTH, (head + 1) * WIDTH)
        dk_ref[...] = jnp.zeros_like(dk_ref)
        dv_ref[...] = jnp.zeros_like(dv_ref)
        for block in range(blocks):
            low, high = reach_of(block)
            rows, reach = pl.ds(block * BLOCK, BLOCK), pl.ds(low, high - low)
            queries, key, value, probs, mixture = score_parts(
                qkv_ref, head, block, low, high, lam, biases[block]
            )
            out = dot(mixture, value)
            scale = rms_scale(out, 1e-05)
            normed = out * scale
            grad = grad_ref[rows, lanes].astype(F32)
            gain_total = gain_total + jnp.sum(grad * normed, 0, keepdims=True)
            grad_out = norm_back(grad * gain, normed, scale).astype(BF16)
            grad_mix = dot(grad_out, value, 1, 1)
            grad_mix = jnp.concatenate([grad_mix, grad_mix], 0)
            mean = jnp.sum(grad_mix * probs, -1, keepdims=True)
            lam_total = lam_total - jnp.sum(mean[BLOCK:], 0, keepdims=True)
            low_scores = (probs * (share * (grad_mix - mean))).astype(BF16)
            dv_ref[reach, :] += dot(mixture, grad_out, 0, 0)
            dk_ref[reach, :] += dot(low_scores, queries, 0, 0)
            grad_query = dot(low_scores, key)
            grad_query = jnp.where(first, grad_query[:BLOCK], grad_query[BLOCK:])
            out_ref[rows, lanes] = (grad_query * HD**-0.5).astype(BF16)
        out_ref[:, ATTN_Q + head * WIDTH : ATTN_Q + (head + 1) * WIDTH] = dk_ref[...].astype(BF16)
        out_ref[:, 2 * ATTN_Q + head * WIDTH : 2 * ATTN_Q + (head + 1) * WIDTH] = dv_ref[
            ...
        ].astype(BF16)
    stat_ref[0:1, :] = gain_total * KEEP
    stat_ref[1:2, :] = jnp.broadcast_to(lam_total, (1, WIDTH))
    stat_ref[2:8, :] = jnp.zeros((6, WIDTH), F32)


def attention_specs(length, lines, part):
    return [
        pl.BlockSpec(memory_space=pltpu.SMEM),
        pl.BlockSpec((length, 3 * ATTN_Q), lambda i: (0, 0)),
        pl.BlockSpec((lines, BLOCK), lambda i: (part, 0)),
        pl.BlockSpec((1, WIDTH), lambda i: (0, 0)),
    ]


def attend(lam, qkv, marks, part, lines, gain):
    length = qkv.shape[0]
    return pl.pallas_call(
        attend_kernel,
        grid=(1,),
        in_specs=attention_specs(length, lines, part),
        out_specs=pl.BlockSpec((length, ATTN_Q), lambda i: (0, 0)),
        out_shape=jax.ShapeDtypeStruct((length, ATTN_Q), BF16),
        compiler_params=pltpu.CompilerParams(vmem_limit_bytes=40 * 2**20),
        cost_estimate=pl.CostEstimate(
            flops=0, bytes_accessed=length * ATTN_Q, transcendentals=0
        ),
        name="attend",
    )(lam, qkv, marks, gain)


def attend_back(lam, qkv, marks, part, lines, gain, grad):
    length = qkv.shape[0]
    return pl.pallas_call(
        attend_back_kernel,
        grid=(1,),
        in_specs=attention_specs(length, lines, part)
        + [pl.BlockSpec((length, ATTN_Q), lambda i: (0, 0))],
        out_specs=[
            pl.BlockSpec((length, 3 * ATTN_Q), lambda i: (0, 0)),
            pl.BlockSpec((8, WIDTH), lambda i: (0, 0)),
        ],
        out_shape=[
            jax.ShapeDtypeStruct((length, 3 * ATTN_Q), BF16),
            jax.ShapeDtypeStruct((8, WIDTH), F32),
        ],
        scratch_shapes=[pltpu.VMEM((length, WIDTH), F32), pltpu.VMEM((length, WIDTH), F32)],
        compiler_params=pltpu.CompilerParams(vmem_limit_bytes=40 * 2**20),
        cost_estimate=pl.CostEstimate(
            flops=0, bytes_accessed=length * ATTN_Q, transcendentals=0
        ),
        name="attend_back",
    )(lam, qkv, marks, gain, grad)


def loss_kernel(everyone, lines, *refs):
    cotangents, smalls, outs = refs[:GROUP], refs[GROUP : 2 * GROUP], refs[2 * GROUP :]
    block = pl.program_id(0)
    needles = sum([small[lines : lines + 1, :] for small in smalls])
    scale = everyone / (everyone + NEEDLE * needles[:, 0:1])
    for k in range(GROUP):
        marks = column_of(smalls[k][pl.ds(block, 1), :])
        weights = 1.0 + NEEDLE * jnp.where(marks >= GROUP, 1.0, 0.0)
        grad = cotangents[k][...].astype(F32) * (weights * scale)
        outs[k][...] = grad.astype(BF16)
        if k == 0:
            outs[GROUP][...] = grad


def loss_gradients(everyone, lines, cotangents, smalls):
    length, width = cotangents[0].shape
    spec = pl.BlockSpec((BLOCK, width), lambda i: (i, 0))
    rows = smalls[0][0].shape[0]
    low = jax.ShapeDtypeStruct((length, width), BF16)
    return pl.pallas_call(
        partial(loss_kernel, everyone, lines),
        grid=(length // BLOCK,),
        in_specs=[spec] * GROUP
        + [pl.BlockSpec((rows, BLOCK), lambda i, p=part: (p, 0)) for _, part in smalls],
        out_specs=[spec] * (GROUP + 1),
        out_shape=[low] * GROUP + [jax.ShapeDtypeStruct((length, width), F32)],
        compiler_params=pltpu.CompilerParams(vmem_limit_bytes=40 * 2**20),
        cost_estimate=pl.CostEstimate(flops=0, bytes_accessed=length * width, transcendentals=0),
        name="loss_gradients",
    )(*cotangents, *[small for small, _ in smalls])


def quarter_kernel(member_ref, *refs):
    for source, target in zip(refs[:GROUP], refs[GROUP:]):
        target[...] = source[...].astype(BF16)


def quarters(member, weight, sections, width):
    rows = weight.shape[0]

    def columns(bits):
        return lambda i, member: (0, i * GROUP + (member[0] ^ bits))

    kind = jax.ShapeDtypeStruct((rows, sections * width), BF16)
    return pl.pallas_call(
        quarter_kernel,
        grid_spec=pltpu.PrefetchScalarGridSpec(
            num_scalar_prefetch=1,
            grid=(sections,),
            in_specs=[pl.BlockSpec((rows, width), columns(bits)) for bits in range(GROUP)],
            out_specs=[pl.BlockSpec((rows, width), lambda i, member: (0, i))] * GROUP,
        ),
        out_shape=[kind] * GROUP,
        compiler_params=pltpu.CompilerParams(vmem_limit_bytes=40 * 2**20),
        cost_estimate=pl.CostEstimate(flops=0, bytes_accessed=rows * width, transcendentals=0),
        name="quarters",
    )(member.reshape(1), *[weight] * GROUP)


def back_kernel(pairs, *refs):
    total = None
    for left, right in zip(refs[:pairs], refs[pairs : 2 * pairs]):
        part = dot(left[...], right[...], 1, 1)
        total = part if total is None else total + part
    if len(refs) > 2 * pairs + 1:
        total = total + refs[2 * pairs][...].astype(F32)
    refs[-1][...] = total.astype(refs[-1].dtype)


def back_product(lefts, right, got=None, kind=BF16, tile=512, first=0, share=32):
    pairs, (length, depth) = len(lefts), lefts[0].shape
    width = right.shape[0]
    specs = [pl.BlockSpec((length, depth), lambda i: (0, 0))] * pairs
    for number in range(pairs):
        specs.append(pl.BlockSpec((tile, depth), lambda i, s=first + number: (i, s)))
    out_spec = pl.BlockSpec((length, tile), lambda i: (0, i))
    operands = list(lefts) + [right] * pairs
    if got is not None:
        specs.append(out_spec)
        operands.append(got)
    return pl.pallas_call(
        partial(back_kernel, pairs),
        grid=(width // tile,),
        in_specs=specs,
        out_specs=out_spec,
        out_shape=jax.ShapeDtypeStruct((length, width), kind),
        compiler_params=pltpu.CompilerParams(vmem_limit_bytes=40 * 2**20),
        cost_estimate=pl.CostEstimate(
            flops=2 * pairs * length * depth * width // share,
            bytes_accessed=2 * pairs * (length + width) * depth // share,
            transcendentals=0,
        ),
        name="back_product",
    )(*operands)


def weight_kernel(*refs):
    out_ref = refs[-1]
    total = None
    for left, right in zip(refs[:GROUP], refs[GROUP : 2 * GROUP]):
        part = dot(left[...], right[...], 0, 0)
        total = part if total is None else total + part
    out_ref[...] = total.astype(BF16)


def weight_product(lefts, rights, columns, place, into=None, rows=512):
    length, depth = lefts[0].shape
    width = rights[0].shape[1]
    specs = [pl.BlockSpec((length, rows), lambda i: (0, i))] * GROUP
    specs += [pl.BlockSpec((length, width), lambda i: (0, 0))] * GROUP
    operands = [*lefts, *rights]
    if into is not None:
        specs.append(pl.BlockSpec(memory_space=pl.ANY))
        operands.append(into)
    return pl.pallas_call(
        weight_kernel,
        grid=(depth // rows,),
        in_specs=specs,
        out_specs=pl.BlockSpec((rows, width), lambda i: (i, place)),
        out_shape=jax.ShapeDtypeStruct((depth, columns), BF16),
        input_output_aliases={} if into is None else {2 * GROUP: 0},
        compiler_params=pltpu.CompilerParams(vmem_limit_bytes=40 * 2**20),
        cost_estimate=pl.CostEstimate(
            flops=GROUP * length * depth * width // 32,
            bytes_accessed=GROUP * length * (depth + width) // 32,
            transcendentals=0,
        ),
        name="weight_product",
    )(*operands)


def project_kernel(left_ref, right_ref, out_ref):
    out_ref[...] = dot(left_ref[...], right_ref[...]).astype(BF16)


def project(left, right, tile=384):
    (length, depth), width = left.shape, right.shape[1]
    return pl.pallas_call(
        project_kernel,
        grid=(width // tile,),
        in_specs=[
            pl.BlockSpec((length, depth), lambda i: (0, 0)),
            pl.BlockSpec((depth, tile), lambda i: (0, i)),
        ],
        out_specs=pl.BlockSpec((length, tile), lambda i: (0, i)),
        out_shape=jax.ShapeDtypeStruct((length, width), BF16),
        compiler_params=pltpu.CompilerParams(vmem_limit_bytes=40 * 2**20),
        cost_estimate=pl.CostEstimate(flops=0, bytes_accessed=length * depth, transcendentals=0),
        name="project",
    )(left, right)


def raise_kernel(*refs):
    mids, (gate_ref, up_ref), outs = refs[:GROUP], refs[GROUP : GROUP + 2], refs[GROUP + 2 :]
    for k, mid_ref in enumerate(mids):
        gate = dot(mid_ref[...], gate_ref[...])
        up = dot(mid_ref[...], up_ref[...])
        outs[k][...] = (gate * jax.nn.sigmoid(gate) * up).astype(BF16)
        outs[GROUP + k][...] = gate
        outs[2 * GROUP + k][...] = up


def raise_up(mids, weight, tile=256):
    length, depth = mids[0].shape
    count = FF_Q // tile
    out_spec = pl.BlockSpec((length, tile), lambda i: (0, i))
    low = jax.ShapeDtypeStruct((length, FF_Q), BF16)
    high = jax.ShapeDtypeStruct((length, FF_Q), F32)
    outs = pl.pallas_call(
        raise_kernel,
        grid=(count,),
        in_specs=[pl.BlockSpec((length, depth), lambda i: (0, 0))] * GROUP
        + [
            pl.BlockSpec((depth, tile), lambda i: (0, i)),
            pl.BlockSpec((depth, tile), lambda i: (0, i + count)),
        ],
        out_specs=[out_spec] * (3 * GROUP),
        out_shape=[low] * GROUP + [high] * (2 * GROUP),
        compiler_params=pltpu.CompilerParams(vmem_limit_bytes=40 * 2**20),
        cost_estimate=pl.CostEstimate(flops=0, bytes_accessed=length * depth, transcendentals=0),
        name="raise_up",
    )(*mids, weight, weight)
    return outs[:GROUP], outs[GROUP : 2 * GROUP], outs[2 * GROUP :]


def raise_back_kernel(*refs):
    grads, down_ref, gates = refs[:GROUP], refs[GROUP], refs[GROUP + 1 : 2 * GROUP + 1]
    ups, outs = refs[2 * GROUP + 1 : 3 * GROUP + 1], refs[3 * GROUP + 1 :]
    for k in range(GROUP):
        grad_hidden = dot(grads[k][...], down_ref[...])
        gate = gates[k][...]
        sigmoid = jax.nn.sigmoid(gate)
        slope = sigmoid * (1.0 + gate * (1.0 - sigmoid))
        outs[k][...] = (grad_hidden * ups[k][...] * slope).astype(BF16)
        outs[GROUP + k][...] = (grad_hidden * gate * sigmoid).astype(BF16)


def raise_back(grads, weight, gates, ups, tile=256):
    length, depth = grads[0].shape
    count = FF_Q // tile
    spec = pl.BlockSpec((length, tile), lambda i: (0, i))
    kind = jax.ShapeDtypeStruct((length, FF_Q), BF16)
    outs = pl.pallas_call(
        raise_back_kernel,
        grid=(count,),
        in_specs=[pl.BlockSpec((length, depth), lambda i: (0, 0))] * GROUP
        + [pl.BlockSpec((depth, tile), lambda i: (0, i + 2 * count))]
        + [spec] * (2 * GROUP),
        out_specs=[spec] * (2 * GROUP),
        out_shape=[kind] * (2 * GROUP),
        compiler_params=pltpu.CompilerParams(vmem_limit_bytes=40 * 2**20),
        cost_estimate=pl.CostEstimate(flops=0, bytes_accessed=length * depth, transcendentals=0),
        name="raise_back",
    )(*grads, weight, *gates, *ups)
    return outs[:GROUP], outs[GROUP:]


def assemble_kernel(place_ref, *refs):
    out_ref = refs[-1]
    number = pl.program_id(0)
    for step, ref in enumerate(refs[:-1]):

        @pl.when(number == step)
        def _():
            out_ref[0, 0] = ref[...]


def assemble(layer, copy, layers, pieces):
    rows, cols = pieces[0].shape

    def target(i, place):
        step, part = i // 2, i % 2
        source = place[0] - step
        source = jnp.where(source < 0, source + layers, source)
        part = jnp.where(step == 0, part, jnp.where(part == 0, place[1], 1 - place[1]))
        return source, part, 0, 0

    return pl.pallas_call(
        assemble_kernel,
        grid_spec=pltpu.PrefetchScalarGridSpec(
            num_scalar_prefetch=1,
            grid=(2 * layers,),
            in_specs=[pl.BlockSpec((rows, cols), lambda i, place: (0, 0))] * (2 * layers),
            out_specs=pl.BlockSpec((1, 1, rows, cols), target),
        ),
        out_shape=jax.ShapeDtypeStruct((layers, 2, rows, cols), pieces[0].dtype),
        compiler_params=pltpu.CompilerParams(vmem_limit_bytes=40 * 2**20),
        cost_estimate=pl.CostEstimate(flops=0, bytes_accessed=rows * cols, transcendentals=0),
        name="assemble",
    )(jnp.stack([layer, copy]), *pieces)


def interleave_kernel(core_ref, own_ref, other_ref, out_ref):
    rows = own_ref.shape[0]
    first = core_ref[0] == 0
    own, other = own_ref[...], other_ref[...]
    out_ref[0:rows] = jnp.where(first, own, other)
    out_ref[rows : 2 * rows] = jnp.where(first, other, own)


def interleave(core, own, other, rows):
    total, cols = own.shape
    spec = pl.BlockSpec((rows, cols), lambda i: (i, 0))
    return pl.pallas_call(
        interleave_kernel,
        grid=(total // rows,),
        in_specs=[pl.BlockSpec(memory_space=pltpu.SMEM), spec, spec],
        out_specs=pl.BlockSpec((2 * rows, cols), lambda i: (i, 0)),
        out_shape=jax.ShapeDtypeStruct((2 * total, cols), own.dtype),
        cost_estimate=pl.CostEstimate(
            flops=0, bytes_accessed=8 * total * cols, transcendentals=0
        ),
        name="interleave",
    )(core.reshape(1), own, other)


def merge_kernel(member_ref, *refs):
    shares, (error_ref, start_ref), outs = refs[:GROUP], refs[GROUP : GROUP + 2], refs[GROUP + 2 :]
    grad_ref, merged_ref, left_ref = outs
    width = shares[0].shape[1]
    values = arrange([share[...].astype(F32) for share in shares], member_ref[0])

    @pl.when(pl.program_id(0) == 0)
    def _():
        left_ref[...] = jnp.zeros_like(left_ref)

    for number, value in enumerate(values):
        lanes = slice(number * width, (number + 1) * width)
        grad_ref[:, lanes] = value
        merged = value + DECAY_ERROR * error_ref[:, lanes]
        merged_ref[:, lanes] = merged
        left_ref[...] += dot(start_ref[:, lanes], merged, 1, 1, precision=HIGHEST)


def merge(member, shares, error, start, width):
    rows, total = error.shape
    rank = start.shape[0]
    wide = pl.BlockSpec((rows, GROUP * width), lambda i: (0, i))
    kind = jax.ShapeDtypeStruct((rows, total), F32)
    return pl.pallas_call(
        merge_kernel,
        grid=(total // (GROUP * width),),
        in_specs=[pl.BlockSpec(memory_space=pltpu.SMEM)]
        + [pl.BlockSpec((rows, width), lambda i: (0, i))] * GROUP
        + [wide, pl.BlockSpec((rank, GROUP * width), lambda i: (0, i))],
        out_specs=[wide, wide, pl.BlockSpec((rank, rows), lambda i: (0, 0))],
        out_shape=[kind, kind, jax.ShapeDtypeStruct((rank, rows), F32)],
        compiler_params=pltpu.CompilerParams(vmem_limit_bytes=40 * 2**20),
        cost_estimate=pl.CostEstimate(flops=0, bytes_accessed=rows * total, transcendentals=0),
        name="merge",
    )(member.reshape(1), *shares, error, start)


def right_kernel(own_ref, other_ref, merged_ref, ortho_ref, right_ref, left_ref):
    @pl.when(pl.program_id(0) == 0)
    def _():
        left = own_ref[...] + other_ref[...]
        number = lax.broadcasted_iota(jnp.int32, (left.shape[0], 1), 0)
        for step in range(left.shape[0]):
            row = left[step : step + 1]
            row = row * lax.rsqrt(jnp.sum(row * row, -1, keepdims=True))
            share = jnp.sum(left * row, -1, keepdims=True)
            left = jnp.where(
                number > step, left - share * row, jnp.where(number == step, row, left)
            )
        left_ref[...] = left
        ortho_ref[...] = left

    right_ref[...] = dot(left_ref[...], merged_ref[...], precision=HIGHEST).astype(BF16)


def right_factor(own, other, merged, tile=3072):
    rank, rows = own.shape
    total = merged.shape[1]
    small = pl.BlockSpec((rank, rows), lambda i: (0, 0))
    return pl.pallas_call(
        right_kernel,
        grid=(total // tile,),
        in_specs=[small, small, pl.BlockSpec((rows, tile), lambda i: (0, i))],
        out_specs=[small, pl.BlockSpec((rank, tile), lambda i: (0, i))],
        out_shape=[
            jax.ShapeDtypeStruct((rank, rows), F32),
            jax.ShapeDtypeStruct((rank, total), BF16),
        ],
        scratch_shapes=[pltpu.VMEM((rank, rows), F32)],
        compiler_params=pltpu.CompilerParams(vmem_limit_bytes=40 * 2**20),
        cost_estimate=pl.CostEstimate(flops=0, bytes_accessed=rows * total, transcendentals=0),
        name="right_factor",
    )(own, other, merged)


def update_kernel(copies, ortho_ref, own_ref, other_ref, merged_ref, momentum_ref, weight_ref, *outs):
    right_ref, error_ref, momentum_out_ref, weight_out_ref = outs
    right = (own_ref[...].astype(F32) + other_ref[...].astype(F32)) / copies
    approx = dot(ortho_ref[...], right, 0, 0, precision=HIGHEST)
    momentum = MOMENTUM * momentum_ref[...] + (1.0 - MOMENTUM) * approx
    right_ref[...] = right
    error_ref[...] = merged_ref[...] - approx
    momentum_out_ref[...] = momentum
    weight_out_ref[...] = weight_ref[...] - RATE_MATRIX * momentum


def update(copies, ortho, own, other, merged, momentum, weight, tile=3072):
    rank, rows = ortho.shape
    total = merged.shape[1]
    small = pl.BlockSpec((rank, rows), lambda i: (0, 0))
    low = pl.BlockSpec((rank, tile), lambda i: (0, i))
    wide = pl.BlockSpec((rows, tile), lambda i: (0, i))
    kind = jax.ShapeDtypeStruct((rows, total), F32)
    return pl.pallas_call(
        partial(update_kernel, copies),
        grid=(total // tile,),
        in_specs=[small, low, low, wide, wide, wide],
        out_specs=[low, wide, wide, wide],
        out_shape=[jax.ShapeDtypeStruct((rank, total), F32), kind, kind, kind],
        compiler_params=pltpu.CompilerParams(vmem_limit_bytes=40 * 2**20),
        cost_estimate=pl.CostEstimate(flops=0, bytes_accessed=rows * total, transcendentals=0),
        name="update",
    )(ortho, own, other, merged, momentum, weight)


def after(value, *earlier):
    return lax.optimization_barrier((value, *earlier))[0]


def swap(value, bits):
    return lax.ppermute(value, "member", [(j, j ^ bits) for j in range(GROUP)])


def swap_layers(value, bits, layers):
    return lax.ppermute(value, "layer", [(z, z ^ bits) for z in range(layers)])


def ring(value, layers):
    return lax.ppermute(value, "layer", [(z, (z + 1) % layers) for z in range(layers)])


def cross(value, copies):
    return lax.ppermute(value, "replica", [(r, (r + 1) % copies) for r in range(copies)])


def sum_layers(partials):
    return lax.psum_scatter(partials, "layer", scatter_dimension=0, tiled=True)


def arrange(items, member):
    low, high = (member & 1) == 1, (member & 2) == 2
    pairs = [jnp.where(low, items[t ^ 1], items[t]) for t in range(GROUP)]
    return [jnp.where(high, pairs[t ^ 2], pairs[t]) for t in range(GROUP)]


class Line:
    def __init__(self, token):
        self.token = token

    def __call__(self, value):
        value, self.token = lax.optimization_barrier((value, self.token))
        return value

    def run(self, step, first, *others):
        return self(step(self(first), *others))


class Gather:
    def __init__(self, line, halves, layer, copy, layers, copies):
        self.line, self.layer, self.copy = line, layer, copy
        self.layers, self.copies = layers, copies
        self.halves = halves
        self.got = jnp.where(copy == 0, halves[0], halves[1])
        self.way, self.over_way, self.pieces, self.over = None, [], [], []

    def hop(self):
        self.way = ring(self.line(self.got), self.layers)

    def land(self):
        self.got = self.line(self.way)
        self.pieces.append(self.got)
        self.over_way.append(cross(self.got, self.copies))

    def land_over(self):
        self.over.append(self.line(self.over_way[len(self.over)]))

    def finish(self):
        while len(self.over) < self.layers - 1:
            if len(self.pieces) < self.layers - 1 and len(self.pieces) == len(self.over):
                self.hop()
                self.land()
            self.land_over()
        pieces = list(self.halves)
        for own, other in zip(self.pieces, self.over):
            pieces += [own, other]
        whole = assemble(self.layer, self.copy, self.layers, pieces)
        return whole.reshape(-1, whole.shape[-1])


def local(
    layers,
    copies,
    tokens,
    cotangent,
    needle_mask,
    segment_ids,
    attn_weight,
    ffn_weight,
    vector_params,
    attn_error,
    ffn_error,
    attn_momentum,
    ffn_momentum,
    attn_start,
    ffn_start,
    vector_momentum,
):
    length = tokens.shape[0]
    copy = lax.axis_index("replica")
    layer, member = lax.axis_index("layer"), lax.axis_index("member")

    gain_in = vector_params[0:D]
    gain_mid = vector_params[D : 2 * D]
    gain_head = vector_params[2 * D : 2 * D + 2 * HD]
    lambda_q_one = vector_params[2 * D + 2 * HD : 2 * D + 3 * HD]
    lambda_k_one = vector_params[2 * D + 3 * HD : 2 * D + 4 * HD]
    lambda_q_two = vector_params[2 * D + 4 * HD : 2 * D + 5 * HD]
    lambda_k_two = vector_params[2 * D + 5 * HD : 2 * D + 6 * HD]
    exp_one = jnp.exp(jnp.sum(lambda_q_one * lambda_k_one))
    exp_two = jnp.exp(jnp.sum(lambda_q_two * lambda_k_two))
    lam = (exp_one - exp_two + LAMBDA_INIT).reshape(1)

    line = Line(jnp.zeros((8, 128), F32))

    def gather(halves):
        return Gather(line, halves, layer, copy, layers, copies)

    def halves_of(block):
        rows = block.shape[0] // 2
        return block[:rows], block[rows:]

    def columns(values, width):
        return [values[:, t * width : (t + 1) * width] for t in range(GROUP)]

    def layer_block(parts):
        return jnp.concatenate(arrange(parts, member), 0)

    needles = jnp.broadcast_to(jnp.sum(needle_mask).astype(F32), (8, 128))
    needles_other = cross(needles, copies)
    qkv_parts = quarters(member, attn_weight, 3, ATTN_Q)
    qkv_got = [swap(qkv_parts[k], k) for k in (2, 3, 1)]
    needles = needles + line(needles_other)
    bits = 1
    while bits < layers:
        needles = needles + line(swap_layers(needles, bits, layers))
        bits *= 2
    qkv_got = [line(got) for got in qkv_got]
    qkv_block = layer_block([qkv_parts[0], qkv_got[2], qkv_got[0], qkv_got[1]])
    qkv_gather = gather(halves_of(qkv_block))
    qkv_gather.hop()
    ffn_parts = quarters(member, line(ffn_weight), 3, FF_Q)
    ffn_got = [swap(line(ffn_parts[k]), k) for k in (2, 3, 1)]
    out_own = line(attn_weight)[:, 3 * D :].astype(BF16)
    out_across = swap(out_own, 2)
    qkv_gather.land()
    qkv_gather.hop()
    residual_in = line(tokens).astype(F32)
    scale_in = rms_scale(residual_in, 1e-06)
    normed_in = residual_in * scale_in
    normed_low = line((normed_in * gain_in).astype(BF16))
    qkv_gather.land()
    qkv_gather.hop()
    lines = length // 128
    marks = segment_ids.reshape(lines, 128) + GROUP * needle_mask.reshape(lines, 128)
    small = jnp.concatenate([marks.astype(F32), needles[: 8 - lines % 8]])
    rows = small.shape[0]
    small_beside = line(swap(line(small), 1))
    small_pair = jnp.concatenate([small, small_beside])
    out_across = swap(line(out_own), 2)
    qkv_gather.land()
    ffn_got = [line(got) for got in ffn_got]
    normed_across = swap(line(normed_low), 2)
    small_across = swap(small_pair, 2)
    normed_beside = swap(normed_low, 1)
    ffn_half = layer_block([ffn_parts[0], ffn_got[2], ffn_got[0], ffn_got[1]])
    ffn_half = ffn_half.reshape(2, -1, ffn_half.shape[1])
    ffn_half = line(lax.dynamic_index_in_dim(ffn_half, copy, 0, False))
    out_across = line(out_across)
    side = (member // 2) == 0
    out_gather = gather(
        (jnp.where(side, out_own, out_across), jnp.where(side, out_across, out_own))
    )
    out_gather.hop()
    qkv_gather.land_over()
    qkv_gather.land_over()
    out_gather.land()
    out_gather.hop()
    qkv_gather.land_over()
    ffn_weight_low = lax.all_gather(line(ffn_half), ("layer", "replica"), axis=0, tiled=True)
    out_gather.land()
    out_gather.hop()
    out_gather.land_over()
    out_gather.land()
    out_gather.land_over()
    normed_across = line(normed_across)
    small_across = line(small_across)
    normed_opposite = swap(normed_across, 1)
    cotangent_across = swap(line(cotangent), 2)
    qkv_weight = qkv_gather.finish()
    normed_beside = line(normed_beside)

    smalls = [(small, 0), (small_beside, 0), (small_across, 0), (small_across, 1)]

    def heads_of(qkv, k):
        return attend(lam, qkv, *smalls[k], rows, gain_head[None])

    qkv = [None] * GROUP
    heads = [None] * GROUP
    qkv[0] = line.run(project, normed_low, qkv_weight)
    qkv[1] = line.run(project, normed_beside, qkv_weight)
    heads[0] = line.run(heads_of, qkv[0], 0)
    heads[1] = line.run(heads_of, qkv[1], 1)
    heads_beside = swap(heads[1], 1)
    cotangent_across = line(cotangent_across)
    out_mine = line(out_gather.finish())
    out_rest = swap(out_mine, 1)
    qkv[2] = line.run(project, normed_across, qkv_weight)
    heads[2] = line.run(heads_of, qkv[2], 2)
    heads_across = swap(heads[2], 2)
    normed_opposite = line(normed_opposite)
    normed_all = [normed_low, normed_beside, normed_across, normed_opposite]
    qkv[3] = line.run(project, normed_opposite, qkv_weight)
    heads[3] = line.run(heads_of, qkv[3], 3)
    heads_opposite = swap(heads[3], 3)
    cotangent_near = swap(line(cotangent), 1)
    cotangent_far = swap(cotangent_across, 1)
    heads_beside, heads_across = line(heads_beside), line(heads_across)
    out_rest = line(out_rest)
    out_weight = line.run(
        lambda x: interleave(member % 2, x, out_rest, D // (layers * GROUP)), out_mine
    )
    heads_opposite = line(heads_opposite)
    heads_low = jnp.concatenate(
        arrange([heads[0], heads_beside, heads_across, heads_opposite], member), 1
    )
    residual_mid = line.run(lambda x: residual_in + dot(x, out_weight), heads_low)
    scale_mid = rms_scale(residual_mid, 1e-06)
    normed_mid = residual_mid * scale_mid
    mid_low = line((normed_mid * gain_mid).astype(BF16))
    mid_across = swap(mid_low, 2)
    mid_beside = swap(mid_low, 1)
    cotangents = [cotangent, line(cotangent_near), cotangent_across, line(cotangent_far)]
    *grad_out_all, grad_out = line.run(
        lambda x: loss_gradients(
            length * layers * GROUP * copies, lines, [x, *cotangents[1:]], smalls
        ),
        cotangent,
    )
    mid_across = line(mid_across)
    mid_opposite = swap(mid_across, 1)
    heads_across_all = swap(line(heads_low), 2)
    mid_beside, mid_opposite = line(mid_beside), line(mid_opposite)
    ffn_weight_low = line(ffn_weight_low)

    def product(lefts, rights, columns, place, into=None):
        return line.run(
            lambda x: weight_product([x, *lefts[1:]], rights, columns, place, into), lefts[0]
        )

    mid_all = [mid_low, mid_beside, mid_across, mid_opposite]
    hidden, gate_proj, up_proj = line.run(
        lambda x: raise_up([x, *mid_all[1:]], ffn_weight_low), mid_low
    )
    grad_gate, grad_up = line.run(
        lambda x: raise_back([x, *grad_out_all[1:]], ffn_weight_low, gate_proj, up_proj),
        grad_out_all[0],
    )
    heads_across_all = line(heads_across_all)
    down_total = sum_layers(product(grad_out_all, hidden, FF_Q, 0))

    def lower(k, got=None, kind=BF16):
        return line.run(
            lambda x: back_product([x, grad_up[k]], ffn_weight_low, got, kind), grad_gate[k]
        )

    def lower_hidden(k, got=None, kind=BF16):
        return line.run(
            lambda x: back_product([x], ffn_weight_low, got, kind, first=2), hidden[k]
        )

    opposite_got = swap(lower(3), 1)
    beside_got = swap(lower(1), 1)
    opposite_got = line(opposite_got)
    beside_got = line(beside_got)
    mid_sum = swap(lower(2, opposite_got), 2)
    up_partial = product(mid_all, grad_gate, 2 * FF_Q, 0)
    grad_mid_own = lower(0, beside_got, F32)
    up_partial = product(mid_all, grad_up, 2 * FF_Q, 1, up_partial)
    ffn_opposite_got = swap(lower_hidden(3), 1)
    ffn_beside_got = swap(lower_hidden(1), 1)
    mid_sum = line(mid_sum)
    down_total = line(down_total)
    up_total = sum_layers(line(up_partial))
    heads_beside_all = swap(line(heads_low), 1)
    heads_opposite_all = swap(heads_across_all, 1)

    grad_mid_low = grad_mid_own + mid_sum.astype(F32)
    grad_mid = grad_out + norm_back(grad_mid_low * gain_mid, normed_mid, scale_mid)
    grad_attn_low = grad_mid.astype(BF16)
    grad_heads = line.run(lambda x: dot(x, out_weight, 1, 1).astype(BF16), grad_attn_low)
    grad_heads = arrange(columns(grad_heads, ATTN_Q), member)
    grad_heads_got = [swap(grad_heads[k], k) for k in (2, 3, 1)]
    grad_attn = arrange(columns(grad_attn_low, ATTN_Q), member)

    def back(grad, k):
        return attend_back(lam, qkv[k], *smalls[k], rows, gain_head[None], grad)

    grad_qkv, stats = [None] * GROUP, [None] * GROUP
    grad_qkv[0], stats[0] = line.run(back, grad_heads[0], 0)
    heads_beside_all, heads_opposite_all = line(heads_beside_all), line(heads_opposite_all)
    heads_all = [heads_low, heads_beside_all, heads_across_all, heads_opposite_all]
    ffn_opposite_got, ffn_beside_got = line(ffn_opposite_got), line(ffn_beside_got)
    grad_qkv[1], stats[1] = line.run(back, line(grad_heads_got[2]), 1)
    grad_heads_across, grad_heads_opposite = line(grad_heads_got[0]), line(grad_heads_got[1])
    grad_attn_got = [swap(line(grad_attn[k]), k) for k in (2, 3, 1)]
    grad_qkv[2], stats[2] = line.run(back, grad_heads_across, 2)
    grad_attn_got = [line(got) for got in grad_attn_got]
    grad_attn_all = [grad_attn[0], grad_attn_got[2], grad_attn_got[0], grad_attn_got[1]]
    ffn_sum = swap(lower_hidden(2, ffn_opposite_got), 2)
    grad_qkv[3], stats[3] = line.run(back, grad_heads_opposite, 3)
    attn_partial = product(heads_all, grad_attn_all, 4 * ATTN_Q, 3)
    ffn_own = lower_hidden(0, ffn_beside_got, F32)
    attn_partial = product(normed_all, grad_qkv, 4 * ATTN_Q, 0, attn_partial)
    ffn_sum = line(ffn_sum)
    attn_total = sum_layers(line(attn_partial))
    mixed = line((residual_mid + ffn_own + ffn_sum.astype(F32)).astype(BF16))
    stats = sum(stats)
    grad_gain_head, grad_lambda = stats[0], stats[1, 0]

    def lower_in(k, got=None, kind=BF16):
        return line.run(
            lambda x: back_product([x], qkv_weight, got, kind, share=1), grad_qkv[k]
        )

    def rows_of(total):
        size = total.shape[0] // GROUP
        return arrange([total[t * size : (t + 1) * size] for t in range(GROUP)], member)

    def share(parts):
        return [parts[0]] + [swap(line(parts[k]), k) for k in range(1, GROUP)]

    def landed(parts):
        return [parts[0]] + [line(part) for part in parts[1:]]

    in_opposite_got = swap(lower_in(3), 1)
    in_beside_got = swap(lower_in(1), 1)
    ffn_total = jnp.concatenate([line(up_total), down_total], 1)
    ffn_shares = share(rows_of(ffn_total))
    in_opposite_got = line(in_opposite_got)
    in_sent = lower_in(2, in_opposite_got)
    in_beside_got = line(in_beside_got)
    in_own = lower_in(0, in_beside_got, F32)
    grad_gain_mid = line(jnp.sum(line(grad_mid_low) * normed_mid, 0))
    ffn_rows = landed(ffn_shares)
    in_sum = swap(line(in_sent), 2)
    ffn_grad, merged_ffn, left_ffn = line.run(
        lambda x: merge(member, [x, *ffn_rows[1:]], ffn_error[0], ffn_start[0], FF_Q), ffn_rows[0]
    )
    left_other = line(cross(left_ffn, copies))
    ortho_ffn, right_ffn = line.run(right_factor, left_ffn, left_other, merged_ffn)
    right_other = line(cross(right_ffn, copies))
    right_ffn, ffn_error_new, ffn_momentum_new, ffn_weight_new = line.run(
        partial(update, copies), ortho_ffn, right_ffn, right_other, merged_ffn, ffn_momentum, ffn_weight
    )
    in_sum = line(in_sum)
    grad_in_low = in_own + in_sum.astype(F32)
    grad_gain_in = line(jnp.sum(grad_in_low * normed_in, 0))
    vector_grad = jnp.concatenate(
        [
            grad_gain_in,
            grad_gain_mid,
            grad_gain_head,
            grad_lambda * exp_one * lambda_k_one,
            grad_lambda * exp_one * lambda_q_one,
            -grad_lambda * exp_two * lambda_k_two,
            -grad_lambda * exp_two * lambda_q_two,
        ]
    ).reshape(-1, 128)
    attn_shares = share(rows_of(line(attn_total)))
    vector_grad = vector_grad + line(cross(vector_grad, copies))
    vector_grad = vector_grad + line(swap(vector_grad, 1))
    bits = 1
    while bits < layers:
        vector_grad = vector_grad + line(swap_layers(vector_grad, bits, layers))
        bits *= 2
    attn_rows = landed(attn_shares)
    vector_other = swap(line(vector_grad), 2)
    attn_grad, merged_attn, left_attn = line.run(
        lambda x: merge(member, [x, *attn_rows[1:]], attn_error[0], attn_start[0], ATTN_Q),
        attn_rows[0],
    )
    left_other = line(cross(left_attn, copies))
    vector_grad = (vector_grad + line(vector_other)).reshape(-1)
    ortho_attn, right_attn = line.run(right_factor, left_attn, left_other, merged_attn)
    right_other = cross(right_attn, copies)
    grad_tokens = line(grad_mid + norm_back(grad_in_low * gain_in, normed_in, scale_in))
    right_other = line(right_other)
    right_attn, attn_error_new, attn_momentum_new, attn_weight_new = line.run(
        partial(update, copies),
        ortho_attn,
        right_attn,
        right_other,
        merged_attn,
        attn_momentum,
        attn_weight,
    )
    vector_grad = vector_grad + line.token[0, 0]
    vector_momentum_new = MOMENTUM * vector_momentum + (1.0 - MOMENTUM) * vector_grad
    vector_new = vector_params - RATE_VECTOR * vector_momentum_new
    return (
        mixed,
        grad_tokens,
        attn_grad[None],
        ffn_grad[None],
        ortho_attn,
        ortho_ffn,
        right_attn[None],
        right_ffn[None],
        attn_error_new[None],
        ffn_error_new[None],
        attn_momentum_new,
        ffn_momentum_new,
        attn_weight_new,
        ffn_weight_new,
        vector_momentum_new,
        vector_new,
    )


def solution(mesh):
    copies, shards = mesh.shape["replica"], mesh.shape["fsdp"]
    layers = shards // GROUP
    mesh = jax.sharding.Mesh(
        mesh.devices.reshape(copies, layers, GROUP), ("replica", "layer", "member")
    )
    fsdp = ("layer", "member")
    everywhere = ("replica", *fsdp)
    in_specs = (
        P(everywhere, None),
        P(everywhere, None),
        P(everywhere),
        P(everywhere, None),
        P(fsdp, None),
        P(fsdp, None),
        P(),
        P("replica", fsdp, None),
        P("replica", fsdp, None),
        P(fsdp, None),
        P(fsdp, None),
        P(fsdp, None, None),
        P(fsdp, None, None),
        P(),
    )
    out_specs = (
        P(everywhere, None),
        P(everywhere, None),
        P("replica", fsdp, None),
        P("replica", fsdp, None),
        P(None, fsdp),
        P(None, fsdp),
        P(fsdp, None, None),
        P(fsdp, None, None),
        P("replica", fsdp, None),
        P("replica", fsdp, None),
        P(fsdp, None),
        P(fsdp, None),
        P(fsdp, None),
        P(fsdp, None),
        P(),
        P(),
    )
    step = partial(local, layers, copies)
    return jax.shard_map(step, mesh=mesh, in_specs=in_specs, out_specs=out_specs, check_vma=False)
```

```python
from functools import partial

import jax
import jax.numpy as jnp
from jax import lax
from jax.experimental import pallas as pl
from jax.experimental.pallas import tpu as pltpu
from jax.sharding import PartitionSpec as P

D = 1536
HEADS = 12
HD = 64
FF = 4096

NEEDLE = 3.0
LAMBDA_INIT = 0.2
KEEP = 1.0 - LAMBDA_INIT
DECAY_ERROR = 0.5
MOMENTUM = 0.9
RATE_MATRIX = 0.005
RATE_VECTOR = 0.02
MASKED = -1e30
HIGHEST = lax.Precision.HIGHEST
BF16 = jnp.bfloat16
F32 = jnp.float32

GROUP = 4
BLOCK = 128
REACH = 256
WIDTH = 2 * HD
OWN_HEADS = HEADS // GROUP
ATTN_Q = D // GROUP
FF_Q = FF // GROUP


def rms_scale(values, epsilon):
    return lax.rsqrt(jnp.mean(values * values, -1, keepdims=True) + epsilon)


def norm_back(grad_normed, normed, scale):
    return scale * (grad_normed - normed * jnp.mean(grad_normed * normed, -1, keepdims=True))


def dot(left, right, left_dim=1, right_dim=0, **kinds):
    return lax.dot_general(
        left, right, (((left_dim,), (right_dim,)), ((), ())), preferred_element_type=F32, **kinds
    )


def score_parts(qkv_ref, head, block, low, high, lam, bias):
    rows, reach = pl.ds(block * BLOCK, BLOCK), pl.ds(low, high - low)
    first = lax.broadcasted_iota(jnp.int32, (1, WIDTH), 1) < HD
    query = qkv_ref[rows, head * WIDTH : (head + 1) * WIDTH] * BF16(HD**-0.5)
    key = qkv_ref[reach, ATTN_Q + head * WIDTH : ATTN_Q + (head + 1) * WIDTH]
    value = qkv_ref[reach, 2 * ATTN_Q + head * WIDTH : 2 * ATTN_Q + (head + 1) * WIDTH]
    zero = jnp.zeros((), BF16)
    queries = jnp.concatenate(
        [jnp.where(first, query, zero), jnp.where(first, zero, query)], 0
    )
    score = dot(queries, key, 1, 1) + jnp.concatenate([bias, bias], 0)
    expo = jnp.exp(score - jnp.max(score, -1, keepdims=True))
    probs = expo * (1.0 / jnp.sum(expo, -1, keepdims=True))
    mixture = (probs[:BLOCK] - lam * probs[BLOCK:]).astype(BF16)
    return queries, key, value, probs, mixture


def column_of(row):
    rows = lax.broadcasted_iota(jnp.int32, (BLOCK, BLOCK), 0)
    cols = lax.broadcasted_iota(jnp.int32, (BLOCK, BLOCK), 1)
    return jnp.sum(jnp.where(rows == cols, row, 0.0), -1, keepdims=True)


def documents_of(marks):
    return jnp.where(marks >= GROUP, marks - GROUP, marks)


def block_bias(marks_ref, block, low, high):
    rows = lax.broadcasted_iota(jnp.int32, (BLOCK, high - low), 0) + block * BLOCK
    cols = lax.broadcasted_iota(jnp.int32, (BLOCK, high - low), 1) + low
    keys = jnp.concatenate(
        [marks_ref[b : b + 1, :] for b in range(low // BLOCK, high // BLOCK)], 1
    )
    queries = column_of(marks_ref[block : block + 1, :])
    same = documents_of(queries) == documents_of(keys)
    return jnp.where((cols <= rows) & same, 0.0, MASKED)


def reach_of(block):
    return max(0, block - REACH // BLOCK) * BLOCK, (block + 1) * BLOCK


def attend_kernel(lam_ref, qkv_ref, marks_ref, gain_ref, heads_ref):
    lam = lam_ref[0]
    gain = gain_ref[...] * KEEP
    for block in range(qkv_ref.shape[0] // BLOCK):
        low, high = reach_of(block)
        bias = block_bias(marks_ref, block, low, high)
        for head in range(OWN_HEADS):
            _, _, value, _, mixture = score_parts(qkv_ref, head, block, low, high, lam, bias)
            out = dot(mixture, value)
            normed = out * rms_scale(out, 1e-05)
            heads_ref[pl.ds(block * BLOCK, BLOCK), head * WIDTH : (head + 1) * WIDTH] = (
                normed * gain
            ).astype(BF16)


def attend_back_kernel(
    lam_ref, qkv_ref, marks_ref, gain_ref, grad_ref, out_ref, stat_ref, dk_ref, dv_ref
):
    lam = lam_ref[0]
    gain = gain_ref[...] * KEEP
    blocks = qkv_ref.shape[0] // BLOCK
    first = lax.broadcasted_iota(jnp.int32, (1, WIDTH), 1) < HD
    upper = lax.broadcasted_iota(jnp.int32, (2 * BLOCK, 1), 0) < BLOCK
    share = jnp.where(upper, 1.0, -lam)
    gain_total = jnp.zeros((1, WIDTH), F32)
    lam_total = jnp.zeros((1, 1), F32)
    biases = [block_bias(marks_ref, b, *reach_of(b)) for b in range(blocks)]
    for head in range(OWN_HEADS):
        lanes = slice(head * WIDTH, (head + 1) * WIDTH)
        dk_ref[...] = jnp.zeros_like(dk_ref)
        dv_ref[...] = jnp.zeros_like(dv_ref)
        for block in range(blocks):
            low, high = reach_of(block)
            rows, reach = pl.ds(block * BLOCK, BLOCK), pl.ds(low, high - low)
            queries, key, value, probs, mixture = score_parts(
                qkv_ref, head, block, low, high, lam, biases[block]
            )
            out = dot(mixture, value)
            scale = rms_scale(out, 1e-05)
            normed = out * scale
            grad = grad_ref[rows, lanes].astype(F32)
            gain_total = gain_total + jnp.sum(grad * normed, 0, keepdims=True)
            grad_out = norm_back(grad * gain, normed, scale).astype(BF16)
            grad_mix = dot(grad_out, value, 1, 1)
            grad_mix = jnp.concatenate([grad_mix, grad_mix], 0)
            mean = jnp.sum(grad_mix * probs, -1, keepdims=True)
            lam_total = lam_total - jnp.sum(mean[BLOCK:], 0, keepdims=True)
            low_scores = (probs * (share * (grad_mix - mean))).astype(BF16)
            dv_ref[reach, :] += dot(mixture, grad_out, 0, 0)
            dk_ref[reach, :] += dot(low_scores, queries, 0, 0)
            grad_query = dot(low_scores, key)
            grad_query = jnp.where(first, grad_query[:BLOCK], grad_query[BLOCK:])
            out_ref[rows, lanes] = (grad_query * HD**-0.5).astype(BF16)
        out_ref[:, ATTN_Q + head * WIDTH : ATTN_Q + (head + 1) * WIDTH] = dk_ref[...].astype(BF16)
        out_ref[:, 2 * ATTN_Q + head * WIDTH : 2 * ATTN_Q + (head + 1) * WIDTH] = dv_ref[
            ...
        ].astype(BF16)
    stat_ref[0:1, :] = gain_total * KEEP
    stat_ref[1:2, :] = jnp.broadcast_to(lam_total, (1, WIDTH))
    stat_ref[2:8, :] = jnp.zeros((6, WIDTH), F32)


def attention_specs(length, lines, part):
    return [
        pl.BlockSpec(memory_space=pltpu.SMEM),
        pl.BlockSpec((length, 3 * ATTN_Q), lambda i: (0, 0)),
        pl.BlockSpec((lines, BLOCK), lambda i: (part, 0)),
        pl.BlockSpec((1, WIDTH), lambda i: (0, 0)),
    ]


def attend(lam, qkv, marks, part, lines, gain):
    length = qkv.shape[0]
    return pl.pallas_call(
        attend_kernel,
        grid=(1,),
        in_specs=attention_specs(length, lines, part),
        out_specs=pl.BlockSpec((length, ATTN_Q), lambda i: (0, 0)),
        out_shape=jax.ShapeDtypeStruct((length, ATTN_Q), BF16),
        compiler_params=pltpu.CompilerParams(vmem_limit_bytes=40 * 2**20),
        cost_estimate=pl.CostEstimate(
            flops=0, bytes_accessed=length * ATTN_Q, transcendentals=0
        ),
        name="attend",
    )(lam, qkv, marks, gain)


def attend_back(lam, qkv, marks, part, lines, gain, grad):
    length = qkv.shape[0]
    return pl.pallas_call(
        attend_back_kernel,
        grid=(1,),
        in_specs=attention_specs(length, lines, part)
        + [pl.BlockSpec((length, ATTN_Q), lambda i: (0, 0))],
        out_specs=[
            pl.BlockSpec((length, 3 * ATTN_Q), lambda i: (0, 0)),
            pl.BlockSpec((8, WIDTH), lambda i: (0, 0)),
        ],
        out_shape=[
            jax.ShapeDtypeStruct((length, 3 * ATTN_Q), BF16),
            jax.ShapeDtypeStruct((8, WIDTH), F32),
        ],
        scratch_shapes=[pltpu.VMEM((length, WIDTH), F32), pltpu.VMEM((length, WIDTH), F32)],
        compiler_params=pltpu.CompilerParams(vmem_limit_bytes=40 * 2**20),
        cost_estimate=pl.CostEstimate(
            flops=0, bytes_accessed=length * ATTN_Q, transcendentals=0
        ),
        name="attend_back",
    )(lam, qkv, marks, gain, grad)


def loss_kernel(everyone, lines, *refs):
    cotangents, smalls, outs = refs[:GROUP], refs[GROUP : 2 * GROUP], refs[2 * GROUP :]
    block = pl.program_id(0)
    needles = sum([small[lines : lines + 1, :] for small in smalls])
    scale = everyone / (everyone + NEEDLE * needles[:, 0:1])
    for k in range(GROUP):
        marks = column_of(smalls[k][pl.ds(block, 1), :])
        weights = 1.0 + NEEDLE * jnp.where(marks >= GROUP, 1.0, 0.0)
        grad = cotangents[k][...].astype(F32) * (weights * scale)
        outs[k][...] = grad.astype(BF16)
        if k == 0:
            outs[GROUP][...] = grad


def loss_gradients(everyone, lines, cotangents, smalls):
    length, width = cotangents[0].shape
    spec = pl.BlockSpec((BLOCK, width), lambda i: (i, 0))
    rows = smalls[0][0].shape[0]
    low = jax.ShapeDtypeStruct((length, width), BF16)
    return pl.pallas_call(
        partial(loss_kernel, everyone, lines),
        grid=(length // BLOCK,),
        in_specs=[spec] * GROUP
        + [pl.BlockSpec((rows, BLOCK), lambda i, p=part: (p, 0)) for _, part in smalls],
        out_specs=[spec] * (GROUP + 1),
        out_shape=[low] * GROUP + [jax.ShapeDtypeStruct((length, width), F32)],
        compiler_params=pltpu.CompilerParams(vmem_limit_bytes=40 * 2**20),
        cost_estimate=pl.CostEstimate(flops=0, bytes_accessed=length * width, transcendentals=0),
        name="loss_gradients",
    )(*cotangents, *[small for small, _ in smalls])


def quarter_kernel(member_ref, *refs):
    for source, target in zip(refs[:GROUP], refs[GROUP:]):
        target[...] = source[...].astype(BF16)


def quarters(member, weight, sections, width):
    rows = weight.shape[0]

    def columns(bits):
        return lambda i, member: (0, i * GROUP + (member[0] ^ bits))

    kind = jax.ShapeDtypeStruct((rows, sections * width), BF16)
    return pl.pallas_call(
        quarter_kernel,
        grid_spec=pltpu.PrefetchScalarGridSpec(
            num_scalar_prefetch=1,
            grid=(sections,),
            in_specs=[pl.BlockSpec((rows, width), columns(bits)) for bits in range(GROUP)],
            out_specs=[pl.BlockSpec((rows, width), lambda i, member: (0, i))] * GROUP,
        ),
        out_shape=[kind] * GROUP,
        compiler_params=pltpu.CompilerParams(vmem_limit_bytes=40 * 2**20),
        cost_estimate=pl.CostEstimate(flops=0, bytes_accessed=rows * width, transcendentals=0),
        name="quarters",
    )(member.reshape(1), *[weight] * GROUP)


def back_kernel(pairs, *refs):
    total = None
    for left, right in zip(refs[:pairs], refs[pairs : 2 * pairs]):
        part = dot(left[...], right[...], 1, 1)
        total = part if total is None else total + part
    if len(refs) > 2 * pairs + 1:
        total = total + refs[2 * pairs][...].astype(F32)
    refs[-1][...] = total.astype(refs[-1].dtype)


def back_product(lefts, right, got=None, kind=BF16, tile=512, first=0, share=32):
    pairs, (length, depth) = len(lefts), lefts[0].shape
    width = right.shape[0]
    specs = [pl.BlockSpec((length, depth), lambda i: (0, 0))] * pairs
    for number in range(pairs):
        specs.append(pl.BlockSpec((tile, depth), lambda i, s=first + number: (i, s)))
    out_spec = pl.BlockSpec((length, tile), lambda i: (0, i))
    operands = list(lefts) + [right] * pairs
    if got is not None:
        specs.append(out_spec)
        operands.append(got)
    return pl.pallas_call(
        partial(back_kernel, pairs),
        grid=(width // tile,),
        in_specs=specs,
        out_specs=out_spec,
        out_shape=jax.ShapeDtypeStruct((length, width), kind),
        compiler_params=pltpu.CompilerParams(vmem_limit_bytes=40 * 2**20),
        cost_estimate=pl.CostEstimate(
            flops=2 * pairs * length * depth * width // share,
            bytes_accessed=2 * pairs * (length + width) * depth // share,
            transcendentals=0,
        ),
        name="back_product",
    )(*operands)


def weight_kernel(*refs):
    out_ref = refs[-1]
    total = None
    for left, right in zip(refs[:GROUP], refs[GROUP : 2 * GROUP]):
        part = dot(left[...], right[...], 0, 0)
        total = part if total is None else total + part
    out_ref[...] = total.astype(BF16)


def weight_product(lefts, rights, columns, place, into=None, rows=512):
    length, depth = lefts[0].shape
    width = rights[0].shape[1]
    specs = [pl.BlockSpec((length, rows), lambda i: (0, i))] * GROUP
    specs += [pl.BlockSpec((length, width), lambda i: (0, 0))] * GROUP
    operands = [*lefts, *rights]
    if into is not None:
        specs.append(pl.BlockSpec(memory_space=pl.ANY))
        operands.append(into)
    return pl.pallas_call(
        weight_kernel,
        grid=(depth // rows,),
        in_specs=specs,
        out_specs=pl.BlockSpec((rows, width), lambda i: (i, place)),
        out_shape=jax.ShapeDtypeStruct((depth, columns), BF16),
        input_output_aliases={} if into is None else {2 * GROUP: 0},
        compiler_params=pltpu.CompilerParams(vmem_limit_bytes=60 * 2**20),
        cost_estimate=pl.CostEstimate(
            flops=GROUP * length * depth * width // 32,
            bytes_accessed=GROUP * length * (depth + width) // 32,
            transcendentals=0,
        ),
        name="weight_product",
    )(*operands)


def project_kernel(left_ref, right_ref, out_ref):
    out_ref[...] = dot(left_ref[...], right_ref[...]).astype(BF16)


def project(left, right, tile=384):
    (length, depth), width = left.shape, right.shape[1]
    return pl.pallas_call(
        project_kernel,
        grid=(width // tile,),
        in_specs=[
            pl.BlockSpec((length, depth), lambda i: (0, 0)),
            pl.BlockSpec((depth, tile), lambda i: (0, i)),
        ],
        out_specs=pl.BlockSpec((length, tile), lambda i: (0, i)),
        out_shape=jax.ShapeDtypeStruct((length, width), BF16),
        compiler_params=pltpu.CompilerParams(vmem_limit_bytes=40 * 2**20),
        cost_estimate=pl.CostEstimate(flops=0, bytes_accessed=length * depth, transcendentals=0),
        name="project",
    )(left, right)


def raise_kernel(*refs):
    mids, (gate_ref, up_ref), outs = refs[:GROUP], refs[GROUP : GROUP + 2], refs[GROUP + 2 :]
    for k, mid_ref in enumerate(mids):
        gate = dot(mid_ref[...], gate_ref[...])
        up = dot(mid_ref[...], up_ref[...])
        outs[k][...] = (gate * jax.nn.sigmoid(gate) * up).astype(BF16)
        outs[GROUP + k][...] = gate
        outs[2 * GROUP + k][...] = up


def raise_up(mids, weight, tile=256):
    length, depth = mids[0].shape
    count = FF_Q // tile
    out_spec = pl.BlockSpec((length, tile), lambda i: (0, i))
    low = jax.ShapeDtypeStruct((length, FF_Q), BF16)
    high = jax.ShapeDtypeStruct((length, FF_Q), F32)
    outs = pl.pallas_call(
        raise_kernel,
        grid=(count,),
        in_specs=[pl.BlockSpec((length, depth), lambda i: (0, 0))] * GROUP
        + [
            pl.BlockSpec((depth, tile), lambda i: (0, i)),
            pl.BlockSpec((depth, tile), lambda i: (0, i + count)),
        ],
        out_specs=[out_spec] * (3 * GROUP),
        out_shape=[low] * GROUP + [high] * (2 * GROUP),
        compiler_params=pltpu.CompilerParams(vmem_limit_bytes=60 * 2**20),
        cost_estimate=pl.CostEstimate(flops=0, bytes_accessed=length * depth, transcendentals=0),
        name="raise_up",
    )(*mids, weight, weight)
    return outs[:GROUP], outs[GROUP : 2 * GROUP], outs[2 * GROUP :]


def raise_back_kernel(*refs):
    grads, down_ref, gates = refs[:GROUP], refs[GROUP], refs[GROUP + 1 : 2 * GROUP + 1]
    ups, outs = refs[2 * GROUP + 1 : 3 * GROUP + 1], refs[3 * GROUP + 1 :]
    for k in range(GROUP):
        grad_hidden = dot(grads[k][...], down_ref[...])
        gate = gates[k][...]
        sigmoid = jax.nn.sigmoid(gate)
        slope = sigmoid * (1.0 + gate * (1.0 - sigmoid))
        outs[k][...] = (grad_hidden * ups[k][...] * slope).astype(BF16)
        outs[GROUP + k][...] = (grad_hidden * gate * sigmoid).astype(BF16)


def raise_back(grads, weight, gates, ups, tile=256):
    length, depth = grads[0].shape
    count = FF_Q // tile
    spec = pl.BlockSpec((length, tile), lambda i: (0, i))
    kind = jax.ShapeDtypeStruct((length, FF_Q), BF16)
    outs = pl.pallas_call(
        raise_back_kernel,
        grid=(count,),
        in_specs=[pl.BlockSpec((length, depth), lambda i: (0, 0))] * GROUP
        + [pl.BlockSpec((depth, tile), lambda i: (0, i + 2 * count))]
        + [spec] * (2 * GROUP),
        out_specs=[spec] * (2 * GROUP),
        out_shape=[kind] * (2 * GROUP),
        compiler_params=pltpu.CompilerParams(vmem_limit_bytes=60 * 2**20),
        cost_estimate=pl.CostEstimate(flops=0, bytes_accessed=length * depth, transcendentals=0),
        name="raise_back",
    )(*grads, weight, *gates, *ups)
    return outs[:GROUP], outs[GROUP:]


def assemble_kernel(place_ref, *refs):
    out_ref = refs[-1]
    number = pl.program_id(0)
    for step, ref in enumerate(refs[:-1]):

        @pl.when(number == step)
        def _():
            out_ref[0, 0] = ref[...]


def assemble(layer, copy, layers, pieces):
    rows, cols = pieces[0].shape

    def target(i, place):
        step, part = i // 2, i % 2
        source = place[0] - step
        source = jnp.where(source < 0, source + layers, source)
        part = jnp.where(step == 0, part, jnp.where(part == 0, place[1], 1 - place[1]))
        return source, part, 0, 0

    return pl.pallas_call(
        assemble_kernel,
        grid_spec=pltpu.PrefetchScalarGridSpec(
            num_scalar_prefetch=1,
            grid=(2 * layers,),
            in_specs=[pl.BlockSpec((rows, cols), lambda i, place: (0, 0))] * (2 * layers),
            out_specs=pl.BlockSpec((1, 1, rows, cols), target),
        ),
        out_shape=jax.ShapeDtypeStruct((layers, 2, rows, cols), pieces[0].dtype),
        compiler_params=pltpu.CompilerParams(vmem_limit_bytes=40 * 2**20),
        cost_estimate=pl.CostEstimate(flops=0, bytes_accessed=rows * cols, transcendentals=0),
        name="assemble",
    )(jnp.stack([layer, copy]), *pieces)


def interleave_kernel(core_ref, own_ref, other_ref, out_ref):
    rows = own_ref.shape[0]
    first = core_ref[0] == 0
    own, other = own_ref[...], other_ref[...]
    out_ref[0:rows] = jnp.where(first, own, other)
    out_ref[rows : 2 * rows] = jnp.where(first, other, own)


def interleave(core, own, other, rows):
    total, cols = own.shape
    spec = pl.BlockSpec((rows, cols), lambda i: (i, 0))
    return pl.pallas_call(
        interleave_kernel,
        grid=(total // rows,),
        in_specs=[pl.BlockSpec(memory_space=pltpu.SMEM), spec, spec],
        out_specs=pl.BlockSpec((2 * rows, cols), lambda i: (i, 0)),
        out_shape=jax.ShapeDtypeStruct((2 * total, cols), own.dtype),
        cost_estimate=pl.CostEstimate(
            flops=0, bytes_accessed=8 * total * cols, transcendentals=0
        ),
        name="interleave",
    )(core.reshape(1), own, other)


def merge_kernel(member_ref, *refs):
    shares, (error_ref, start_ref), outs = refs[:GROUP], refs[GROUP : GROUP + 2], refs[GROUP + 2 :]
    grad_ref, merged_ref, left_ref = outs
    width = shares[0].shape[1]
    values = arrange([share[...].astype(F32) for share in shares], member_ref[0])

    @pl.when(pl.program_id(0) == 0)
    def _():
        left_ref[...] = jnp.zeros_like(left_ref)

    for number, value in enumerate(values):
        lanes = slice(number * width, (number + 1) * width)
        grad_ref[:, lanes] = value
        merged = value + DECAY_ERROR * error_ref[:, lanes]
        merged_ref[:, lanes] = merged
        left_ref[...] += dot(start_ref[:, lanes], merged, 1, 1, precision=HIGHEST)


def merge(member, shares, error, start, width):
    rows, total = error.shape
    rank = start.shape[0]
    wide = pl.BlockSpec((rows, GROUP * width), lambda i: (0, i))
    kind = jax.ShapeDtypeStruct((rows, total), F32)
    return pl.pallas_call(
        merge_kernel,
        grid=(total // (GROUP * width),),
        in_specs=[pl.BlockSpec(memory_space=pltpu.SMEM)]
        + [pl.BlockSpec((rows, width), lambda i: (0, i))] * GROUP
        + [wide, pl.BlockSpec((rank, GROUP * width), lambda i: (0, i))],
        out_specs=[wide, wide, pl.BlockSpec((rank, rows), lambda i: (0, 0))],
        out_shape=[kind, kind, jax.ShapeDtypeStruct((rank, rows), F32)],
        compiler_params=pltpu.CompilerParams(vmem_limit_bytes=40 * 2**20),
        cost_estimate=pl.CostEstimate(flops=0, bytes_accessed=rows * total, transcendentals=0),
        name="merge",
    )(member.reshape(1), *shares, error, start)


def right_kernel(own_ref, other_ref, merged_ref, ortho_ref, right_ref, left_ref):
    @pl.when(pl.program_id(0) == 0)
    def _():
        left = own_ref[...] + other_ref[...]
        number = lax.broadcasted_iota(jnp.int32, (left.shape[0], 1), 0)
        for step in range(left.shape[0]):
            row = left[step : step + 1]
            row = row * lax.rsqrt(jnp.sum(row * row, -1, keepdims=True))
            share = jnp.sum(left * row, -1, keepdims=True)
            left = jnp.where(
                number > step, left - share * row, jnp.where(number == step, row, left)
            )
        left_ref[...] = left
        ortho_ref[...] = left

    right_ref[...] = dot(left_ref[...], merged_ref[...], precision=HIGHEST).astype(BF16)


def right_factor(own, other, merged, tile=3072):
    rank, rows = own.shape
    total = merged.shape[1]
    small = pl.BlockSpec((rank, rows), lambda i: (0, 0))
    return pl.pallas_call(
        right_kernel,
        grid=(total // tile,),
        in_specs=[small, small, pl.BlockSpec((rows, tile), lambda i: (0, i))],
        out_specs=[small, pl.BlockSpec((rank, tile), lambda i: (0, i))],
        out_shape=[
            jax.ShapeDtypeStruct((rank, rows), F32),
            jax.ShapeDtypeStruct((rank, total), BF16),
        ],
        scratch_shapes=[pltpu.VMEM((rank, rows), F32)],
        compiler_params=pltpu.CompilerParams(vmem_limit_bytes=40 * 2**20),
        cost_estimate=pl.CostEstimate(flops=0, bytes_accessed=rows * total, transcendentals=0),
        name="right_factor",
    )(own, other, merged)


def update_kernel(copies, ortho_ref, own_ref, other_ref, merged_ref, momentum_ref, weight_ref, *outs):
    right_ref, error_ref, momentum_out_ref, weight_out_ref = outs
    right = (own_ref[...].astype(F32) + other_ref[...].astype(F32)) / copies
    approx = dot(ortho_ref[...], right, 0, 0, precision=HIGHEST)
    momentum = MOMENTUM * momentum_ref[...] + (1.0 - MOMENTUM) * approx
    right_ref[...] = right
    error_ref[...] = merged_ref[...] - approx
    momentum_out_ref[...] = momentum
    weight_out_ref[...] = weight_ref[...] - RATE_MATRIX * momentum


def update(copies, ortho, own, other, merged, momentum, weight, tile=3072):
    rank, rows = ortho.shape
    total = merged.shape[1]
    small = pl.BlockSpec((rank, rows), lambda i: (0, 0))
    low = pl.BlockSpec((rank, tile), lambda i: (0, i))
    wide = pl.BlockSpec((rows, tile), lambda i: (0, i))
    kind = jax.ShapeDtypeStruct((rows, total), F32)
    return pl.pallas_call(
        partial(update_kernel, copies),
        grid=(total // tile,),
        in_specs=[small, low, low, wide, wide, wide],
        out_specs=[low, wide, wide, wide],
        out_shape=[jax.ShapeDtypeStruct((rank, total), F32), kind, kind, kind],
        compiler_params=pltpu.CompilerParams(vmem_limit_bytes=40 * 2**20),
        cost_estimate=pl.CostEstimate(flops=0, bytes_accessed=rows * total, transcendentals=0),
        name="update",
    )(ortho, own, other, merged, momentum, weight)


def after(value, *earlier):
    return lax.optimization_barrier((value, *earlier))[0]


def swap(value, bits):
    return lax.ppermute(value, "member", [(j, j ^ bits) for j in range(GROUP)])


def swap_layers(value, bits, layers):
    return lax.ppermute(value, "layer", [(z, z ^ bits) for z in range(layers)])


def ring(value, layers):
    return lax.ppermute(value, "layer", [(z, (z + 1) % layers) for z in range(layers)])


def cross(value, copies):
    return lax.ppermute(value, "replica", [(r, (r + 1) % copies) for r in range(copies)])


def sum_layers(partials):
    return lax.psum_scatter(partials, "layer", scatter_dimension=0, tiled=True)


def arrange(items, member):
    low, high = (member & 1) == 1, (member & 2) == 2
    pairs = [jnp.where(low, items[t ^ 1], items[t]) for t in range(GROUP)]
    return [jnp.where(high, pairs[t ^ 2], pairs[t]) for t in range(GROUP)]


class Line:
    def __init__(self, token):
        self.token = token

    def __call__(self, value):
        value, self.token = lax.optimization_barrier((value, self.token))
        return value

    def run(self, step, first, *others):
        return self(step(self(first), *others))


class Gather:
    def __init__(self, line, halves, layer, copy, layers, copies):
        self.line, self.layer, self.copy = line, layer, copy
        self.layers, self.copies = layers, copies
        self.halves = halves
        self.got = jnp.where(copy == 0, halves[0], halves[1])
        self.way, self.over_way, self.pieces, self.over = None, [], [], []

    def hop(self):
        self.way = ring(self.line(self.got), self.layers)

    def land(self):
        self.got = self.line(self.way)
        self.pieces.append(self.got)
        self.over_way.append(cross(self.got, self.copies))

    def land_over(self):
        self.over.append(self.line(self.over_way[len(self.over)]))

    def finish(self):
        while len(self.over) < self.layers - 1:
            if len(self.pieces) < self.layers - 1 and len(self.pieces) == len(self.over):
                self.hop()
                self.land()
            self.land_over()
        pieces = list(self.halves)
        for own, other in zip(self.pieces, self.over):
            pieces += [own, other]
        whole = assemble(self.layer, self.copy, self.layers, pieces)
        return whole.reshape(-1, whole.shape[-1])


def local(
    layers,
    copies,
    tokens,
    cotangent,
    needle_mask,
    segment_ids,
    attn_weight,
    ffn_weight,
    vector_params,
    attn_error,
    ffn_error,
    attn_momentum,
    ffn_momentum,
    attn_start,
    ffn_start,
    vector_momentum,
):
    length = tokens.shape[0]
    copy = lax.axis_index("replica")
    layer, member = lax.axis_index("layer"), lax.axis_index("member")

    gain_in = vector_params[0:D]
    gain_mid = vector_params[D : 2 * D]
    gain_head = vector_params[2 * D : 2 * D + 2 * HD]
    lambda_q_one = vector_params[2 * D + 2 * HD : 2 * D + 3 * HD]
    lambda_k_one = vector_params[2 * D + 3 * HD : 2 * D + 4 * HD]
    lambda_q_two = vector_params[2 * D + 4 * HD : 2 * D + 5 * HD]
    lambda_k_two = vector_params[2 * D + 5 * HD : 2 * D + 6 * HD]
    exp_one = jnp.exp(jnp.sum(lambda_q_one * lambda_k_one))
    exp_two = jnp.exp(jnp.sum(lambda_q_two * lambda_k_two))
    lam = (exp_one - exp_two + LAMBDA_INIT).reshape(1)

    line = Line(jnp.zeros((8, 128), F32))

    def gather(halves):
        return Gather(line, halves, layer, copy, layers, copies)

    def halves_of(block):
        rows = block.shape[0] // 2
        return block[:rows], block[rows:]

    def columns(values, width):
        return [values[:, t * width : (t + 1) * width] for t in range(GROUP)]

    def layer_block(parts):
        return jnp.concatenate(arrange(parts, member), 0)

    needles = jnp.broadcast_to(jnp.sum(needle_mask).astype(F32), (8, 128))
    needles_other = cross(needles, copies)
    qkv_parts = quarters(member, attn_weight, 3, ATTN_Q)
    qkv_got = [swap(qkv_parts[k], k) for k in (2, 3, 1)]
    needles = needles + line(needles_other)
    bits = 1
    while bits < layers:
        needles = needles + line(swap_layers(needles, bits, layers))
        bits *= 2
    qkv_got = [line(got) for got in qkv_got]
    qkv_block = layer_block([qkv_parts[0], qkv_got[2], qkv_got[0], qkv_got[1]])
    qkv_gather = gather(halves_of(qkv_block))
    qkv_gather.hop()
    ffn_parts = quarters(member, line(ffn_weight), 3, FF_Q)
    ffn_got = [swap(line(ffn_parts[k]), k) for k in (2, 3, 1)]
    out_own = line(attn_weight)[:, 3 * D :].astype(BF16)
    out_across = swap(out_own, 2)
    qkv_gather.land()
    qkv_gather.hop()
    residual_in = line(tokens).astype(F32)
    scale_in = rms_scale(residual_in, 1e-06)
    normed_in = residual_in * scale_in
    normed_low = line((normed_in * gain_in).astype(BF16))
    qkv_gather.land()
    qkv_gather.hop()
    lines = length // 128
    marks = segment_ids.reshape(lines, 128) + GROUP * needle_mask.reshape(lines, 128)
    small = jnp.concatenate([marks.astype(F32), needles[: 8 - lines % 8]])
    rows = small.shape[0]
    small_beside = line(swap(line(small), 1))
    small_pair = jnp.concatenate([small, small_beside])
    out_across = swap(line(out_own), 2)
    qkv_gather.land()
    ffn_got = [line(got) for got in ffn_got]
    normed_across = swap(line(normed_low), 2)
    small_across = swap(small_pair, 2)
    normed_beside = swap(normed_low, 1)
    ffn_half = layer_block([ffn_parts[0], ffn_got[2], ffn_got[0], ffn_got[1]])
    ffn_half = ffn_half.reshape(2, -1, ffn_half.shape[1])
    ffn_half = line(lax.dynamic_index_in_dim(ffn_half, copy, 0, False))
    out_across = line(out_across)
    side = (member // 2) == 0
    out_gather = gather(
        (jnp.where(side, out_own, out_across), jnp.where(side, out_across, out_own))
    )
    out_gather.hop()
    qkv_gather.land_over()
    qkv_gather.land_over()
    out_gather.land()
    out_gather.hop()
    qkv_gather.land_over()
    ffn_weight_low = lax.all_gather(line(ffn_half), ("layer", "replica"), axis=0, tiled=True)
    out_gather.land()
    out_gather.hop()
    out_gather.land_over()
    out_gather.land()
    out_gather.land_over()
    normed_across = line(normed_across)
    small_across = line(small_across)
    normed_opposite = swap(normed_across, 1)
    cotangent_across = swap(line(cotangent), 2)
    qkv_weight = qkv_gather.finish()
    normed_beside = line(normed_beside)

    smalls = [(small, 0), (small_beside, 0), (small_across, 0), (small_across, 1)]

    def heads_of(qkv, k):
        return attend(lam, qkv, *smalls[k], rows, gain_head[None])

    qkv = [None] * GROUP
    heads = [None] * GROUP
    qkv[0] = line.run(project, normed_low, qkv_weight)
    qkv[1] = line.run(project, normed_beside, qkv_weight)
    heads[0] = line.run(heads_of, qkv[0], 0)
    heads[1] = line.run(heads_of, qkv[1], 1)
    heads_beside = swap(heads[1], 1)
    qkv[2] = line.run(project, normed_across, qkv_weight)
    heads[2] = line.run(heads_of, qkv[2], 2)
    heads_across = swap(heads[2], 2)
    cotangent_across = line(cotangent_across)
    out_mine = line(out_gather.finish())
    out_rest = swap(out_mine, 1)
    normed_opposite = line(normed_opposite)
    normed_all = [normed_low, normed_beside, normed_across, normed_opposite]
    qkv[3] = line.run(project, normed_opposite, qkv_weight)
    heads[3] = line.run(heads_of, qkv[3], 3)
    heads_opposite = swap(heads[3], 3)
    cotangent_near = swap(line(cotangent), 1)
    cotangent_far = swap(cotangent_across, 1)
    heads_beside, heads_across = line(heads_beside), line(heads_across)
    out_rest = line(out_rest)
    out_weight = line.run(
        lambda x: interleave(member % 2, x, out_rest, D // (layers * GROUP)), out_mine
    )
    heads_opposite = line(heads_opposite)
    heads_low = jnp.concatenate(
        arrange([heads[0], heads_beside, heads_across, heads_opposite], member), 1
    )
    residual_mid = line.run(lambda x: residual_in + dot(x, out_weight), heads_low)
    scale_mid = rms_scale(residual_mid, 1e-06)
    normed_mid = residual_mid * scale_mid
    mid_low = line((normed_mid * gain_mid).astype(BF16))
    mid_across = swap(mid_low, 2)
    mid_beside = swap(mid_low, 1)
    cotangents = [cotangent, line(cotangent_near), cotangent_across, line(cotangent_far)]
    *grad_out_all, grad_out = line.run(
        lambda x: loss_gradients(
            length * layers * GROUP * copies, lines, [x, *cotangents[1:]], smalls
        ),
        cotangent,
    )
    mid_across = line(mid_across)
    mid_opposite = swap(mid_across, 1)
    heads_across_all = swap(line(heads_low), 2)
    mid_beside, mid_opposite = line(mid_beside), line(mid_opposite)
    ffn_weight_low = line(ffn_weight_low)

    def product(lefts, rights, columns, place, into=None):
        return line.run(
            lambda x: weight_product([x, *lefts[1:]], rights, columns, place, into), lefts[0]
        )

    mid_all = [mid_low, mid_beside, mid_across, mid_opposite]
    hidden, gate_proj, up_proj = line.run(
        lambda x: raise_up([x, *mid_all[1:]], ffn_weight_low), mid_low
    )
    grad_gate, grad_up = line.run(
        lambda x: raise_back([x, *grad_out_all[1:]], ffn_weight_low, gate_proj, up_proj),
        grad_out_all[0],
    )
    heads_across_all = line(heads_across_all)
    down_total = sum_layers(product(grad_out_all, hidden, FF_Q, 0))

    def lower(k, got=None, kind=BF16):
        return line.run(
            lambda x: back_product([x, grad_up[k]], ffn_weight_low, got, kind), grad_gate[k]
        )

    def lower_hidden(k, got=None, kind=BF16):
        return line.run(
            lambda x: back_product([x], ffn_weight_low, got, kind, first=2), hidden[k]
        )

    opposite_got = swap(lower(3), 1)
    beside_got = swap(lower(1), 1)
    opposite_got = line(opposite_got)
    mid_sum = swap(lower(2, opposite_got), 2)
    beside_got = line(beside_got)
    up_partial = product(mid_all, grad_gate, 2 * FF_Q, 0)
    grad_mid_own = lower(0, beside_got, F32)
    up_partial = product(mid_all, grad_up, 2 * FF_Q, 1, up_partial)
    ffn_opposite_got = swap(lower_hidden(3), 1)
    ffn_beside_got = swap(lower_hidden(1), 1)
    mid_sum = line(mid_sum)
    down_total = line(down_total)
    up_total = sum_layers(line(up_partial))
    heads_beside_all = swap(line(heads_low), 1)
    heads_opposite_all = swap(heads_across_all, 1)

    grad_mid_low = grad_mid_own + mid_sum.astype(F32)
    grad_mid = grad_out + norm_back(grad_mid_low * gain_mid, normed_mid, scale_mid)
    grad_attn_low = grad_mid.astype(BF16)
    grad_heads = line.run(lambda x: dot(x, out_weight, 1, 1).astype(BF16), grad_attn_low)
    grad_heads = arrange(columns(grad_heads, ATTN_Q), member)
    grad_heads_got = [swap(grad_heads[k], k) for k in (2, 3, 1)]
    grad_attn = arrange(columns(grad_attn_low, ATTN_Q), member)

    def back(grad, k):
        return attend_back(lam, qkv[k], *smalls[k], rows, gain_head[None], grad)

    grad_qkv, stats = [None] * GROUP, [None] * GROUP
    grad_qkv[0], stats[0] = line.run(back, grad_heads[0], 0)
    heads_beside_all, heads_opposite_all = line(heads_beside_all), line(heads_opposite_all)
    heads_all = [heads_low, heads_beside_all, heads_across_all, heads_opposite_all]
    ffn_opposite_got, ffn_beside_got = line(ffn_opposite_got), line(ffn_beside_got)
    grad_qkv[1], stats[1] = line.run(back, line(grad_heads_got[2]), 1)
    grad_heads_across, grad_heads_opposite = line(grad_heads_got[0]), line(grad_heads_got[1])
    grad_attn_got = [swap(line(grad_attn[k]), k) for k in (2, 3, 1)]
    grad_qkv[2], stats[2] = line.run(back, grad_heads_across, 2)
    grad_attn_got = [line(got) for got in grad_attn_got]
    grad_attn_all = [grad_attn[0], grad_attn_got[2], grad_attn_got[0], grad_attn_got[1]]
    ffn_sum = swap(lower_hidden(2, ffn_opposite_got), 2)
    grad_qkv[3], stats[3] = line.run(back, grad_heads_opposite, 3)
    attn_partial = product(heads_all, grad_attn_all, 4 * ATTN_Q, 3)
    ffn_own = lower_hidden(0, ffn_beside_got, F32)
    attn_partial = product(normed_all, grad_qkv, 4 * ATTN_Q, 0, attn_partial)
    ffn_sum = line(ffn_sum)
    attn_total = sum_layers(line(attn_partial))
    mixed = line((residual_mid + ffn_own + ffn_sum.astype(F32)).astype(BF16))
    stats = sum(stats)
    grad_gain_head, grad_lambda = stats[0], stats[1, 0]

    def lower_in(k, got=None, kind=BF16):
        return line.run(
            lambda x: back_product([x], qkv_weight, got, kind, share=1), grad_qkv[k]
        )

    def rows_of(total):
        size = total.shape[0] // GROUP
        return arrange([total[t * size : (t + 1) * size] for t in range(GROUP)], member)

    def share(parts):
        return [parts[0]] + [swap(line(parts[k]), k) for k in range(1, GROUP)]

    def landed(parts):
        return [parts[0]] + [line(part) for part in parts[1:]]

    in_opposite_got = swap(lower_in(3), 1)
    in_beside_got = swap(lower_in(1), 1)
    ffn_total = jnp.concatenate([line(up_total), down_total], 1)
    ffn_shares = share(rows_of(ffn_total))
    in_opposite_got = line(in_opposite_got)
    in_sent = lower_in(2, in_opposite_got)
    in_beside_got = line(in_beside_got)
    in_own = lower_in(0, in_beside_got, F32)
    grad_gain_mid = line(jnp.sum(line(grad_mid_low) * normed_mid, 0))
    ffn_rows = landed(ffn_shares)
    in_sum = swap(line(in_sent), 2)
    ffn_grad, merged_ffn, left_ffn = line.run(
        lambda x: merge(member, [x, *ffn_rows[1:]], ffn_error[0], ffn_start[0], FF_Q), ffn_rows[0]
    )
    left_other = line(cross(left_ffn, copies))
    ortho_ffn, right_ffn = line.run(right_factor, left_ffn, left_other, merged_ffn)
    right_other = line(cross(right_ffn, copies))
    right_ffn, ffn_error_new, ffn_momentum_new, ffn_weight_new = line.run(
        partial(update, copies), ortho_ffn, right_ffn, right_other, merged_ffn, ffn_momentum, ffn_weight
    )
    in_sum = line(in_sum)
    grad_in_low = in_own + in_sum.astype(F32)
    grad_gain_in = line(jnp.sum(grad_in_low * normed_in, 0))
    vector_grad = jnp.concatenate(
        [
            grad_gain_in,
            grad_gain_mid,
            grad_gain_head,
            grad_lambda * exp_one * lambda_k_one,
            grad_lambda * exp_one * lambda_q_one,
            -grad_lambda * exp_two * lambda_k_two,
            -grad_lambda * exp_two * lambda_q_two,
        ]
    ).reshape(-1, 128)
    attn_shares = share(rows_of(line(attn_total)))
    vector_grad = vector_grad + line(cross(vector_grad, copies))
    vector_grad = vector_grad + line(swap(vector_grad, 1))
    bits = 1
    while bits < layers:
        vector_grad = vector_grad + line(swap_layers(vector_grad, bits, layers))
        bits *= 2
    attn_rows = landed(attn_shares)
    vector_other = swap(line(vector_grad), 2)
    attn_grad, merged_attn, left_attn = line.run(
        lambda x: merge(member, [x, *attn_rows[1:]], attn_error[0], attn_start[0], ATTN_Q),
        attn_rows[0],
    )
    left_other = line(cross(left_attn, copies))
    vector_grad = (vector_grad + line(vector_other)).reshape(-1)
    ortho_attn, right_attn = line.run(right_factor, left_attn, left_other, merged_attn)
    right_other = cross(right_attn, copies)
    grad_tokens = line(grad_mid + norm_back(grad_in_low * gain_in, normed_in, scale_in))
    right_other = line(right_other)
    right_attn, attn_error_new, attn_momentum_new, attn_weight_new = line.run(
        partial(update, copies),
        ortho_attn,
        right_attn,
        right_other,
        merged_attn,
        attn_momentum,
        attn_weight,
    )
    vector_grad = vector_grad + line.token[0, 0]
    vector_momentum_new = MOMENTUM * vector_momentum + (1.0 - MOMENTUM) * vector_grad
    vector_new = vector_params - RATE_VECTOR * vector_momentum_new
    return (
        mixed,
        grad_tokens,
        attn_grad[None],
        ffn_grad[None],
        ortho_attn,
        ortho_ffn,
        right_attn[None],
        right_ffn[None],
        attn_error_new[None],
        ffn_error_new[None],
        attn_momentum_new,
        ffn_momentum_new,
        attn_weight_new,
        ffn_weight_new,
        vector_momentum_new,
        vector_new,
    )


def solution(mesh):
    copies, shards = mesh.shape["replica"], mesh.shape["fsdp"]
    layers = shards // GROUP
    mesh = jax.sharding.Mesh(
        mesh.devices.reshape(copies, layers, GROUP), ("replica", "layer", "member")
    )
    fsdp = ("layer", "member")
    everywhere = ("replica", *fsdp)
    in_specs = (
        P(everywhere, None),
        P(everywhere, None),
        P(everywhere),
        P(everywhere, None),
        P(fsdp, None),
        P(fsdp, None),
        P(),
        P("replica", fsdp, None),
        P("replica", fsdp, None),
        P(fsdp, None),
        P(fsdp, None),
        P(fsdp, None, None),
        P(fsdp, None, None),
        P(),
    )
    out_specs = (
        P(everywhere, None),
        P(everywhere, None),
        P("replica", fsdp, None),
        P("replica", fsdp, None),
        P(None, fsdp),
        P(None, fsdp),
        P(fsdp, None, None),
        P(fsdp, None, None),
        P("replica", fsdp, None),
        P("replica", fsdp, None),
        P(fsdp, None),
        P(fsdp, None),
        P(fsdp, None),
        P(fsdp, None),
        P(),
        P(),
    )
    step = partial(local, layers, copies)
    return jax.shard_map(step, mesh=mesh, in_specs=in_specs, out_specs=out_specs, check_vma=False)
```

```python
from functools import partial

import jax
import jax.numpy as jnp
from jax import lax
from jax.experimental import pallas as pl
from jax.experimental.pallas import tpu as pltpu
from jax.sharding import PartitionSpec as P

D = 1536
HEADS = 12
HD = 64
FF = 4096

NEEDLE = 3.0
LAMBDA_INIT = 0.2
KEEP = 1.0 - LAMBDA_INIT
DECAY_ERROR = 0.5
MOMENTUM = 0.9
RATE_MATRIX = 0.005
RATE_VECTOR = 0.02
MASKED = -1e30
HIGHEST = lax.Precision.HIGHEST
BF16 = jnp.bfloat16
F32 = jnp.float32

GROUP = 4
BLOCK = 128
REACH = 256
WIDTH = 2 * HD
OWN_HEADS = HEADS // GROUP
ATTN_Q = D // GROUP
FF_Q = FF // GROUP


def rms_scale(values, epsilon):
    return lax.rsqrt(jnp.mean(values * values, -1, keepdims=True) + epsilon)


def norm_back(grad_normed, normed, scale):
    return scale * (grad_normed - normed * jnp.mean(grad_normed * normed, -1, keepdims=True))


def dot(left, right, left_dim=1, right_dim=0, **kinds):
    return lax.dot_general(
        left, right, (((left_dim,), (right_dim,)), ((), ())), preferred_element_type=F32, **kinds
    )


def score_parts(qkv_ref, head, block, low, high, lam, bias):
    rows, reach = pl.ds(block * BLOCK, BLOCK), pl.ds(low, high - low)
    first = lax.broadcasted_iota(jnp.int32, (1, WIDTH), 1) < HD
    query = qkv_ref[rows, head * WIDTH : (head + 1) * WIDTH] * BF16(HD**-0.5)
    key = qkv_ref[reach, ATTN_Q + head * WIDTH : ATTN_Q + (head + 1) * WIDTH]
    value = qkv_ref[reach, 2 * ATTN_Q + head * WIDTH : 2 * ATTN_Q + (head + 1) * WIDTH]
    zero = jnp.zeros((), BF16)
    queries = jnp.concatenate(
        [jnp.where(first, query, zero), jnp.where(first, zero, query)], 0
    )
    score = dot(queries, key, 1, 1) + jnp.concatenate([bias, bias], 0)
    expo = jnp.exp(score - jnp.max(score, -1, keepdims=True))
    probs = expo * (1.0 / jnp.sum(expo, -1, keepdims=True))
    mixture = (probs[:BLOCK] - lam * probs[BLOCK:]).astype(BF16)
    return queries, key, value, probs, mixture


def column_of(row):
    rows = lax.broadcasted_iota(jnp.int32, (BLOCK, BLOCK), 0)
    cols = lax.broadcasted_iota(jnp.int32, (BLOCK, BLOCK), 1)
    return jnp.sum(jnp.where(rows == cols, row, 0.0), -1, keepdims=True)


def documents_of(marks):
    return jnp.where(marks >= GROUP, marks - GROUP, marks)


def block_bias(marks_ref, block, low, high):
    rows = lax.broadcasted_iota(jnp.int32, (BLOCK, high - low), 0) + block * BLOCK
    cols = lax.broadcasted_iota(jnp.int32, (BLOCK, high - low), 1) + low
    keys = jnp.concatenate(
        [marks_ref[b : b + 1, :] for b in range(low // BLOCK, high // BLOCK)], 1
    )
    queries = column_of(marks_ref[block : block + 1, :])
    same = documents_of(queries) == documents_of(keys)
    return jnp.where((cols <= rows) & same, 0.0, MASKED)


def reach_of(block):
    return max(0, block - REACH // BLOCK) * BLOCK, (block + 1) * BLOCK


def attend_kernel(lam_ref, qkv_ref, marks_ref, gain_ref, heads_ref):
    lam = lam_ref[0]
    gain = gain_ref[...] * KEEP
    for block in range(qkv_ref.shape[0] // BLOCK):
        low, high = reach_of(block)
        bias = block_bias(marks_ref, block, low, high)
        for head in range(OWN_HEADS):
            _, _, value, _, mixture = score_parts(qkv_ref, head, block, low, high, lam, bias)
            out = dot(mixture, value)
            normed = out * rms_scale(out, 1e-05)
            heads_ref[pl.ds(block * BLOCK, BLOCK), head * WIDTH : (head + 1) * WIDTH] = (
                normed * gain
            ).astype(BF16)


def attend_back_kernel(
    lam_ref, qkv_ref, marks_ref, gain_ref, grad_ref, out_ref, stat_ref, dk_ref, dv_ref
):
    lam = lam_ref[0]
    gain = gain_ref[...] * KEEP
    blocks = qkv_ref.shape[0] // BLOCK
    first = lax.broadcasted_iota(jnp.int32, (1, WIDTH), 1) < HD
    upper = lax.broadcasted_iota(jnp.int32, (2 * BLOCK, 1), 0) < BLOCK
    share = jnp.where(upper, 1.0, -lam)
    gain_total = jnp.zeros((1, WIDTH), F32)
    lam_total = jnp.zeros((1, 1), F32)
    biases = [block_bias(marks_ref, b, *reach_of(b)) for b in range(blocks)]
    for head in range(OWN_HEADS):
        lanes = slice(head * WIDTH, (head + 1) * WIDTH)
        dk_ref[...] = jnp.zeros_like(dk_ref)
        dv_ref[...] = jnp.zeros_like(dv_ref)
        for block in range(blocks):
            low, high = reach_of(block)
            rows, reach = pl.ds(block * BLOCK, BLOCK), pl.ds(low, high - low)
            queries, key, value, probs, mixture = score_parts(
                qkv_ref, head, block, low, high, lam, biases[block]
            )
            out = dot(mixture, value)
            scale = rms_scale(out, 1e-05)
            normed = out * scale
            grad = grad_ref[rows, lanes].astype(F32)
            gain_total = gain_total + jnp.sum(grad * normed, 0, keepdims=True)
            grad_out = norm_back(grad * gain, normed, scale).astype(BF16)
            grad_mix = dot(grad_out, value, 1, 1)
            grad_mix = jnp.concatenate([grad_mix, grad_mix], 0)
            mean = jnp.sum(grad_mix * probs, -1, keepdims=True)
            lam_total = lam_total - jnp.sum(mean[BLOCK:], 0, keepdims=True)
            low_scores = (probs * (share * (grad_mix - mean))).astype(BF16)
            dv_ref[reach, :] += dot(mixture, grad_out, 0, 0)
            dk_ref[reach, :] += dot(low_scores, queries, 0, 0)
            grad_query = dot(low_scores, key)
            grad_query = jnp.where(first, grad_query[:BLOCK], grad_query[BLOCK:])
            out_ref[rows, lanes] = (grad_query * HD**-0.5).astype(BF16)
        out_ref[:, ATTN_Q + head * WIDTH : ATTN_Q + (head + 1) * WIDTH] = dk_ref[...].astype(BF16)
        out_ref[:, 2 * ATTN_Q + head * WIDTH : 2 * ATTN_Q + (head + 1) * WIDTH] = dv_ref[
            ...
        ].astype(BF16)
    stat_ref[0:1, :] = gain_total * KEEP
    stat_ref[1:2, :] = jnp.broadcast_to(lam_total, (1, WIDTH))
    stat_ref[2:8, :] = jnp.zeros((6, WIDTH), F32)


def attention_specs(length, lines, part):
    return [
        pl.BlockSpec(memory_space=pltpu.SMEM),
        pl.BlockSpec((length, 3 * ATTN_Q), lambda i: (0, 0)),
        pl.BlockSpec((lines, BLOCK), lambda i: (part, 0)),
        pl.BlockSpec((1, WIDTH), lambda i: (0, 0)),
    ]


def attend(lam, qkv, marks, part, lines, gain):
    length = qkv.shape[0]
    return pl.pallas_call(
        attend_kernel,
        grid=(1,),
        in_specs=attention_specs(length, lines, part),
        out_specs=pl.BlockSpec((length, ATTN_Q), lambda i: (0, 0)),
        out_shape=jax.ShapeDtypeStruct((length, ATTN_Q), BF16),
        compiler_params=pltpu.CompilerParams(vmem_limit_bytes=40 * 2**20),
        cost_estimate=pl.CostEstimate(
            flops=0, bytes_accessed=length * ATTN_Q, transcendentals=0
        ),
        name="attend",
    )(lam, qkv, marks, gain)


def attend_back(lam, qkv, marks, part, lines, gain, grad):
    length = qkv.shape[0]
    return pl.pallas_call(
        attend_back_kernel,
        grid=(1,),
        in_specs=attention_specs(length, lines, part)
        + [pl.BlockSpec((length, ATTN_Q), lambda i: (0, 0))],
        out_specs=[
            pl.BlockSpec((length, 3 * ATTN_Q), lambda i: (0, 0)),
            pl.BlockSpec((8, WIDTH), lambda i: (0, 0)),
        ],
        out_shape=[
            jax.ShapeDtypeStruct((length, 3 * ATTN_Q), BF16),
            jax.ShapeDtypeStruct((8, WIDTH), F32),
        ],
        scratch_shapes=[pltpu.VMEM((length, WIDTH), F32), pltpu.VMEM((length, WIDTH), F32)],
        compiler_params=pltpu.CompilerParams(vmem_limit_bytes=40 * 2**20),
        cost_estimate=pl.CostEstimate(
            flops=0, bytes_accessed=length * ATTN_Q, transcendentals=0
        ),
        name="attend_back",
    )(lam, qkv, marks, gain, grad)


def loss_kernel(everyone, lines, *refs):
    cotangents, smalls, outs = refs[:GROUP], refs[GROUP : 2 * GROUP], refs[2 * GROUP :]
    block = pl.program_id(0)
    needles = sum([small[lines : lines + 1, :] for small in smalls])
    scale = everyone / (everyone + NEEDLE * needles[:, 0:1])
    for k in range(GROUP):
        marks = column_of(smalls[k][pl.ds(block, 1), :])
        weights = 1.0 + NEEDLE * jnp.where(marks >= GROUP, 1.0, 0.0)
        grad = cotangents[k][...].astype(F32) * (weights * scale)
        outs[k][...] = grad.astype(BF16)
        if k == 0:
            outs[GROUP][...] = grad


def loss_gradients(everyone, lines, cotangents, smalls):
    length, width = cotangents[0].shape
    spec = pl.BlockSpec((BLOCK, width), lambda i: (i, 0))
    rows = smalls[0][0].shape[0]
    low = jax.ShapeDtypeStruct((length, width), BF16)
    return pl.pallas_call(
        partial(loss_kernel, everyone, lines),
        grid=(length // BLOCK,),
        in_specs=[spec] * GROUP
        + [pl.BlockSpec((rows, BLOCK), lambda i, p=part: (p, 0)) for _, part in smalls],
        out_specs=[spec] * (GROUP + 1),
        out_shape=[low] * GROUP + [jax.ShapeDtypeStruct((length, width), F32)],
        compiler_params=pltpu.CompilerParams(vmem_limit_bytes=40 * 2**20),
        cost_estimate=pl.CostEstimate(flops=0, bytes_accessed=length * width, transcendentals=0),
        name="loss_gradients",
    )(*cotangents, *[small for small, _ in smalls])


def quarter_kernel(member_ref, *refs):
    for source, target in zip(refs[:GROUP], refs[GROUP:]):
        target[...] = source[...].astype(BF16)


def quarters(member, weight, sections, width):
    rows = weight.shape[0]

    def columns(bits):
        return lambda i, member: (0, i * GROUP + (member[0] ^ bits))

    kind = jax.ShapeDtypeStruct((rows, sections * width), BF16)
    return pl.pallas_call(
        quarter_kernel,
        grid_spec=pltpu.PrefetchScalarGridSpec(
            num_scalar_prefetch=1,
            grid=(sections,),
            in_specs=[pl.BlockSpec((rows, width), columns(bits)) for bits in range(GROUP)],
            out_specs=[pl.BlockSpec((rows, width), lambda i, member: (0, i))] * GROUP,
        ),
        out_shape=[kind] * GROUP,
        compiler_params=pltpu.CompilerParams(vmem_limit_bytes=40 * 2**20),
        cost_estimate=pl.CostEstimate(flops=0, bytes_accessed=rows * width, transcendentals=0),
        name="quarters",
    )(member.reshape(1), *[weight] * GROUP)


def back_kernel(pairs, *refs):
    total = None
    for left, right in zip(refs[:pairs], refs[pairs : 2 * pairs]):
        part = dot(left[...], right[...], 1, 1)
        total = part if total is None else total + part
    if len(refs) > 2 * pairs + 1:
        total = total + refs[2 * pairs][...].astype(F32)
    refs[-1][...] = total.astype(refs[-1].dtype)


def back_product(lefts, right, got=None, kind=BF16, tile=512, first=0, share=32):
    pairs, (length, depth) = len(lefts), lefts[0].shape
    width = right.shape[0]
    specs = [pl.BlockSpec((length, depth), lambda i: (0, 0))] * pairs
    for number in range(pairs):
        specs.append(pl.BlockSpec((tile, depth), lambda i, s=first + number: (i, s)))
    out_spec = pl.BlockSpec((length, tile), lambda i: (0, i))
    operands = list(lefts) + [right] * pairs
    if got is not None:
        specs.append(out_spec)
        operands.append(got)
    return pl.pallas_call(
        partial(back_kernel, pairs),
        grid=(width // tile,),
        in_specs=specs,
        out_specs=out_spec,
        out_shape=jax.ShapeDtypeStruct((length, width), kind),
        compiler_params=pltpu.CompilerParams(vmem_limit_bytes=40 * 2**20),
        cost_estimate=pl.CostEstimate(
            flops=2 * pairs * length * depth * width // share,
            bytes_accessed=2 * pairs * (length + width) * depth // share,
            transcendentals=0,
        ),
        name="back_product",
    )(*operands)


def weight_kernel(*refs):
    out_ref = refs[-1]
    total = None
    for left, right in zip(refs[:GROUP], refs[GROUP : 2 * GROUP]):
        part = dot(left[...], right[...], 0, 0)
        total = part if total is None else total + part
    out_ref[...] = total.astype(BF16)


def weight_product(lefts, rights, columns, place, into=None, rows=512):
    length, depth = lefts[0].shape
    width = rights[0].shape[1]
    specs = [pl.BlockSpec((length, rows), lambda i: (0, i))] * GROUP
    specs += [pl.BlockSpec((length, width), lambda i: (0, 0))] * GROUP
    operands = [*lefts, *rights]
    if into is not None:
        specs.append(pl.BlockSpec(memory_space=pl.ANY))
        operands.append(into)
    return pl.pallas_call(
        weight_kernel,
        grid=(depth // rows,),
        in_specs=specs,
        out_specs=pl.BlockSpec((rows, width), lambda i: (i, place)),
        out_shape=jax.ShapeDtypeStruct((depth, columns), BF16),
        input_output_aliases={} if into is None else {2 * GROUP: 0},
        compiler_params=pltpu.CompilerParams(vmem_limit_bytes=60 * 2**20),
        cost_estimate=pl.CostEstimate(
            flops=GROUP * length * depth * width // 32,
            bytes_accessed=GROUP * length * (depth + width) // 32,
            transcendentals=0,
        ),
        name="weight_product",
    )(*operands)


def project_kernel(left_ref, right_ref, out_ref):
    out_ref[...] = dot(left_ref[...], right_ref[...]).astype(BF16)


def project(left, right, tile=384):
    (length, depth), width = left.shape, right.shape[1]
    return pl.pallas_call(
        project_kernel,
        grid=(width // tile,),
        in_specs=[
            pl.BlockSpec((length, depth), lambda i: (0, 0)),
            pl.BlockSpec((depth, tile), lambda i: (0, i)),
        ],
        out_specs=pl.BlockSpec((length, tile), lambda i: (0, i)),
        out_shape=jax.ShapeDtypeStruct((length, width), BF16),
        compiler_params=pltpu.CompilerParams(vmem_limit_bytes=40 * 2**20),
        cost_estimate=pl.CostEstimate(flops=0, bytes_accessed=length * depth, transcendentals=0),
        name="project",
    )(left, right)


def raise_kernel(*refs):
    mids, (gate_ref, up_ref), outs = refs[:GROUP], refs[GROUP : GROUP + 2], refs[GROUP + 2 :]
    for k, mid_ref in enumerate(mids):
        gate = dot(mid_ref[...], gate_ref[...])
        up = dot(mid_ref[...], up_ref[...])
        outs[k][...] = (gate * jax.nn.sigmoid(gate) * up).astype(BF16)
        outs[GROUP + k][...] = gate
        outs[2 * GROUP + k][...] = up


def raise_up(mids, weight, tile=256):
    length, depth = mids[0].shape
    count = FF_Q // tile
    out_spec = pl.BlockSpec((length, tile), lambda i: (0, i))
    low = jax.ShapeDtypeStruct((length, FF_Q), BF16)
    high = jax.ShapeDtypeStruct((length, FF_Q), F32)
    outs = pl.pallas_call(
        raise_kernel,
        grid=(count,),
        in_specs=[pl.BlockSpec((length, depth), lambda i: (0, 0))] * GROUP
        + [
            pl.BlockSpec((depth, tile), lambda i: (0, i)),
            pl.BlockSpec((depth, tile), lambda i: (0, i + count)),
        ],
        out_specs=[out_spec] * (3 * GROUP),
        out_shape=[low] * GROUP + [high] * (2 * GROUP),
        compiler_params=pltpu.CompilerParams(vmem_limit_bytes=60 * 2**20),
        cost_estimate=pl.CostEstimate(flops=0, bytes_accessed=length * depth, transcendentals=0),
        name="raise_up",
    )(*mids, weight, weight)
    return outs[:GROUP], outs[GROUP : 2 * GROUP], outs[2 * GROUP :]


def raise_back_kernel(*refs):
    grads, down_ref, gates = refs[:GROUP], refs[GROUP], refs[GROUP + 1 : 2 * GROUP + 1]
    ups, outs = refs[2 * GROUP + 1 : 3 * GROUP + 1], refs[3 * GROUP + 1 :]
    for k in range(GROUP):
        grad_hidden = dot(grads[k][...], down_ref[...])
        gate = gates[k][...]
        sigmoid = jax.nn.sigmoid(gate)
        slope = sigmoid * (1.0 + gate * (1.0 - sigmoid))
        outs[k][...] = (grad_hidden * ups[k][...] * slope).astype(BF16)
        outs[GROUP + k][...] = (grad_hidden * gate * sigmoid).astype(BF16)


def raise_back(grads, weight, gates, ups, tile=256):
    length, depth = grads[0].shape
    count = FF_Q // tile
    spec = pl.BlockSpec((length, tile), lambda i: (0, i))
    kind = jax.ShapeDtypeStruct((length, FF_Q), BF16)
    outs = pl.pallas_call(
        raise_back_kernel,
        grid=(count,),
        in_specs=[pl.BlockSpec((length, depth), lambda i: (0, 0))] * GROUP
        + [pl.BlockSpec((depth, tile), lambda i: (0, i + 2 * count))]
        + [spec] * (2 * GROUP),
        out_specs=[spec] * (2 * GROUP),
        out_shape=[kind] * (2 * GROUP),
        compiler_params=pltpu.CompilerParams(vmem_limit_bytes=60 * 2**20),
        cost_estimate=pl.CostEstimate(flops=0, bytes_accessed=length * depth, transcendentals=0),
        name="raise_back",
    )(*grads, weight, *gates, *ups)
    return outs[:GROUP], outs[GROUP:]


def assemble_kernel(place_ref, *refs):
    out_ref = refs[-1]
    number = pl.program_id(0)
    for step, ref in enumerate(refs[:-1]):

        @pl.when(number == step)
        def _():
            out_ref[0, 0] = ref[...]


def assemble(layer, copy, layers, pieces):
    rows, cols = pieces[0].shape

    def target(i, place):
        step, part = i // 2, i % 2
        source = place[0] - step
        source = jnp.where(source < 0, source + layers, source)
        part = jnp.where(step == 0, part, jnp.where(part == 0, place[1], 1 - place[1]))
        return source, part, 0, 0

    return pl.pallas_call(
        assemble_kernel,
        grid_spec=pltpu.PrefetchScalarGridSpec(
            num_scalar_prefetch=1,
            grid=(2 * layers,),
            in_specs=[pl.BlockSpec((rows, cols), lambda i, place: (0, 0))] * (2 * layers),
            out_specs=pl.BlockSpec((1, 1, rows, cols), target),
        ),
        out_shape=jax.ShapeDtypeStruct((layers, 2, rows, cols), pieces[0].dtype),
        compiler_params=pltpu.CompilerParams(vmem_limit_bytes=40 * 2**20),
        cost_estimate=pl.CostEstimate(flops=0, bytes_accessed=rows * cols, transcendentals=0),
        name="assemble",
    )(jnp.stack([layer, copy]), *pieces)


def interleave_kernel(core_ref, own_ref, other_ref, out_ref):
    rows = own_ref.shape[0]
    first = core_ref[0] == 0
    own, other = own_ref[...], other_ref[...]
    out_ref[0:rows] = jnp.where(first, own, other)
    out_ref[rows : 2 * rows] = jnp.where(first, other, own)


def interleave(core, own, other, rows):
    total, cols = own.shape
    spec = pl.BlockSpec((rows, cols), lambda i: (i, 0))
    return pl.pallas_call(
        interleave_kernel,
        grid=(total // rows,),
        in_specs=[pl.BlockSpec(memory_space=pltpu.SMEM), spec, spec],
        out_specs=pl.BlockSpec((2 * rows, cols), lambda i: (i, 0)),
        out_shape=jax.ShapeDtypeStruct((2 * total, cols), own.dtype),
        cost_estimate=pl.CostEstimate(
            flops=0, bytes_accessed=8 * total * cols, transcendentals=0
        ),
        name="interleave",
    )(core.reshape(1), own, other)


def merge_kernel(member_ref, *refs):
    shares, (error_ref, start_ref), outs = refs[:GROUP], refs[GROUP : GROUP + 2], refs[GROUP + 2 :]
    grad_ref, merged_ref, left_ref = outs
    width = shares[0].shape[1]
    values = arrange([share[...].astype(F32) for share in shares], member_ref[0])

    @pl.when(pl.program_id(0) == 0)
    def _():
        left_ref[...] = jnp.zeros_like(left_ref)

    for number, value in enumerate(values):
        lanes = slice(number * width, (number + 1) * width)
        grad_ref[:, lanes] = value
        merged = value + DECAY_ERROR * error_ref[:, lanes]
        merged_ref[:, lanes] = merged
        left_ref[...] += dot(start_ref[:, lanes], merged, 1, 1, precision=HIGHEST)


def merge(member, shares, error, start, width):
    rows, total = error.shape
    rank = start.shape[0]
    wide = pl.BlockSpec((rows, GROUP * width), lambda i: (0, i))
    kind = jax.ShapeDtypeStruct((rows, total), F32)
    return pl.pallas_call(
        merge_kernel,
        grid=(total // (GROUP * width),),
        in_specs=[pl.BlockSpec(memory_space=pltpu.SMEM)]
        + [pl.BlockSpec((rows, width), lambda i: (0, i))] * GROUP
        + [wide, pl.BlockSpec((rank, GROUP * width), lambda i: (0, i))],
        out_specs=[wide, wide, pl.BlockSpec((rank, rows), lambda i: (0, 0))],
        out_shape=[kind, kind, jax.ShapeDtypeStruct((rank, rows), F32)],
        compiler_params=pltpu.CompilerParams(vmem_limit_bytes=40 * 2**20),
        cost_estimate=pl.CostEstimate(flops=0, bytes_accessed=rows * total, transcendentals=0),
        name="merge",
    )(member.reshape(1), *shares, error, start)


def right_kernel(own_ref, other_ref, merged_ref, ortho_ref, right_ref, left_ref):
    @pl.when(pl.program_id(0) == 0)
    def _():
        left = own_ref[...] + other_ref[...]
        number = lax.broadcasted_iota(jnp.int32, (left.shape[0], 1), 0)
        for step in range(left.shape[0]):
            row = left[step : step + 1]
            row = row * lax.rsqrt(jnp.sum(row * row, -1, keepdims=True))
            share = jnp.sum(left * row, -1, keepdims=True)
            left = jnp.where(
                number > step, left - share * row, jnp.where(number == step, row, left)
            )
        left_ref[...] = left
        ortho_ref[...] = left

    right_ref[...] = dot(left_ref[...], merged_ref[...], precision=HIGHEST).astype(BF16)


def right_factor(own, other, merged, steps=4):
    rank, rows = own.shape
    total = merged.shape[1]
    tile = total // steps
    small = pl.BlockSpec((rank, rows), lambda i: (0, 0))
    return pl.pallas_call(
        right_kernel,
        grid=(total // tile,),
        in_specs=[small, small, pl.BlockSpec((rows, tile), lambda i: (0, i))],
        out_specs=[small, pl.BlockSpec((rank, tile), lambda i: (0, i))],
        out_shape=[
            jax.ShapeDtypeStruct((rank, rows), F32),
            jax.ShapeDtypeStruct((rank, total), BF16),
        ],
        scratch_shapes=[pltpu.VMEM((rank, rows), F32)],
        compiler_params=pltpu.CompilerParams(vmem_limit_bytes=40 * 2**20),
        cost_estimate=pl.CostEstimate(flops=0, bytes_accessed=rows * total, transcendentals=0),
        name="right_factor",
    )(own, other, merged)


def update_kernel(copies, ortho_ref, own_ref, other_ref, merged_ref, momentum_ref, weight_ref, *outs):
    right_ref, error_ref, momentum_out_ref, weight_out_ref = outs
    right = (own_ref[...].astype(F32) + other_ref[...].astype(F32)) / copies
    approx = dot(ortho_ref[...], right, 0, 0, precision=HIGHEST)
    momentum = MOMENTUM * momentum_ref[...] + (1.0 - MOMENTUM) * approx
    right_ref[...] = right
    error_ref[...] = merged_ref[...] - approx
    momentum_out_ref[...] = momentum
    weight_out_ref[...] = weight_ref[...] - RATE_MATRIX * momentum


def update(copies, ortho, own, other, merged, momentum, weight, steps=4):
    rank, rows = ortho.shape
    total = merged.shape[1]
    tile = total // steps
    small = pl.BlockSpec((rank, rows), lambda i: (0, 0))
    low = pl.BlockSpec((rank, tile), lambda i: (0, i))
    wide = pl.BlockSpec((rows, tile), lambda i: (0, i))
    kind = jax.ShapeDtypeStruct((rows, total), F32)
    return pl.pallas_call(
        partial(update_kernel, copies),
        grid=(total // tile,),
        in_specs=[small, low, low, wide, wide, wide],
        out_specs=[low, wide, wide, wide],
        out_shape=[jax.ShapeDtypeStruct((rank, total), F32), kind, kind, kind],
        compiler_params=pltpu.CompilerParams(vmem_limit_bytes=40 * 2**20),
        cost_estimate=pl.CostEstimate(flops=0, bytes_accessed=rows * total, transcendentals=0),
        name="update",
    )(ortho, own, other, merged, momentum, weight)


def after(value, *earlier):
    return lax.optimization_barrier((value, *earlier))[0]


def swap(value, bits):
    return lax.ppermute(value, "member", [(j, j ^ bits) for j in range(GROUP)])


def swap_layers(value, bits, layers):
    return lax.ppermute(value, "layer", [(z, z ^ bits) for z in range(layers)])


def ring(value, layers):
    return lax.ppermute(value, "layer", [(z, (z + 1) % layers) for z in range(layers)])


def cross(value, copies):
    return lax.ppermute(value, "replica", [(r, (r + 1) % copies) for r in range(copies)])


def sum_layers(partials):
    return lax.psum_scatter(partials, "layer", scatter_dimension=0, tiled=True)


def arrange(items, member):
    low, high = (member & 1) == 1, (member & 2) == 2
    pairs = [jnp.where(low, items[t ^ 1], items[t]) for t in range(GROUP)]
    return [jnp.where(high, pairs[t ^ 2], pairs[t]) for t in range(GROUP)]


class Line:
    def __init__(self, token):
        self.token = token

    def __call__(self, value):
        value, self.token = lax.optimization_barrier((value, self.token))
        return value

    def run(self, step, first, *others):
        return self(step(self(first), *others))


class Gather:
    def __init__(self, line, halves, layer, copy, layers, copies):
        self.line, self.layer, self.copy = line, layer, copy
        self.layers, self.copies = layers, copies
        self.halves = halves
        self.got = jnp.where(copy == 0, halves[0], halves[1])
        self.way, self.over_way, self.pieces, self.over = None, [], [], []

    def hop(self):
        self.way = ring(self.line(self.got), self.layers)

    def land(self):
        self.got = self.line(self.way)
        self.pieces.append(self.got)
        self.over_way.append(cross(self.got, self.copies))

    def land_over(self):
        self.over.append(self.line(self.over_way[len(self.over)]))

    def finish(self):
        while len(self.over) < self.layers - 1:
            if len(self.pieces) < self.layers - 1 and len(self.pieces) == len(self.over):
                self.hop()
                self.land()
            self.land_over()
        pieces = list(self.halves)
        for own, other in zip(self.pieces, self.over):
            pieces += [own, other]
        whole = assemble(self.layer, self.copy, self.layers, pieces)
        return whole.reshape(-1, whole.shape[-1])


def local(
    layers,
    copies,
    tokens,
    cotangent,
    needle_mask,
    segment_ids,
    attn_weight,
    ffn_weight,
    vector_params,
    attn_error,
    ffn_error,
    attn_momentum,
    ffn_momentum,
    attn_start,
    ffn_start,
    vector_momentum,
):
    length = tokens.shape[0]
    copy = lax.axis_index("replica")
    layer, member = lax.axis_index("layer"), lax.axis_index("member")

    gain_in = vector_params[0:D]
    gain_mid = vector_params[D : 2 * D]
    gain_head = vector_params[2 * D : 2 * D + 2 * HD]
    lambda_q_one = vector_params[2 * D + 2 * HD : 2 * D + 3 * HD]
    lambda_k_one = vector_params[2 * D + 3 * HD : 2 * D + 4 * HD]
    lambda_q_two = vector_params[2 * D + 4 * HD : 2 * D + 5 * HD]
    lambda_k_two = vector_params[2 * D + 5 * HD : 2 * D + 6 * HD]
    exp_one = jnp.exp(jnp.sum(lambda_q_one * lambda_k_one))
    exp_two = jnp.exp(jnp.sum(lambda_q_two * lambda_k_two))
    lam = (exp_one - exp_two + LAMBDA_INIT).reshape(1)

    line = Line(jnp.zeros((8, 128), F32))

    def gather(halves):
        return Gather(line, halves, layer, copy, layers, copies)

    def halves_of(block):
        rows = block.shape[0] // 2
        return block[:rows], block[rows:]

    def columns(values, width):
        return [values[:, t * width : (t + 1) * width] for t in range(GROUP)]

    def layer_block(parts):
        return jnp.concatenate(arrange(parts, member), 0)

    needles = jnp.broadcast_to(jnp.sum(needle_mask).astype(F32), (8, 128))
    needles_other = cross(needles, copies)
    qkv_parts = quarters(member, attn_weight, 3, ATTN_Q)
    qkv_got = [swap(qkv_parts[k], k) for k in (2, 3, 1)]
    needles = needles + line(needles_other)
    bits = 1
    while bits < layers:
        needles = needles + line(swap_layers(needles, bits, layers))
        bits *= 2
    qkv_got = [line(got) for got in qkv_got]
    qkv_block = layer_block([qkv_parts[0], qkv_got[2], qkv_got[0], qkv_got[1]])
    qkv_gather = gather(halves_of(qkv_block))
    qkv_gather.hop()
    ffn_parts = quarters(member, line(ffn_weight), 3, FF_Q)
    ffn_got = [swap(line(ffn_parts[k]), k) for k in (2, 3, 1)]
    out_own = line(attn_weight)[:, 3 * D :].astype(BF16)
    out_across = swap(out_own, 2)
    qkv_gather.land()
    qkv_gather.hop()
    residual_in = line(tokens).astype(F32)
    scale_in = rms_scale(residual_in, 1e-06)
    normed_in = residual_in * scale_in
    normed_low = line((normed_in * gain_in).astype(BF16))
    qkv_gather.land()
    qkv_gather.hop()
    lines = length // 128
    marks = segment_ids.reshape(lines, 128) + GROUP * needle_mask.reshape(lines, 128)
    small = jnp.concatenate([marks.astype(F32), needles[: 8 - lines % 8]])
    rows = small.shape[0]
    small_beside = line(swap(line(small), 1))
    small_pair = jnp.concatenate([small, small_beside])
    out_across = swap(line(out_own), 2)
    qkv_gather.land()
    ffn_got = [line(got) for got in ffn_got]
    normed_across = swap(line(normed_low), 2)
    small_across = swap(small_pair, 2)
    normed_beside = swap(normed_low, 1)
    ffn_half = layer_block([ffn_parts[0], ffn_got[2], ffn_got[0], ffn_got[1]])
    ffn_half = ffn_half.reshape(2, -1, ffn_half.shape[1])
    ffn_half = line(lax.dynamic_index_in_dim(ffn_half, copy, 0, False))
    out_across = line(out_across)
    side = (member // 2) == 0
    out_gather = gather(
        (jnp.where(side, out_own, out_across), jnp.where(side, out_across, out_own))
    )
    out_gather.hop()
    qkv_gather.land_over()
    qkv_gather.land_over()
    out_gather.land()
    out_gather.hop()
    qkv_gather.land_over()
    ffn_weight_low = lax.all_gather(line(ffn_half), ("layer", "replica"), axis=0, tiled=True)
    out_gather.land()
    out_gather.hop()
    out_gather.land_over()
    out_gather.land()
    out_gather.land_over()
    normed_across = line(normed_across)
    small_across = line(small_across)
    normed_opposite = swap(normed_across, 1)
    cotangent_across = swap(line(cotangent), 2)
    qkv_weight = qkv_gather.finish()
    normed_beside = line(normed_beside)

    smalls = [(small, 0), (small_beside, 0), (small_across, 0), (small_across, 1)]

    def heads_of(qkv, k):
        return attend(lam, qkv, *smalls[k], rows, gain_head[None])

    qkv = [None] * GROUP
    heads = [None] * GROUP
    qkv[0] = line.run(project, normed_low, qkv_weight)
    qkv[1] = line.run(project, normed_beside, qkv_weight)
    heads[0] = line.run(heads_of, qkv[0], 0)
    heads[1] = line.run(heads_of, qkv[1], 1)
    heads_beside = swap(heads[1], 1)
    qkv[2] = line.run(project, normed_across, qkv_weight)
    heads[2] = line.run(heads_of, qkv[2], 2)
    heads_across = swap(heads[2], 2)
    cotangent_across = line(cotangent_across)
    out_mine = line(out_gather.finish())
    out_rest = swap(out_mine, 1)
    normed_opposite = line(normed_opposite)
    normed_all = [normed_low, normed_beside, normed_across, normed_opposite]
    qkv[3] = line.run(project, normed_opposite, qkv_weight)
    heads[3] = line.run(heads_of, qkv[3], 3)
    heads_opposite = swap(heads[3], 3)
    cotangent_near = swap(line(cotangent), 1)
    cotangent_far = swap(cotangent_across, 1)
    heads_beside, heads_across = line(heads_beside), line(heads_across)
    out_rest = line(out_rest)
    out_weight = line.run(
        lambda x: interleave(member % 2, x, out_rest, D // (layers * GROUP)), out_mine
    )
    heads_opposite = line(heads_opposite)
    heads_low = jnp.concatenate(
        arrange([heads[0], heads_beside, heads_across, heads_opposite], member), 1
    )
    residual_mid = line.run(lambda x: residual_in + dot(x, out_weight), heads_low)
    scale_mid = rms_scale(residual_mid, 1e-06)
    normed_mid = residual_mid * scale_mid
    mid_low = line((normed_mid * gain_mid).astype(BF16))
    mid_across = swap(mid_low, 2)
    mid_beside = swap(mid_low, 1)
    cotangents = [cotangent, line(cotangent_near), cotangent_across, line(cotangent_far)]
    *grad_out_all, grad_out = line.run(
        lambda x: loss_gradients(
            length * layers * GROUP * copies, lines, [x, *cotangents[1:]], smalls
        ),
        cotangent,
    )
    mid_across = line(mid_across)
    mid_opposite = swap(mid_across, 1)
    heads_across_all = swap(line(heads_low), 2)
    mid_beside, mid_opposite = line(mid_beside), line(mid_opposite)
    ffn_weight_low = line(ffn_weight_low)

    def product(lefts, rights, columns, place, into=None):
        return line.run(
            lambda x: weight_product([x, *lefts[1:]], rights, columns, place, into), lefts[0]
        )

    mid_all = [mid_low, mid_beside, mid_across, mid_opposite]
    hidden, gate_proj, up_proj = line.run(
        lambda x: raise_up([x, *mid_all[1:]], ffn_weight_low), mid_low
    )
    grad_gate, grad_up = line.run(
        lambda x: raise_back([x, *grad_out_all[1:]], ffn_weight_low, gate_proj, up_proj),
        grad_out_all[0],
    )
    heads_across_all = line(heads_across_all)
    down_total = sum_layers(product(grad_out_all, hidden, FF_Q, 0))

    def lower(k, got=None, kind=BF16):
        return line.run(
            lambda x: back_product([x, grad_up[k]], ffn_weight_low, got, kind), grad_gate[k]
        )

    def lower_hidden(k, got=None, kind=BF16):
        return line.run(
            lambda x: back_product([x], ffn_weight_low, got, kind, first=2), hidden[k]
        )

    opposite_got = swap(lower(3), 1)
    beside_got = swap(lower(1), 1)
    opposite_got = line(opposite_got)
    mid_sum = swap(lower(2, opposite_got), 2)
    beside_got = line(beside_got)
    up_partial = product(mid_all, grad_gate, 2 * FF_Q, 0)
    grad_mid_own = lower(0, beside_got, F32)
    up_partial = product(mid_all, grad_up, 2 * FF_Q, 1, up_partial)
    ffn_opposite_got = swap(lower_hidden(3), 1)
    ffn_beside_got = swap(lower_hidden(1), 1)
    mid_sum = line(mid_sum)
    down_total = line(down_total)
    up_total = sum_layers(line(up_partial))
    heads_beside_all = swap(line(heads_low), 1)
    heads_opposite_all = swap(heads_across_all, 1)

    grad_mid_low = grad_mid_own + mid_sum.astype(F32)
    grad_mid = grad_out + norm_back(grad_mid_low * gain_mid, normed_mid, scale_mid)
    grad_attn_low = grad_mid.astype(BF16)
    grad_heads = line.run(lambda x: dot(x, out_weight, 1, 1).astype(BF16), grad_attn_low)
    grad_heads = arrange(columns(grad_heads, ATTN_Q), member)
    grad_heads_got = [swap(grad_heads[k], k) for k in (2, 3, 1)]
    grad_attn = arrange(columns(grad_attn_low, ATTN_Q), member)

    def back(grad, k):
        return attend_back(lam, qkv[k], *smalls[k], rows, gain_head[None], grad)

    grad_qkv, stats = [None] * GROUP, [None] * GROUP
    grad_qkv[0], stats[0] = line.run(back, grad_heads[0], 0)
    heads_beside_all, heads_opposite_all = line(heads_beside_all), line(heads_opposite_all)
    heads_all = [heads_low, heads_beside_all, heads_across_all, heads_opposite_all]
    ffn_opposite_got, ffn_beside_got = line(ffn_opposite_got), line(ffn_beside_got)
    grad_qkv[1], stats[1] = line.run(back, line(grad_heads_got[2]), 1)
    grad_heads_across, grad_heads_opposite = line(grad_heads_got[0]), line(grad_heads_got[1])
    grad_attn_got = [swap(line(grad_attn[k]), k) for k in (2, 3, 1)]
    grad_qkv[2], stats[2] = line.run(back, grad_heads_across, 2)
    grad_attn_got = [line(got) for got in grad_attn_got]
    grad_attn_all = [grad_attn[0], grad_attn_got[2], grad_attn_got[0], grad_attn_got[1]]
    ffn_sum = swap(lower_hidden(2, ffn_opposite_got), 2)
    grad_qkv[3], stats[3] = line.run(back, grad_heads_opposite, 3)
    attn_partial = product(heads_all, grad_attn_all, 4 * ATTN_Q, 3)
    ffn_own = lower_hidden(0, ffn_beside_got, F32)
    attn_partial = product(normed_all, grad_qkv, 4 * ATTN_Q, 0, attn_partial)
    ffn_sum = line(ffn_sum)
    attn_total = sum_layers(line(attn_partial))
    mixed = line((residual_mid + ffn_own + ffn_sum.astype(F32)).astype(BF16))
    stats = sum(stats)
    grad_gain_head, grad_lambda = stats[0], stats[1, 0]

    def lower_in(k, got=None, kind=BF16):
        return line.run(
            lambda x: back_product([x], qkv_weight, got, kind, share=1), grad_qkv[k]
        )

    def rows_of(total):
        size = total.shape[0] // GROUP
        return arrange([total[t * size : (t + 1) * size] for t in range(GROUP)], member)

    def share(parts):
        return [parts[0]] + [swap(line(parts[k]), k) for k in range(1, GROUP)]

    def landed(parts):
        return [parts[0]] + [line(part) for part in parts[1:]]

    in_opposite_got = swap(lower_in(3), 1)
    in_beside_got = swap(lower_in(1), 1)
    ffn_total = jnp.concatenate([line(up_total), down_total], 1)
    ffn_shares = share(rows_of(ffn_total))
    in_opposite_got = line(in_opposite_got)
    in_sent = lower_in(2, in_opposite_got)
    in_beside_got = line(in_beside_got)
    in_own = lower_in(0, in_beside_got, F32)
    grad_gain_mid = line(jnp.sum(line(grad_mid_low) * normed_mid, 0))
    ffn_rows = landed(ffn_shares)
    in_sum = swap(line(in_sent), 2)
    ffn_grad, merged_ffn, left_ffn = line.run(
        lambda x: merge(member, [x, *ffn_rows[1:]], ffn_error[0], ffn_start[0], FF_Q), ffn_rows[0]
    )
    left_other = line(cross(left_ffn, copies))
    ortho_ffn, right_ffn = line.run(right_factor, left_ffn, left_other, merged_ffn)
    right_other = line(cross(right_ffn, copies))
    right_ffn, ffn_error_new, ffn_momentum_new, ffn_weight_new = line.run(
        partial(update, copies), ortho_ffn, right_ffn, right_other, merged_ffn, ffn_momentum, ffn_weight
    )
    in_sum = line(in_sum)
    grad_in_low = in_own + in_sum.astype(F32)
    grad_gain_in = line(jnp.sum(grad_in_low * normed_in, 0))
    vector_grad = jnp.concatenate(
        [
            grad_gain_in,
            grad_gain_mid,
            grad_gain_head,
            grad_lambda * exp_one * lambda_k_one,
            grad_lambda * exp_one * lambda_q_one,
            -grad_lambda * exp_two * lambda_k_two,
            -grad_lambda * exp_two * lambda_q_two,
        ]
    ).reshape(-1, 128)
    attn_shares = share(rows_of(line(attn_total)))
    vector_grad = vector_grad + line(cross(vector_grad, copies))
    vector_grad = vector_grad + line(swap(vector_grad, 1))
    bits = 1
    while bits < layers:
        vector_grad = vector_grad + line(swap_layers(vector_grad, bits, layers))
        bits *= 2
    attn_rows = landed(attn_shares)
    vector_other = swap(line(vector_grad), 2)
    attn_grad, merged_attn, left_attn = line.run(
        lambda x: merge(member, [x, *attn_rows[1:]], attn_error[0], attn_start[0], ATTN_Q),
        attn_rows[0],
    )
    left_other = line(cross(left_attn, copies))
    vector_grad = (vector_grad + line(vector_other)).reshape(-1)
    ortho_attn, right_attn = line.run(right_factor, left_attn, left_other, merged_attn)
    right_other = cross(right_attn, copies)
    grad_tokens = line(grad_mid + norm_back(grad_in_low * gain_in, normed_in, scale_in))
    right_other = line(right_other)
    right_attn, attn_error_new, attn_momentum_new, attn_weight_new = line.run(
        partial(update, copies),
        ortho_attn,
        right_attn,
        right_other,
        merged_attn,
        attn_momentum,
        attn_weight,
    )
    vector_grad = vector_grad + line.token[0, 0]
    vector_momentum_new = MOMENTUM * vector_momentum + (1.0 - MOMENTUM) * vector_grad
    vector_new = vector_params - RATE_VECTOR * vector_momentum_new
    return (
        mixed,
        grad_tokens,
        attn_grad[None],
        ffn_grad[None],
        ortho_attn,
        ortho_ffn,
        right_attn[None],
        right_ffn[None],
        attn_error_new[None],
        ffn_error_new[None],
        attn_momentum_new,
        ffn_momentum_new,
        attn_weight_new,
        ffn_weight_new,
        vector_momentum_new,
        vector_new,
    )


def solution(mesh):
    copies, shards = mesh.shape["replica"], mesh.shape["fsdp"]
    layers = shards // GROUP
    mesh = jax.sharding.Mesh(
        mesh.devices.reshape(copies, layers, GROUP), ("replica", "layer", "member")
    )
    fsdp = ("layer", "member")
    everywhere = ("replica", *fsdp)
    in_specs = (
        P(everywhere, None),
        P(everywhere, None),
        P(everywhere),
        P(everywhere, None),
        P(fsdp, None),
        P(fsdp, None),
        P(),
        P("replica", fsdp, None),
        P("replica", fsdp, None),
        P(fsdp, None),
        P(fsdp, None),
        P(fsdp, None, None),
        P(fsdp, None, None),
        P(),
    )
    out_specs = (
        P(everywhere, None),
        P(everywhere, None),
        P("replica", fsdp, None),
        P("replica", fsdp, None),
        P(None, fsdp),
        P(None, fsdp),
        P(fsdp, None, None),
        P(fsdp, None, None),
        P("replica", fsdp, None),
        P("replica", fsdp, None),
        P(fsdp, None),
        P(fsdp, None),
        P(fsdp, None),
        P(fsdp, None),
        P(),
        P(),
    )
    step = partial(local, layers, copies)
    return jax.shard_map(step, mesh=mesh, in_specs=in_specs, out_specs=out_specs, check_vma=False)
```
